32 devices in a mesh: rep: 8 (over y, x, core), shard: 4 (over z).
Axes of the slice: x: 2, y: 2, z: 4, core: 2. Of those that a mesh axis runs over, the one named last changes fastest.
Arguments:
- hidden: bfloat16 [16384, 1536], P(('rep', 'shard')), may hold values from -6 to 6
- seg_ids: int32 [32, 512], P(('rep', 'shard')), may hold values from 0 to 2, never falling along the last dimension, each value on 1 to 384 neighbouring positions
- cotangent: bfloat16 [16384, 1536], P(('rep', 'shard')), may hold values from -6 to 6
- in_weight: bfloat16 [1536, 6448], P('shard'), may hold values from -0.15625 to 0.15625
- out_weight: bfloat16 [3072, 1536], P('shard'), may hold values from -0.109375 to 0.109375
- norm_gain: bfloat16 [1536], P('shard'), may hold values from 0.5 to 1.5
- gated_gain: bfloat16 [3072], P('shard'), may hold values from 0.5 to 1.5
- conv_weight: bfloat16 [4, 3328], P(None, 'shard'), may hold values from -3 to 3
- conv_bias: bfloat16 [3328], P('shard'), may hold values from -3 to 3
- a_log: bfloat16 [48], P('shard'), may hold values from -4 to 0.69921875
- d_skip: bfloat16 [48], P('shard'), may hold values from 0.5 to 1.5
- dt_bias: bfloat16 [48], P('shard'), may hold values from -4 to -1
Outputs:
- mixed: bfloat16 [16384, 1536], P(('rep', 'shard'))
- grad_hidden: float32 [16384, 1536], P(('rep', 'shard'))
- grad_in_weight: float32 [1536, 6448], P('shard')
- grad_out_weight: float32 [3072, 1536], P('shard')
- grad_norm_gain: float32 [1536], P('shard')
- grad_gated_gain: float32 [3072], P('shard')
- grad_conv_weight: float32 [4, 3328], P(None, 'shard')
- grad_conv_bias: float32 [3328], P('shard')
- grad_a_log: float32 [48], P('shard')
- grad_d_skip: float32 [48], P('shard')
- grad_dt_bias: float32 [48], P('shard')
The draws below stay inside these ranges and needn't reach their ends.
All inputs are finite; a program needn't handle non-finite values.
Results may differ from the reference program's by a relative error of at most 0.0072.
Values may be sent and summed in bfloat16 or wider, within the bound.
A program may use at most 320 MiB of HBM per device.

```python
import math
import jax
import jax.numpy as jnp
import numpy as np
from jax import lax

D = 1536
HEADS = 48
HEAD_DIM = 64
STATE = 128
CONV = 4
BLOCK_LEN = 256
TOK_DEV = 512
SEGS = 3
INNER = 3072
CONV_CH = 3328
PROJ = 6448
SEQ_MOST = 384
TOKENS = 16384
DEVICES = 32


def block_levels(rng, shape, shards, least, top_value):
    def one(axis_at, blocks):
        heights = jax.random.uniform(jax.random.fold_in(jax.random.fold_in(rng, 6), axis_at), (blocks,), jnp.float32, least / len(shards), top_value / len(shards))
        return jnp.repeat(jnp.exp(heights), shape[axis_at] // blocks).reshape((-1,) + (1,) * (len(shape) - axis_at - 1))

    factor_of = one(*shards[0])
    for cut in shards[1:]:
        factor_of = factor_of * one(*cut)
    return factor_of


def split_up(count, total, reach, lean):
    portions = [(1 << 20) // math.isqrt(standing ** lean) + 1 for standing in range(2, count + 1)]
    rest, holding = total - reach - (count - 1), [1] * (count - 1)
    while rest > 0:
        free = [i for i in range(count - 1) if holding[i] < reach]
        whole, budget = sum([portions[i] for i in free]), rest
        for i in free:
            more = min(reach - holding[i], max(1, budget * portions[i] // whole), rest)
            holding[i] = holding[i] + more
            rest = rest - more
    return np.array([reach] + holding)


def ragged_sizes(stream_key, number_of, total, most, skew):
    if number_of == 2:
        one = jax.random.randint(stream_key, (), max(1, total - most), min(most, total - 1) + 1)
        return jnp.stack([one, total - one])
    sizes = jnp.asarray(split_up(number_of, total, most, skew), jnp.int32)
    couples = (number_of - 1) // 2
    donor, receiver = sizes[1:1 + 2 * couples:2], sizes[2:2 + 2 * couples:2]
    margin = jnp.minimum(donor - 1, most - receiver)
    moved = jax.random.randint(jax.random.fold_in(stream_key, 1), (couples,), 0, 1 << 20) % (margin + 1)
    sizes = sizes.at[1:1 + 2 * couples:2].set(donor - moved).at[2:2 + 2 * couples:2].set(receiver + moved)
    return sizes[jax.random.permutation(jax.random.fold_in(stream_key, 2), number_of)]


def normal_values(stream_key, extent, width, reach, shards=(), kind=jnp.bfloat16):
    drawn = jax.random.normal(stream_key, extent, jnp.float32) * width
    if len(shards) > 0:
        drawn = block_levels(stream_key, extent, shards, -0.22, 0.18) * drawn
    return jnp.clip(drawn, min=-reach, max=reach).astype(kind)


def setup_inputs(seed: int = 0) -> dict:
    splits = jax.random.split(jax.random.key(seed), 13)
    return {
        "hidden": normal_values(splits[0], (TOKENS, D), 1.0, 6.0, ((0, 32),)),
        "seg_ids": jax.vmap(lambda own: jnp.searchsorted(jnp.cumsum(ragged_sizes(own, SEGS, TOK_DEV, SEQ_MOST, 2)), jnp.arange(TOK_DEV), side="right"))(jax.random.split(splits[1], DEVICES)).reshape((DEVICES, TOK_DEV)).astype(jnp.int32),
        "cotangent": normal_values(splits[2], (TOKENS, D), 1.0, 6.0, ((0, 32),)),
        "in_weight": normal_values(splits[3], (D, PROJ), D ** -0.5, 0.15625, ((0, 4),)),
        "out_weight": normal_values(splits[4], (INNER, D), INNER ** -0.5, 0.109375, ((0, 4),)),
        "norm_gain": jnp.clip(1.0 + 0.1 * jax.random.normal(splits[5], (D,), jnp.float32), 0.5, 1.5).astype(jnp.bfloat16),
        "gated_gain": jnp.clip(1.0 + 0.1 * jax.random.normal(splits[6], (INNER,), jnp.float32), 0.5, 1.5).astype(jnp.bfloat16),
        "conv_weight": normal_values(splits[7], (CONV, CONV_CH), 0.5, 3.0, ((1, 4),)),
        "conv_bias": normal_values(splits[8], (CONV_CH,), 0.3, 3.0, ((0, 4),)),
        "a_log": jnp.clip(-4.0 + 4.6992188 * jax.random.uniform(splits[9], (HEADS,), jnp.float32) ** block_levels(splits[9], (HEADS,), ((0, 4),), -0.2, 0.2), -4.0, 0.69921875).astype(jnp.bfloat16),
        "d_skip": jnp.clip(0.5 + 1.0 * jax.random.uniform(splits[10], (HEADS,), jnp.float32) ** block_levels(splits[10], (HEADS,), ((0, 4),), -0.2, 0.2), 0.5, 1.5).astype(jnp.bfloat16),
        "dt_bias": jnp.clip(-4.0 + 3.0 * jax.random.uniform(splits[11], (HEADS,), jnp.float32) ** block_levels(splits[11], (HEADS,), ((0, 4),), -0.2, 0.2), -4.0, -1.0).astype(jnp.bfloat16),
    }


epsilon = 1e-05

@jax.custom_vjp
def low(v):
    return lax.optimization_barrier(v.astype(jnp.bfloat16)).astype(jnp.float32)

@jax.custom_vjp
def low_back(v):
    return v

def low_keep(v):
    return (low(v), None)

def low_pass(kept, grad):
    return (grad,)

def back_keep(v):
    return (v, None)

def back_low(kept, grad):
    return (low(grad),)
low.defvjp(low_keep, low_pass)
low_back.defvjp(back_keep, back_low)

def rms_scale(values, gain_vec):
    return values * lax.rsqrt(lax.optimization_barrier(jnp.mean(values * values, axis=-1, keepdims=True)) + epsilon) * gain_vec

def segment_conv(conv_input, segments, conv_weight, conv_bias):
    length = conv_input.shape[0]
    padded = jnp.concatenate([jnp.zeros((CONV - 1, conv_input.shape[1]), conv_input.dtype), conv_input], axis=0)
    padded_seg = jnp.concatenate([jnp.full((CONV - 1,), -1, jnp.int32), segments.astype(jnp.int32)], axis=0)
    total = jnp.zeros_like(conv_input) + conv_bias[None, :]
    for offset in range(CONV):
        window = padded[offset:offset + length]
        same = (padded_seg[offset:offset + length] == segments).astype(conv_input.dtype)
        total = total + conv_weight[offset][None, :] * window * same[:, None]
    return total

def ssd_scan(inputs_x, b_proj, c_proj, step_sizes, a_rate, segments):
    count = inputs_x.shape[0] // BLOCK_LEN
    highest = lax.Precision.HIGHEST
    causal_lower = jnp.arange(BLOCK_LEN)[:, None] >= jnp.arange(BLOCK_LEN)[None, :]

    def step_fn(carry, block_in):
        carried, previous = carry
        x_block, b_block, c_block, dt_block, seg_block = block_in
        log_rates = dt_block * a_rate[None, :]
        cumulative = jnp.cumsum(log_rates, axis=0)
        allowed = (causal_lower & (seg_block[:, None] == seg_block[None, :]))[None]
        log_gap = cumulative.T[:, :, None] - cumulative.T[:, None, :]
        decays = jnp.where(allowed, jnp.exp(jnp.where(allowed, log_gap, 0.0)), 0.0)
        intersection = jnp.dot(c_block, b_block.T, precision=highest)
        mixing = decays * intersection[None] * dt_block.T[:, None, :]
        within = jnp.einsum('hij,jhp->ihp', mixing, x_block, precision=highest)
        from_prev = (seg_block == previous).astype(x_block.dtype)[:, None] * jnp.exp(cumulative)
        across = jnp.einsum('in,hpn->ihp', c_block, carried, precision=highest) * from_prev[:, :, None]
        last_seg = seg_block[BLOCK_LEN - 1]
        to_end = (seg_block == last_seg).astype(x_block.dtype)[:, None] * jnp.exp(cumulative[BLOCK_LEN - 1][None, :] - cumulative) * dt_block
        fresh_state = jnp.einsum('jhp,jn->hpn', x_block * to_end[:, :, None], b_block, precision=highest)
        keep_factor = (previous == last_seg).astype(x_block.dtype) * jnp.exp(cumulative[BLOCK_LEN - 1])
        new_state = keep_factor[:, None, None] * carried + fresh_state
        return ((new_state, last_seg), within + across)
    start = (jnp.zeros((HEADS, HEAD_DIM, STATE), inputs_x.dtype), jnp.int32(-1))
    blocks = (inputs_x.reshape(count, BLOCK_LEN, HEADS, HEAD_DIM), b_proj.reshape(count, BLOCK_LEN, STATE), c_proj.reshape(count, BLOCK_LEN, STATE), step_sizes.reshape(count, BLOCK_LEN, HEADS), segments.reshape(count, BLOCK_LEN).astype(jnp.int32))
    ignored, outputs = lax.scan(jax.checkpoint(step_fn), start, blocks)
    return outputs.reshape(-1, HEADS, HEAD_DIM)

def mixer_core(projected, segments, conv_weight, conv_bias, a_log, d_skip, dt_bias, gated_gain):
    gate_in = projected[:, :INNER]
    conv_input = projected[:, INNER:INNER + CONV_CH]
    dt_raw = projected[:, INNER + CONV_CH:]
    conv_out = jax.nn.silu(segment_conv(conv_input, segments, conv_weight, conv_bias))
    inputs_x = conv_out[:, :INNER].reshape(-1, HEADS, HEAD_DIM)
    b_proj = conv_out[:, INNER:INNER + STATE]
    c_proj = conv_out[:, INNER + STATE:]
    step_sizes = jax.nn.softplus(dt_raw + dt_bias[None, :])
    a_rate = -jnp.exp(a_log)
    scanned = ssd_scan(inputs_x, b_proj, c_proj, step_sizes, a_rate, segments) + d_skip[None, :, None] * inputs_x
    gated = scanned.reshape(-1, INNER) * jax.nn.silu(gate_in)
    return rms_scale(gated, gated_gain)

def layer(segments, row_in, in_weight, out_weight, norm_gain, gated_gain, conv_weight, conv_bias, a_log, d_skip, dt_bias):
    highest = lax.Precision.HIGHEST
    normed = low(rms_scale(row_in, norm_gain))
    projected = low_back(jnp.dot(normed, in_weight, precision=highest))
    gated_norm = low(mixer_core(projected, segments, conv_weight, conv_bias, a_log, d_skip, dt_bias, gated_gain))
    return row_in + jnp.dot(gated_norm, out_weight, precision=highest)

def reference(hidden, seg_ids, cotangent, in_weight, out_weight, norm_gain, gated_gain, conv_weight, conv_bias, a_log, d_skip, dt_bias):
    weight_set = tuple((part.astype(jnp.float32) for part in (in_weight, out_weight, norm_gain, gated_gain, conv_weight, conv_bias, a_log, d_skip, dt_bias)))
    rows = hidden.astype(jnp.float32).reshape(-1, TOK_DEV, D)
    cot_rows = cotangent.astype(jnp.float32).reshape(-1, TOK_DEV, D)

    def per_device(totals, block_in):
        row_in, segments, cot_row = block_in

        def local_layer(row_value, *params):
            return layer(segments, row_value, *params)
        result, back_fn = jax.vjp(local_layer, row_in, *weight_set)
        grads = back_fn(cot_row)
        totals = tuple((total + grad for total, grad in zip(totals, grads[1:])))
        return (totals, (result.astype(jnp.bfloat16), grads[0]))
    start = tuple((jnp.zeros_like(part) for part in weight_set))
    totals, (outputs, grad_rows) = lax.scan(per_device, start, (rows, seg_ids, cot_rows))
    return (outputs.reshape(-1, D), grad_rows.reshape(-1, D), totals[0], totals[1], totals[2], totals[3], totals[4], totals[5], totals[6], totals[7], totals[8])
```

```python
import functools
import jax
import jax.numpy as jnp
from jax import lax
from jax.experimental import pallas as pl
from jax.experimental.pallas import tpu as pltpu
from jax.sharding import PartitionSpec as P

HEADS = 48
HEAD_DIM = 64
STATE = 128
CONV = 4
INNER = 3072
CONV_CH = 3328
LANES = 128
EPS = 1e-05
BF = jnp.bfloat16
F32 = jnp.float32
HIGH = lax.Precision.HIGHEST
VMEM_LIMIT = 60 * 2**20


def mm(a, b):
    return jnp.dot(a, b, preferred_element_type=F32)


def mm_t(a, b):
    return lax.dot_general(a, b, (((1,), (1,)), ((), ())), preferred_element_type=F32)


def pieces(value, count):
    parts = []
    for _ in range(count):
        part = value.astype(BF)
        parts.append(part)
        value = value - part.astype(F32)
    return parts


def iota(shape, dim):
    return lax.broadcasted_iota(jnp.int32, shape, dim)


def head_of_lane(pair):
    heads, lanes = iota((LANES, LANES), 0), iota((LANES, LANES), 1)
    return (heads == 2 * pair + lanes // HEAD_DIM).astype(BF)


def one_head(head):
    return (iota((LANES, LANES), 0) == head).astype(BF)


def conv_shifts(value, masks):
    return [pltpu.roll(value, k, 0) * masks[k - 1] for k in range(1, CONV)]


def conv_apply(value, shifts, weight, bias):
    total = bias + weight[CONV - 1 : CONV] * value
    for k in range(1, CONV):
        total = total + weight[CONV - 1 - k : CONV - k] * shifts[k - 1]
    return total


def conv_back(d_pre, value, shifts, masks, weight):
    rows = d_pre.shape[0]
    d_value = weight[CONV - 1 : CONV] * d_pre
    d_weight = [jnp.sum(d_pre * value, axis=0, keepdims=True)]
    for k in range(1, CONV):
        d_weight.append(jnp.sum(d_pre * shifts[k - 1], axis=0, keepdims=True))
        d_value = d_value + weight[CONV - 1 - k : CONV - k] * pltpu.roll(
            d_pre * masks[k - 1], rows - k, 0
        )
    d_bias = jnp.sum(d_pre, axis=0, keepdims=True)
    return d_value, d_weight[::-1], d_bias


def silu_parts(value):
    sig = 1.0 / (1.0 + jnp.exp(-value))
    return sig, value * sig


def decay(col, row, clamp):
    gap = col - row
    return jnp.exp(jnp.minimum(gap, 0.0) if clamp else gap)


def wide(col, width):
    return jnp.concatenate([col] * (width // LANES), axis=1)


def forward_kernel(
    z_ref, x_ref, bc_ref, dt_ref, seg_col, seg_row, cw_ref, cb_ref, cw_bc, cb_bc, alog_ref, bias_ref,
    skip_ref, gain_ref,
    y_out, low_out, r_out, b_out, c_out, cbt_out, dt_out, cum_out, cumt_out, mask_out,
    cb_scr, dt2, cum3, gated, ssq, *, tiles
):
    pair = pl.program_id(0)
    rows = z_ref.shape[0]
    half = rows // 2

    @pl.when(pair == 0)
    def _():
        at = iota((rows, LANES), 0)
        seg = seg_col[...]
        for k in range(1, CONV):
            same = (pltpu.roll(seg, k, 0) == seg) & (at >= k)
            mask_out[k - 1] = same.astype(F32)
        masks = [mask_out[k - 1] for k in range(1, CONV)]
        outs = []
        for i in range(2):
            cols = slice(i * LANES, (i + 1) * LANES)
            value = bc_ref[:, cols]
            pre = conv_apply(value, conv_shifts(value, masks), cw_bc[:, cols], cb_bc[:, cols])
            outs.append(silu_parts(pre)[1])
        b_out[...] = outs[0]
        c_out[...] = outs[1]
        cb = lax.dot_general(
            outs[1], outs[0], (((1,), (1,)), ((), ())), precision=HIGH, preferred_element_type=F32
        )
        lower = iota((rows, rows), 0) >= iota((rows, rows), 1)
        allowed = lower & (wide(seg, rows) == seg_row[...])
        cb = jnp.where(allowed, cb, 0.0)
        cb_scr[...] = cb
        cbt_out[...] = cb.T
        live = iota((rows, LANES), 1) < HEADS
        raw = jnp.where(live, dt_ref[...] + bias_ref[...], 0.0)
        step = jnp.where(live, jnp.maximum(raw, 0.0) + jnp.log(1.0 + jnp.exp(-jnp.abs(raw))), 0.0)
        dt_out[...] = step
        hi, lo = pieces(step, 2)
        dt2[:, :LANES] = hi
        dt2[:, LANES:] = lo
        log_rate = step * -jnp.exp(alog_ref[...])
        tri = lower.astype(BF)
        cum = sum(mm(tri, part) for part in pieces(log_rate, 3)[::-1])
        cum_out[...] = cum
        cumt_out[...] = cum.T
        for i, part in enumerate(pieces(cum, 3)):
            cum3[:, i * LANES : (i + 1) * LANES] = part
        ssq[...] = jnp.zeros_like(ssq)

    masks = [mask_out[k - 1] for k in range(1, CONV)]
    value = x_ref[...]
    pre = conv_apply(value, conv_shifts(value, masks), cw_ref[...], cb_ref[...])
    x = silu_parts(pre)[1]
    spread = head_of_lane(pair)
    step = mm(dt2[...], jnp.concatenate([spread, spread], axis=0))
    xt = (x * step).astype(BF)
    first = iota((rows, LANES), 1) < HEAD_DIM
    ys = []
    for side in range(2):
        head = 2 * pair + side
        pick = one_head(head)
        col = mm(cum3[...], jnp.concatenate([pick] * 3, axis=0))
        row = cumt_out[pl.ds(head, 1), :]
        low_row, high_row = row[:, :half], row[:, half:]
        top, bottom = wide(col[:half], half), wide(col[half:], half)
        m00 = (decay(top, low_row, True) * cb_scr[:half, :half]).astype(BF)
        m10 = (decay(bottom, low_row, False) * cb_scr[half:, :half]).astype(BF)
        m11 = (decay(bottom, high_row, True) * cb_scr[half:, half:]).astype(BF)
        ys.append(
            jnp.concatenate([mm(m00, xt[:half]), mm(m10, xt[:half]) + mm(m11, xt[half:])], axis=0)
        )
    y = jnp.where(first, ys[0], ys[1])
    y_out[...] = y
    g = (y + skip_ref[...] * x) * silu_parts(z_ref[...])[1]
    gated[pair] = g
    ssq[...] += g * g

    @pl.when(pair == tiles - 1)
    def _():
        mean = jnp.sum(ssq[...], axis=1, keepdims=True) * (1.0 / (tiles * LANES))
        r = jnp.broadcast_to(lax.rsqrt(mean + EPS), (rows, LANES))
        r_out[...] = r

        def write(i, carry):
            cols = pl.ds(pl.multiple_of(i * LANES, LANES), LANES)
            low_out[:, cols] = (gated[i] * r * gain_ref[:, cols]).astype(BF)
            return carry

        lax.fori_loop(0, tiles, write, 0)


def whole(shape):
    return pl.BlockSpec(shape, lambda i: (0,) * len(shape))


def mixer_forward(proj, seg_col, seg_row, conv_w, conv_b, a_log, d_skip, dt_bias, gain):
    rows = proj.shape[0]
    tiles = INNER // LANES
    tile = lambda offset: pl.BlockSpec((rows, LANES), lambda i: (0, offset + i))
    lane = lambda n: pl.BlockSpec((n, LANES), lambda i: (0, i))
    f = lambda *s: jax.ShapeDtypeStruct(s, F32)
    out_shape = [
        f(rows, INNER), jax.ShapeDtypeStruct((rows, INNER), BF), f(rows, LANES), f(rows, LANES), f(rows, LANES),
        f(rows, rows), f(rows, LANES), f(rows, LANES), f(LANES, rows), f(CONV - 1, rows, LANES),
    ]
    return pl.pallas_call(
        functools.partial(forward_kernel, tiles=tiles),
        grid=(tiles,),
        in_specs=[
            tile(0), tile(tiles),
            pl.BlockSpec((rows, 2 * LANES), lambda i: (0, tiles)),
            pl.BlockSpec((rows, LANES), lambda i: (0, 2 * tiles + 2)),
            whole((rows, LANES)), whole((1, rows)), lane(CONV), lane(1),
            pl.BlockSpec((CONV, 2 * LANES), lambda i: (0, tiles // 2)),
            pl.BlockSpec((1, 2 * LANES), lambda i: (0, tiles // 2)),
            whole((1, LANES)), whole((1, LANES)), lane(1), whole((1, INNER)),
        ],
        out_specs=[tile(0)] + [whole(s.shape) for s in out_shape[1:]],
        out_shape=out_shape,
        scratch_shapes=[
            pltpu.VMEM((rows, rows), F32), pltpu.VMEM((rows, 2 * LANES), BF), pltpu.VMEM((rows, 3 * LANES), BF),
            pltpu.VMEM((tiles, rows, LANES), F32), pltpu.VMEM((rows, LANES), F32),
        ],
        compiler_params=pltpu.CompilerParams(vmem_limit_bytes=VMEM_LIMIT),
        cost_estimate=pl.CostEstimate(flops=10**10, bytes_accessed=40 * 10**6, transcendentals=10**7),
        name="mixer_forward",
    )(proj, proj, proj, proj, seg_col, seg_row, conv_w, conv_b, conv_w, conv_b, a_log, dt_bias, d_skip, gain)


def backward_kernel(
    z_ref, x_ref, bc_ref, dtraw_ref, y_ref, dgn_ref, r_ref, rd_ref, b_ref, c_ref, cbt_ref, dt_ref, cum_ref,
    cumt_ref, mask_ref, seg_col, seg_row, cw_ref, cb_ref, cw_bc, cb_bc, alog_ref, bias_ref, skip_ref, gain_ref,
    dz_out, dx_out, dbc_out, dgain_out, dskip_out, dcw_out, dcb_out, dcwbc_out, dcbbc_out, dalog_out, dbias_out,
    dt2, cum3, g_scr, dcum, ddt, *, tiles
):
    pair = pl.program_id(0)
    rows = z_ref.shape[0]
    half = rows // 2

    @pl.when(pair == 0)
    def _():
        hi, lo = pieces(dt_ref[...], 2)
        dt2[:, :LANES] = hi
        dt2[:, LANES:] = lo
        for i, part in enumerate(pieces(cum_ref[...], 3)):
            cum3[:, i * LANES : (i + 1) * LANES] = part
        g_scr[...] = jnp.zeros_like(g_scr)
        dcum[...] = jnp.zeros_like(dcum)
        ddt[...] = jnp.zeros_like(ddt)

    masks = [mask_ref[k - 1] for k in range(1, CONV)]
    value = x_ref[...]
    shifts = conv_shifts(value, masks)
    pre = conv_apply(value, shifts, cw_ref[...], cb_ref[...])
    sp, x = silu_parts(pre)
    z = z_ref[...]
    sg, sz = silu_parts(z)
    y = y_ref[...]
    scanned = y + skip_ref[...] * x
    g = scanned * sz
    r = r_ref[...]
    dgn = dgn_ref[...]
    dgn_r = dgn * r
    dgain_out[...] = jnp.sum(dgn_r * g, axis=0, keepdims=True)
    dg = gain_ref[...] * dgn_r - g * rd_ref[...]
    dz_out[...] = (dg * scanned * (sg * (1.0 + z * (1.0 - sg)))).astype(BF)
    dsc = dg * sz
    dskip_out[...] = jnp.sum(dsc * x, axis=0, keepdims=True)
    dy = dsc.astype(BF)
    spread = head_of_lane(pair)
    step = mm(dt2[...], jnp.concatenate([spread, spread], axis=0))
    xt = (x * step).astype(BF)
    first = iota((rows, LANES), 1) < HEAD_DIM
    zero = jnp.zeros_like(xt)
    dxts = []
    for side in range(2):
        head = 2 * pair + side
        pick = one_head(head)
        col = mm(cum3[...], jnp.concatenate([pick] * 3, axis=0))
        row = cumt_ref[pl.ds(head, 1), :]
        low_row, high_row = row[:, :half], row[:, half:]
        top, bottom = wide(col[:half], half), wide(col[half:], half)
        xs = jnp.where(first == (side == 0), xt, zero)
        parts = []
        for js, is_, jcol, irow, clamp in (
            (slice(0, half), slice(0, half), top, low_row, True),
            (slice(0, half), slice(half, rows), top, high_row, False),
            (slice(half, rows), slice(half, rows), bottom, high_row, True),
        ):
            e = decay(irow, jcol, clamp)
            parts.append(mm((e * cbt_ref[js, is_]).astype(BF), dy[is_]))
            g_scr[js, is_] += e * mm_t(xs[js], dy[is_])
        dxts.append(jnp.concatenate([parts[0] + parts[1], parts[2]], axis=0))
    dxt = jnp.where(first, dxts[0], dxts[1])
    gather = head_of_lane(pair)
    for ref, q in ((dcum, dy.astype(F32) * y - xt.astype(F32) * dxt), (ddt, x * dxt)):
        hi, lo = pieces(q, 2)
        ref[...] += mm_t(hi, gather) + mm_t(lo, gather)
    dx = skip_ref[...] * dsc + step * dxt
    d_pre = dx * (sp * (1.0 + pre * (1.0 - sp)))
    d_value, d_weight, d_bias = conv_back(d_pre, value, shifts, masks, cw_ref[...])
    dx_out[...] = d_value.astype(BF)
    for k in range(CONV):
        dcw_out[k : k + 1, :] = d_weight[k]
    dcb_out[...] = d_bias

    @pl.when(pair == tiles - 1)
    def _():
        same = wide(seg_col[...], rows) == seg_row[...]
        later = (iota((rows, rows), 0) <= iota((rows, rows), 1)) & same
        gt = jnp.where(later, g_scr[...], 0.0)
        db = jnp.dot(gt, c_ref[...], precision=HIGH, preferred_element_type=F32)
        dc = jnp.dot(gt.T, b_ref[...], precision=HIGH, preferred_element_type=F32)
        for i, d_out in enumerate((db, dc)):
            cols = slice(i * LANES, (i + 1) * LANES)
            value = bc_ref[:, cols]
            shifts = conv_shifts(value, masks)
            pre = conv_apply(value, shifts, cw_bc[:, cols], cb_bc[:, cols])
            sp, _ = silu_parts(pre)
            d_pre = d_out * (sp * (1.0 + pre * (1.0 - sp)))
            d_value, d_weight, d_bias = conv_back(d_pre, value, shifts, masks, cw_bc[:, cols])
            dbc_out[:, cols] = d_value.astype(BF)
            for k in range(CONV):
                dcwbc_out[k : k + 1, cols] = d_weight[k]
            dcbbc_out[:, cols] = d_bias
        step = dt_ref[...]
        live = iota((rows, LANES), 1) < HEADS
        rate = -jnp.exp(alog_ref[...])
        later_bf = later.astype(BF)
        dlog = sum(mm(later_bf, part) for part in pieces(dcum[...], 3)[::-1])
        dstep = ddt[...] + dlog * rate
        raw = jnp.where(live, dtraw_ref[...] + bias_ref[...], 0.0)
        draw = jnp.where(live, dstep / (1.0 + jnp.exp(-raw)), 0.0)
        dbc_out[:, 2 * LANES :] = draw.astype(BF)
        dalog_out[...] = jnp.sum(dlog * step, axis=0, keepdims=True) * rate
        dbias_out[...] = jnp.sum(draw, axis=0, keepdims=True)


def mixer_backward(proj, saved, dgn, rd, seg_col, seg_row, conv_w, conv_b, a_log, d_skip, dt_bias, gain):
    y, _, r, b, c, cbt, dt, cum, cumt, mask = saved
    rows = proj.shape[0]
    tiles = INNER // LANES
    tile = lambda offset: pl.BlockSpec((rows, LANES), lambda i: (0, offset + i))
    lane = lambda n: pl.BlockSpec((n, LANES), lambda i: (0, i))
    f = lambda *s: jax.ShapeDtypeStruct(s, F32)
    h = lambda *s: jax.ShapeDtypeStruct(s, BF)
    bc_w = pl.BlockSpec((CONV, 2 * LANES), lambda i: (0, tiles // 2))
    bc_b = pl.BlockSpec((1, 2 * LANES), lambda i: (0, tiles // 2))
    return pl.pallas_call(
        functools.partial(backward_kernel, tiles=tiles),
        grid=(tiles,),
        in_specs=[
            tile(0), tile(tiles),
            pl.BlockSpec((rows, 2 * LANES), lambda i: (0, tiles)),
            pl.BlockSpec((rows, LANES), lambda i: (0, 2 * tiles + 2)),
            tile(0), tile(0), whole((rows, LANES)), whole((rows, LANES)), whole((rows, LANES)), whole((rows, LANES)),
            whole((rows, rows)), whole((rows, LANES)), whole((rows, LANES)), whole((LANES, rows)),
            whole((CONV - 1, rows, LANES)), whole((rows, LANES)), whole((1, rows)), lane(CONV), lane(1), bc_w, bc_b,
            whole((1, LANES)), whole((1, LANES)), lane(1), lane(1),
        ],
        out_specs=[
            tile(0), tile(0), whole((rows, 3 * LANES)), lane(1), lane(1), lane(CONV), lane(1),
            whole((CONV, 2 * LANES)), whole((1, 2 * LANES)), whole((1, LANES)), whole((1, LANES)),
        ],
        out_shape=[
            h(rows, INNER), h(rows, INNER), h(rows, 3 * LANES), f(1, INNER), f(1, INNER), f(CONV, INNER), f(1, INNER),
            f(CONV, 2 * LANES), f(1, 2 * LANES), f(1, LANES), f(1, LANES),
        ],
        scratch_shapes=[
            pltpu.VMEM((rows, 2 * LANES), BF), pltpu.VMEM((rows, 3 * LANES), BF), pltpu.VMEM((rows, rows), F32),
            pltpu.VMEM((rows, LANES), F32), pltpu.VMEM((rows, LANES), F32),
        ],
        compiler_params=pltpu.CompilerParams(vmem_limit_bytes=VMEM_LIMIT),
        cost_estimate=pl.CostEstimate(flops=2 * 10**10, bytes_accessed=60 * 10**6, transcendentals=10**7),
        name="mixer_backward",
    )(
        proj, proj, proj, proj, y, dgn, r, rd, b, c, cbt, dt, cum, cumt, mask, seg_col, seg_row,
        conv_w, conv_b, conv_w, conv_b, a_log, dt_bias, d_skip, gain,
    )


def rows_scale(value):
    return lax.rsqrt(jnp.mean(value * value, axis=-1, keepdims=True) + EPS)


def per_device(
    hidden, seg_ids, cotangent, in_weight, out_weight, norm_gain, gated_gain, conv_weight, conv_bias, a_log, d_skip,
    dt_bias,
):
    rep, shards = lax.axis_size("rep"), lax.axis_size("shard")
    rows = hidden.shape[0]
    rep_at, shard_at = lax.axis_index("rep"), lax.axis_index("shard")

    def gather(weight):
        part = weight.shape[0] // rep
        mine = lax.dynamic_slice_in_dim(weight, rep_at * part, part, 0)
        return lax.all_gather(mine, ("shard", "rep"), axis=0, tiled=True)

    smalls = (norm_gain, gated_gain, conv_weight.reshape(-1), conv_bias, a_log, d_skip, dt_bias)
    sizes = [part.shape[0] for part in smalls]
    packed = lax.all_gather(jnp.concatenate(smalls), "shard", axis=0).astype(F32)
    starts = [sum(sizes[:i]) for i in range(len(sizes))]
    cuts = [packed[:, at : at + size] for at, size in zip(starts, sizes)]
    ngain, ggain, cb, alog, dskip, dtb = (cuts[i].reshape(1, -1) for i in (0, 1, 3, 4, 5, 6))
    cw = cuts[2].reshape(shards, CONV, -1).transpose(1, 0, 2).reshape(CONV, -1)
    pad = lambda v: jnp.pad(v, ((0, 0), (0, LANES - HEADS)))
    alog, dtb = pad(alog), pad(dtb)
    dskip = jnp.repeat(dskip, HEAD_DIM, axis=1)
    in_full, out_full = gather(in_weight), gather(out_weight)

    residual = hidden.astype(F32)
    scale = rows_scale(residual)
    unit = residual * scale
    normed = (unit * ngain).astype(BF)
    proj = mm(normed, in_full)
    seg_col = jnp.broadcast_to(seg_ids[0][:, None], (rows, LANES))
    shared = (seg_col, seg_ids, cw, cb, alog, dskip, dtb, ggain)
    saved = mixer_forward(proj, *shared)
    low, r = saved[1], saved[2]
    mixed = (residual + mm(low, out_full)).astype(BF)
    d_gated = mm_t(cotangent, out_full)
    rowdot = jnp.sum(d_gated * low.astype(F32), axis=1, keepdims=True)
    rd = r * r * (rowdot * (1.0 / INNER))
    first = (((0,), (0,)), ((), ()))
    grad_out = lax.dot_general(low, cotangent, first, preferred_element_type=F32)
    dz, dx, dbc, dgain, dsk, dcw, dcb, dcwb, dcbb, dal, dbias = mixer_backward(proj, saved, d_gated, rd, *shared)
    d_proj = jnp.concatenate([dz, dx, dbc[:, : 2 * STATE + HEADS]], axis=1)
    d_normed = mm_t(d_proj, in_full)
    grad_in = lax.dot_general(normed, d_proj, first, preferred_element_type=F32)
    grad_norm = jnp.sum(d_normed * unit, axis=0)
    du = d_normed * ngain
    grad_hidden = cotangent.astype(F32) + scale * (du - unit * jnp.mean(du * unit, axis=1, keepdims=True))

    def reduce(grad):
        part = lax.psum_scatter(grad.astype(BF), ("shard", "rep"), scatter_dimension=0, tiled=True)
        return lax.all_gather(part, "rep", axis=0, tiled=True).astype(F32)

    g_in, g_out = reduce(grad_in), reduce(grad_out)
    dcw = jnp.concatenate([dcw, dcwb], axis=1)
    dcb = jnp.concatenate([dcb, dcbb], axis=1)
    own = lambda v: v.reshape(shards, -1)
    small_grads = (
        own(grad_norm), own(dgain), dcw.reshape(CONV, shards, -1).transpose(1, 0, 2).reshape(shards, -1), own(dcb),
        own(dal[:, :HEADS]), own(dsk.reshape(HEADS, HEAD_DIM).sum(1)), own(dbias[:, :HEADS]),
    )
    total = lax.psum(jnp.concatenate(small_grads, axis=1), ("rep", "shard"))
    mine = lax.dynamic_index_in_dim(total, shard_at, 0, keepdims=False)
    outs = [mine[at : at + size] for at, size in zip(starts, sizes)]
    outs[2] = outs[2].reshape(CONV, -1)
    return (mixed, grad_hidden, g_in, g_out, *outs)


def solution(mesh):
    both = ("rep", "shard")
    shard = P("shard")
    placed = (P(both, None), P(both, None), P(both, None), P("shard", None), P("shard", None), shard, shard,
              P(None, "shard"), shard, shard, shard, shard)
    outs = (P(both, None), P(both, None), P("shard", None), P("shard", None), shard, shard, P(None, "shard"), shard,
            shard, shard, shard)
    return jax.shard_map(per_device, mesh=mesh, in_specs=placed, out_specs=outs, check_vma=False)
```

```python
import functools
import jax
import jax.numpy as jnp
from jax import lax
from jax.experimental import pallas as pl
from jax.experimental.pallas import tpu as pltpu
from jax.sharding import PartitionSpec as P

HEADS = 48
HEAD_DIM = 64
STATE = 128
CONV = 4
INNER = 3072
CONV_CH = 3328
LANES = 128
EPS = 1e-05
BF = jnp.bfloat16
F32 = jnp.float32
HIGH = lax.Precision.HIGHEST
VMEM_LIMIT = 60 * 2**20
MESH = pl.DeviceIdType.MESH


def mm(a, b):
    return jnp.dot(a, b, preferred_element_type=F32)


def mm_t(a, b):
    return lax.dot_general(a, b, (((1,), (1,)), ((), ())), preferred_element_type=F32)


def pieces(value, count):
    parts = []
    for _ in range(count):
        part = value.astype(BF)
        parts.append(part)
        value = value - part.astype(F32)
    return parts


def iota(shape, dim):
    return lax.broadcasted_iota(jnp.int32, shape, dim)


def head_of_lane(pair):
    heads, lanes = iota((LANES, LANES), 0), iota((LANES, LANES), 1)
    return (heads == 2 * pair + lanes // HEAD_DIM).astype(BF)


def one_head(head):
    return (iota((LANES, LANES), 0) == head).astype(BF)


def conv_shifts(value, masks):
    return [pltpu.roll(value, k, 0) * masks[k - 1] for k in range(1, CONV)]


def conv_apply(value, shifts, weight, bias):
    total = bias + weight[CONV - 1 : CONV] * value
    for k in range(1, CONV):
        total = total + weight[CONV - 1 - k : CONV - k] * shifts[k - 1]
    return total


def conv_back(d_pre, value, shifts, masks, weight):
    rows = d_pre.shape[0]
    d_value = weight[CONV - 1 : CONV] * d_pre
    d_weight = [jnp.sum(d_pre * value, axis=0, keepdims=True)]
    for k in range(1, CONV):
        d_weight.append(jnp.sum(d_pre * shifts[k - 1], axis=0, keepdims=True))
        d_value = d_value + weight[CONV - 1 - k : CONV - k] * pltpu.roll(
            d_pre * masks[k - 1], rows - k, 0
        )
    d_bias = jnp.sum(d_pre, axis=0, keepdims=True)
    return d_value, d_weight[::-1], d_bias


def silu_parts(value):
    sig = 1.0 / (1.0 + jnp.exp(-value))
    return sig, value * sig


def decay(col, row, clamp):
    gap = col - row
    return jnp.exp(jnp.minimum(gap, 0.0) if clamp else gap)


def wide(col, width):
    return jnp.concatenate([col] * (width // LANES), axis=1)


def forward_kernel(
    z_ref, x_ref, bc_ref, dt_ref, seg_col, seg_row, cw_ref, cb_ref, cw_bc, cb_bc, alog_ref, bias_ref,
    skip_ref, gain_ref,
    y_out, low_out, r_out, b_out, c_out, cbt_out, dt_out, cum_out, cumt_out, mask_out,
    cb_scr, dt2, cum3, gated, ssq, *, tiles
):
    pair = pl.program_id(0)
    rows = z_ref.shape[0]
    half = rows // 2

    @pl.when(pair == 0)
    def _():
        at = iota((rows, LANES), 0)
        seg = seg_col[...]
        for k in range(1, CONV):
            same = (pltpu.roll(seg, k, 0) == seg) & (at >= k)
            mask_out[k - 1] = same.astype(F32)
        masks = [mask_out[k - 1] for k in range(1, CONV)]
        outs = []
        for i in range(2):
            cols = slice(i * LANES, (i + 1) * LANES)
            value = bc_ref[:, cols]
            pre = conv_apply(value, conv_shifts(value, masks), cw_bc[:, cols], cb_bc[:, cols])
            outs.append(silu_parts(pre)[1])
        b_out[...] = outs[0]
        c_out[...] = outs[1]
        cb = lax.dot_general(
            outs[1], outs[0], (((1,), (1,)), ((), ())), precision=HIGH, preferred_element_type=F32
        )
        lower = iota((rows, rows), 0) >= iota((rows, rows), 1)
        allowed = lower & (wide(seg, rows) == seg_row[...])
        cb = jnp.where(allowed, cb, 0.0)
        cb_scr[...] = cb
        cbt_out[...] = cb.T
        live = iota((rows, LANES), 1) < HEADS
        raw = jnp.where(live, dt_ref[...] + bias_ref[...], 0.0)
        step = jnp.where(live, jnp.maximum(raw, 0.0) + jnp.log(1.0 + jnp.exp(-jnp.abs(raw))), 0.0)
        dt_out[...] = step
        hi, lo = pieces(step, 2)
        dt2[:, :LANES] = hi
        dt2[:, LANES:] = lo
        log_rate = step * -jnp.exp(alog_ref[...])
        tri = lower.astype(BF)
        cum = sum(mm(tri, part) for part in pieces(log_rate, 3)[::-1])
        cum_out[...] = cum
        cumt_out[...] = cum.T
        for i, part in enumerate(pieces(cum, 3)):
            cum3[:, i * LANES : (i + 1) * LANES] = part
        ssq[...] = jnp.zeros_like(ssq)

    masks = [mask_out[k - 1] for k in range(1, CONV)]
    value = x_ref[...]
    pre = conv_apply(value, conv_shifts(value, masks), cw_ref[...], cb_ref[...])
    x = silu_parts(pre)[1]
    spread = head_of_lane(pair)
    step = mm(dt2[...], jnp.concatenate([spread, spread], axis=0))
    xt = (x * step).astype(BF)
    first = iota((rows, LANES), 1) < HEAD_DIM
    ys = []
    for side in range(2):
        head = 2 * pair + side
        pick = one_head(head)
        col = mm(cum3[...], jnp.concatenate([pick] * 3, axis=0))
        row = cumt_out[pl.ds(head, 1), :]
        low_row, high_row = row[:, :half], row[:, half:]
        top, bottom = wide(col[:half], half), wide(col[half:], half)
        m00 = (decay(top, low_row, True) * cb_scr[:half, :half]).astype(BF)
        m10 = (decay(bottom, low_row, False) * cb_scr[half:, :half]).astype(BF)
        m11 = (decay(bottom, high_row, True) * cb_scr[half:, half:]).astype(BF)
        ys.append(
            jnp.concatenate([mm(m00, xt[:half]), mm(m10, xt[:half]) + mm(m11, xt[half:])], axis=0)
        )
    y = jnp.where(first, ys[0], ys[1])
    y_out[...] = y
    g = (y + skip_ref[...] * x) * silu_parts(z_ref[...])[1]
    gated[pair] = g
    ssq[...] += g * g

    @pl.when(pair == tiles - 1)
    def _():
        mean = jnp.sum(ssq[...], axis=1, keepdims=True) * (1.0 / (tiles * LANES))
        r = jnp.broadcast_to(lax.rsqrt(mean + EPS), (rows, LANES))
        r_out[...] = r

        def write(i, carry):
            cols = pl.ds(pl.multiple_of(i * LANES, LANES), LANES)
            low_out[:, cols] = (gated[i] * r * gain_ref[:, cols]).astype(BF)
            return carry

        lax.fori_loop(0, tiles, write, 0)


def whole(shape):
    return pl.BlockSpec(shape, lambda i: (0,) * len(shape))


def mixer_forward(proj, seg_col, seg_row, conv_w, conv_b, a_log, d_skip, dt_bias, gain):
    rows = proj.shape[0]
    tiles = INNER // LANES
    tile = lambda offset: pl.BlockSpec((rows, LANES), lambda i: (0, offset + i))
    lane = lambda n: pl.BlockSpec((n, LANES), lambda i: (0, i))
    f = lambda *s: jax.ShapeDtypeStruct(s, F32)
    out_shape = [
        f(rows, INNER), jax.ShapeDtypeStruct((rows, INNER), BF), f(rows, LANES), f(rows, LANES), f(rows, LANES),
        f(rows, rows), f(rows, LANES), f(rows, LANES), f(LANES, rows), f(CONV - 1, rows, LANES),
    ]
    return pl.pallas_call(
        functools.partial(forward_kernel, tiles=tiles),
        grid=(tiles,),
        in_specs=[
            tile(0), tile(tiles),
            pl.BlockSpec((rows, 2 * LANES), lambda i: (0, tiles)),
            pl.BlockSpec((rows, LANES), lambda i: (0, 2 * tiles + 2)),
            whole((rows, LANES)), whole((1, rows)), lane(CONV), lane(1),
            pl.BlockSpec((CONV, 2 * LANES), lambda i: (0, tiles // 2)),
            pl.BlockSpec((1, 2 * LANES), lambda i: (0, tiles // 2)),
            whole((1, LANES)), whole((1, LANES)), lane(1), whole((1, INNER)),
        ],
        out_specs=[tile(0)] + [whole(s.shape) for s in out_shape[1:]],
        out_shape=out_shape,
        scratch_shapes=[
            pltpu.VMEM((rows, rows), F32), pltpu.VMEM((rows, 2 * LANES), BF), pltpu.VMEM((rows, 3 * LANES), BF),
            pltpu.VMEM((tiles, rows, LANES), F32), pltpu.VMEM((rows, LANES), F32),
        ],
        compiler_params=pltpu.CompilerParams(vmem_limit_bytes=VMEM_LIMIT),
        cost_estimate=pl.CostEstimate(flops=10**10, bytes_accessed=40 * 10**6, transcendentals=10**7),
        name="mixer_forward",
    )(proj, proj, proj, proj, seg_col, seg_row, conv_w, conv_b, conv_w, conv_b, a_log, dt_bias, d_skip, gain)


def backward_pair(
    pair, z, value, y, dgn, r, rd, cw, cb, skip, gain, masks, dt2, cum3, cumt_ref, cbt_ref, g_scr, dcum, ddt
):
    rows = z.shape[0]
    half = rows // 2
    shifts = conv_shifts(value, masks)
    pre = conv_apply(value, shifts, cw, cb)
    sp, x = silu_parts(pre)
    sg, sz = silu_parts(z)
    scanned = y + skip * x
    g = scanned * sz
    dgn_r = dgn * r
    d_gain = jnp.sum(dgn_r * g, axis=0, keepdims=True)
    dg = gain * dgn_r - g * rd
    dz = (dg * scanned * (sg * (1.0 + z * (1.0 - sg)))).astype(BF)
    dsc = dg * sz
    d_skip = jnp.sum(dsc * x, axis=0, keepdims=True)
    dy = dsc.astype(BF)
    spread = head_of_lane(pair)
    step = mm(dt2[...], jnp.concatenate([spread, spread], axis=0))
    xt = (x * step).astype(BF)
    first = iota((rows, LANES), 1) < HEAD_DIM
    zero = jnp.zeros_like(xt)
    dxts = []
    for side in range(2):
        head = 2 * pair + side
        pick = one_head(head)
        col = mm(cum3[...], jnp.concatenate([pick] * 3, axis=0))
        row = cumt_ref[pl.ds(head, 1), :]
        low_row, high_row = row[:, :half], row[:, half:]
        top, bottom = wide(col[:half], half), wide(col[half:], half)
        xs = jnp.where(first == (side == 0), xt, zero)
        parts = []
        for js, is_, jcol, irow, clamp in (
            (slice(0, half), slice(0, half), top, low_row, True),
            (slice(0, half), slice(half, rows), top, high_row, False),
            (slice(half, rows), slice(half, rows), bottom, high_row, True),
        ):
            e = decay(irow, jcol, clamp)
            parts.append(mm((e * cbt_ref[js, is_]).astype(BF), dy[is_]))
            g_scr[js, is_] += e * mm_t(xs[js], dy[is_])
        dxts.append(jnp.concatenate([parts[0] + parts[1], parts[2]], axis=0))
    dxt = jnp.where(first, dxts[0], dxts[1])
    for ref, term in ((dcum, dy.astype(F32) * y - xt.astype(F32) * dxt), (ddt, x * dxt)):
        hi, lo = pieces(term, 2)
        ref[...] += mm_t(hi, spread) + mm_t(lo, spread)
    dx = skip * dsc + step * dxt
    d_pre = dx * (sp * (1.0 + pre * (1.0 - sp)))
    d_value, d_weight, d_bias = conv_back(d_pre, value, shifts, masks, cw)
    return dz, d_value.astype(BF), d_gain, d_skip, d_weight, d_bias


def backward_tail(
    bc_ref, dtraw_ref, b_ref, c_ref, dt_ref, masks, seg_col, seg_row, cw_bc, cb_bc, alog_ref, bias_ref,
    g_scr, dcum, ddt
):
    rows = dt_ref.shape[0]
    same = wide(seg_col[...], rows) == seg_row[...]
    later = (iota((rows, rows), 0) <= iota((rows, rows), 1)) & same
    gt = jnp.where(later, g_scr[...], 0.0)
    db = jnp.dot(gt, c_ref[...], precision=HIGH, preferred_element_type=F32)
    dc = jnp.dot(gt.T, b_ref[...], precision=HIGH, preferred_element_type=F32)
    d_bc, d_weights, d_biases = [], [], []
    for i, d_out in enumerate((db, dc)):
        cols = slice(i * LANES, (i + 1) * LANES)
        value = bc_ref[:, cols]
        shifts = conv_shifts(value, masks)
        pre = conv_apply(value, shifts, cw_bc[:, cols], cb_bc[:, cols])
        sp, _ = silu_parts(pre)
        d_pre = d_out * (sp * (1.0 + pre * (1.0 - sp)))
        d_value, d_weight, d_bias = conv_back(d_pre, value, shifts, masks, cw_bc[:, cols])
        d_bc.append(d_value)
        d_weights.append(d_weight)
        d_biases.append(d_bias)
    step = dt_ref[...]
    live = iota((rows, LANES), 1) < HEADS
    rate = -jnp.exp(alog_ref[...])
    later_bf = later.astype(BF)
    dlog = sum(mm(later_bf, part) for part in pieces(dcum[...], 3)[::-1])
    dstep = ddt[...] + dlog * rate
    raw = jnp.where(live, dtraw_ref[...] + bias_ref[...], 0.0)
    d_raw = jnp.where(live, dstep / (1.0 + jnp.exp(-raw)), 0.0)
    d_alog = jnp.sum(dlog * step, axis=0, keepdims=True) * rate
    return d_bc, d_raw, d_weights, d_biases, d_alog, jnp.sum(d_raw, axis=0, keepdims=True)


class Place:
    def __init__(self, rep, shards):
        self.rep, self.shards = rep, shards
        r, self.me = lax.axis_index("rep"), lax.axis_index("shard")
        self.r = r
        self.core, self.a, self.b = r % 2, (r // 2) % 2, (r // 4) % 2
        self.core_peer = (r + 1 - 2 * self.core, self.me)
        self.a_peer = (r + 2 - 4 * self.a, self.me)
        self.b_peer = (r + 4 - 8 * self.b, self.me)
        self.extra = []
        stride = 8
        while stride < rep:
            bit = (r // stride) % 2
            self.extra.append((r + stride - 2 * stride * bit, self.me))
            stride *= 2
        self.quarter = 2 * self.a + self.b

    def shard_peer(self, distance):
        return (self.r, (self.me + distance) % self.shards)

    def partners(self):
        return [self.core_peer, self.a_peer, self.b_peer, *self.extra] + [
            self.shard_peer(d) for d in range(1, self.shards)
        ]

    def greet(self):
        barrier = pltpu.get_barrier_semaphore()
        partners = self.partners()
        for partner in partners:
            pl.semaphore_signal(barrier, inc=1, device_id=partner, device_id_type=MESH)
        pl.semaphore_wait(barrier, len(partners))


def remote(src, dst, send, recv, device):
    return pltpu.make_async_remote_copy(
        src_ref=src, dst_ref=dst, send_sem=send, recv_sem=recv, device_id=device, device_id_type=MESH
    )


class SmallSum:
    def __init__(self, place, buf, slots, sends, recvs):
        self.buf, self.slots, self.sends, self.recvs = buf, slots, sends, recvs
        pairs = [place.core_peer, place.a_peer, place.b_peer, *place.extra]
        self.groups = [[peer] for peer in pairs] + [[place.shard_peer(d) for d in range(1, place.shards)]]
        self.stages = len(self.groups) + 1

    @staticmethod
    def count(rep, shards):
        return rep.bit_length() - 1 + shards - 1

    def copies(self, group):
        at = sum(len(g) for g in self.groups[:group])
        return [
            remote(self.buf, self.slots.at[at + i], self.sends.at[at + i], self.recvs.at[at + i], peer)
            for i, peer in enumerate(self.groups[group])
        ]

    def stage(self, number):
        if number > 0:
            at = sum(len(g) for g in self.groups[: number - 1])
            copies = self.copies(number - 1)
            for copy in copies:
                copy.wait()
            total = self.buf[...]
            for i in range(len(copies)):
                total = total + self.slots[at + i]
            self.buf[...] = total
        if number < len(self.groups):
            for copy in self.copies(number):
                copy.start()


def reduce_kernel(
    z_ref, x_ref, y_ref, dgn_ref, cw_ref, cb_ref, skip_ref, gain_ref,
    bc_ref, dtraw_ref, r_ref, rd_ref, b_ref, c_ref, cbt_ref, dt_ref, cum_ref, cumt_ref, mask_ref, seg_col, seg_row,
    cw_bc, cb_bc, alog_ref, bias_ref,
    w_ref, low_t, cot_ref, normed_t, hidden_ref, ngain_ref,
    gin_out, gout_out, gh_out, small_out, norm_out,
    dt2, cum3, g_scr, dcum, ddt, dp, dn,
    keep1, send1, recv1, keep2, send2, recv2, keep3, send3, recv3, keep4, send4, recv4, ag,
    slots_small, slots_norm,
    s1, r1, s2, r2, s3, r3, s4, r4, s5, r5, s6, r6, l7, s7, r7, xtra, sx, rx, ss, rs, sn, rn,
    *, rep, shards, q, blocks, n_out, n_in, tail
):
    step = pl.program_id(0)
    place = Place(rep, shards)
    rows = z_ref.shape[0]
    per = INNER // LANES // blocks
    chunks = n_out + n_in
    a, b, core, me, quarter = place.a, place.b, place.core, place.me, place.quarter

    small = SmallSum(place, small_out, slots_small, ss, rs)
    norm = SmallSum(place, norm_out, slots_norm, sn, rn)

    @pl.when(step == 0)
    def _():
        place.greet()
        small_out[...] = jnp.zeros_like(small_out)
        norm_out[...] = jnp.zeros_like(norm_out)
        dn[...] = jnp.zeros_like(dn)
        hi, lo = pieces(dt_ref[...], 2)
        dt2[:, :LANES] = hi
        dt2[:, LANES:] = lo
        for i, part in enumerate(pieces(cum_ref[...], 3)):
            cum3[:, i * LANES : (i + 1) * LANES] = part
        g_scr[...] = jnp.zeros_like(g_scr)
        dcum[...] = jnp.zeros_like(dcum)
        ddt[...] = jnp.zeros_like(ddt)

    def copy1(k):
        return [remote(send1.at[k], recv1.at[k], s1.at[k], r1.at[k], place.core_peer)]

    def copy2(k):
        return [
            remote(send2.at[k, o], recv2.at[k, o], s2.at[k, o], r2.at[k, o], peer)
            for o, peer in enumerate((place.a_peer, place.b_peer))
        ]

    def copy3(k):
        return [
            remote(send3.at[k, o], recv3.at[k, o], s3.at[k, o], r3.at[k, o], peer)
            for o, peer in enumerate((place.b_peer, place.a_peer))
        ]

    def copy4(k):
        return [
            remote(send4.at[k, d - 1], recv4.at[k, d - 1], s4.at[k, d - 1], r4.at[k, d - 1], place.shard_peer(d))
            for d in range(1, shards)
        ]

    def block(g, quarter):
        return ag.at[g, :, pl.ds(pl.multiple_of(quarter * q, q), q)]

    def half_block(g, o, quarter):
        return ag.at[g, o, pl.ds(pl.multiple_of(quarter * q, q), q)]

    def copy5(g):
        mine = block(g, quarter)
        return [
            remote(mine, mine, s5.at[g, i], r5.at[g, i], peer) for i, peer in enumerate((place.a_peer, place.b_peer))
        ]

    def copy6(g):
        from_a = half_block(g, 0, 2 * (1 - a) + b)
        from_b = half_block(g, 1, 2 * a + 1 - b)
        return [
            remote(from_a, from_a, s6.at[g, 0], r6.at[g, 0], place.b_peer),
            remote(from_b, from_b, s6.at[g, 1], r6.at[g, 1], place.a_peer),
        ]

    def targets(c, is_out):
        if is_out:
            cols = pl.ds(pl.multiple_of(c * 2 * LANES + core * LANES, LANES), LANES)
            return [gout_out.at[pl.ds(o * 4 * q, 4 * q), cols] for o in range(2)]
        base = (c - n_out) * 4 * LANES + core * 2 * LANES
        return [gin_out.at[:, pl.ds(pl.multiple_of(base + o * LANES, LANES), LANES)] for o in range(2)]

    def copy7(g, c, is_out):
        ends = targets(c, is_out)
        local = [pltpu.make_async_copy(ag.at[g, o], ends[o], l7.at[g, o]) for o in range(2)]
        far = [remote(ag.at[g, o], ends[o], s7.at[g, o], r7.at[g, o], place.core_peer) for o in range(2)]
        return local + far

    def at_stage(number, run):
        c = step - (number - 1)

        @pl.when((c >= 0) & (c < chunks))
        def _():
            run(c, c % 2, c % 4)

    def over_shards(body):
        def run(s, carry):
            body(s)
            return carry

        lax.fori_loop(0, shards, run, 0)

    def stage8(c, k, g):
        for is_out in (True, False):

            @pl.when((c < n_out) == is_out)
            def _():
                for copy in copy7(g, c, is_out):
                    copy.wait()

        for copy in copy5(g) + copy6(g):
            copy.wait_send()

    def stage7(c, k, g):
        for copy in copy6(g):
            copy.wait_recv()
        for is_out in (True, False):

            @pl.when((c < n_out) == is_out)
            def _():
                for copy in copy7(g, c, is_out):
                    copy.start()

    def stage6(c, k, g):
        for copy in copy5(g):
            copy.wait_recv()
        for copy in copy6(g):
            copy.start()

    def stage5(c, k, g):
        copies = copy4(k)
        for copy in copies:
            copy.wait()
        total = keep4[k]
        for d in range(1, shards):
            total = total + recv4[k, d - 1].astype(F32)
        for i, peer in enumerate(place.extra):
            keep4[k] = total
            copy = remote(keep4.at[k], xtra.at[k, i], sx.at[k, i], rx.at[k, i], peer)
            copy.start()
            copy.wait()
            total = total + xtra[k, i]
        for o in range(2):
            ag[g, o, pl.ds(pl.multiple_of(quarter * q, q), q)] = total[o].astype(BF)
        for copy in copy5(g):
            copy.start()

    def stage4(c, k, g):
        for copy in copy3(k):
            copy.wait()
        for o in range(2):
            keep4[k, o] = keep3[k, o, me] + recv3[k, o, me].astype(F32)
        for d in range(1, shards):
            s = (me + d) % shards
            for o in range(2):
                send4[k, d - 1, o] = (keep3[k, o, s] + recv3[k, o, s].astype(F32)).astype(BF)
        for copy in copy4(k):
            copy.start()

    def stage3(c, k, g):
        for copy in copy2(k):
            copy.wait()

        def part(s):
            for o, bit in enumerate((b, a)):
                own = pl.ds(pl.multiple_of(bit * q, q), q)
                other = pl.ds(pl.multiple_of((1 - bit) * q, q), q)
                keep3[k, o, s] = keep2[k, o, s, own] + recv2[k, o, s, own].astype(F32)
                send3[k, o, s] = (keep2[k, o, s, other] + recv2[k, o, s, other].astype(F32)).astype(BF)

        over_shards(part)
        for copy in copy3(k):
            copy.start()

    def stage2(c, k, g):
        for copy in copy1(k):
            copy.wait()

        def part(s):
            own = pl.ds(pl.multiple_of(a * 2 * q, 2 * q), 2 * q)
            other = pl.ds(pl.multiple_of((1 - a) * 2 * q, 2 * q), 2 * q)
            keep2[k, 0, s] = keep1[k, 0, s, own] + recv1[k, 0, s, own].astype(F32)
            send2[k, 0, s] = (keep1[k, 0, s, other] + recv1[k, 0, s, other].astype(F32)).astype(BF)
            for i in range(2):
                own = pl.ds(pl.multiple_of((2 * i + b) * q, q), q)
                other = pl.ds(pl.multiple_of((2 * i + 1 - b) * q, q), q)
                end = slice(i * q, (i + 1) * q)
                keep2[k, 1, s, end] = keep1[k, 1, s, own] + recv1[k, 1, s, own].astype(F32)
                send2[k, 1, s, end] = (keep1[k, 1, s, other] + recv1[k, 1, s, other].astype(F32)).astype(BF)

        over_shards(part)
        for copy in copy2(k):
            copy.start()

    def stage1(c, k, g):
        @pl.when(c < n_out)
        def _():
            base = c * 2 * LANES

            def part(s):
                lhs = low_t[pl.ds(pl.multiple_of(s * 8 * q, 8 * q), 8 * q), :]
                for side, ref in ((core, keep1), (1 - core, send1)):
                    cols = pl.ds(pl.multiple_of(base + side * LANES, LANES), LANES)
                    grad = mm(lhs, cot_ref[:, cols])
                    for o in range(2):
                        ref[k, o, s] = grad[o * 4 * q : (o + 1) * 4 * q].astype(ref.dtype)

            over_shards(part)

        @pl.when(c >= n_out)
        def _():
            def part(s):
                lhs = normed_t[pl.ds(pl.multiple_of(s * 4 * q, 4 * q), 4 * q), :]
                for side, ref in ((core, keep1), (1 - core, send1)):
                    cols = pl.ds(pl.multiple_of(side * 2 * LANES, 2 * LANES), 2 * LANES)
                    grad = mm(lhs, dp[c - n_out, :, cols])
                    for o in range(2):
                        ref[k, o, s] = grad[:, o * LANES : (o + 1) * LANES].astype(ref.dtype)

            over_shards(part)

        for copy in copy1(k):
            copy.start()

    for number, run in ((8, stage8), (7, stage7), (6, stage6), (5, stage5), (4, stage4), (3, stage3), (2, stage2), (1, stage1)):
        at_stage(number, run)

    masks = lambda: [mask_ref[k - 1] for k in range(1, CONV)]

    @pl.when(step < blocks)
    def _():
        def one(p, carry):
            pair = step * per + p
            cols = pl.ds(pl.multiple_of(p * LANES, LANES), LANES)
            at = pl.ds(pl.multiple_of(pair * LANES, LANES), LANES)
            res = backward_pair(
                pair, z_ref[:, cols], x_ref[:, cols], y_ref[:, cols], dgn_ref[:, cols], r_ref[...], rd_ref[...],
                cw_ref[:, cols], cb_ref[:, cols], skip_ref[:, cols], gain_ref[:, cols],
                masks(), dt2, cum3, cumt_ref, cbt_ref, g_scr, dcum, ddt,
            )
            dp[step, :, cols] = res[0]
            dp[blocks + step, :, cols] = res[1]
            for k in range(CONV):
                small_out[k : k + 1, at] = res[4][k]
            small_out[4:5, at] = res[5]
            small_out[5:6, at] = res[2]
            small_out[6:7, at] = res[3]
            return carry

        lax.fori_loop(0, per, one, 0)

    @pl.when(step == blocks - 1)
    def _():
        d_bc, d_raw, d_weight, d_bias, d_alog, d_dtb = backward_tail(
            bc_ref, dtraw_ref, b_ref, c_ref, dt_ref, masks(), seg_col, seg_row, cw_bc, cb_bc, alog_ref, bias_ref,
            g_scr, dcum, ddt,
        )
        for i in range(2):
            cols = slice(i * LANES, (i + 1) * LANES)
            dp[2 * blocks, :, cols] = d_bc[i].astype(BF)
            end = slice(INNER + i * LANES, INNER + (i + 1) * LANES)
            for k in range(CONV):
                small_out[k : k + 1, end] = d_weight[i][k]
            small_out[4:5, end] = d_bias[i]
        dp[2 * blocks, :, 2 * LANES : 3 * LANES] = d_raw.astype(BF)
        dp[2 * blocks, :, 3 * LANES :] = jnp.zeros((rows, LANES), BF)
        small_out[5:6, INNER : INNER + LANES] = d_alog
        small_out[5:6, INNER + LANES :] = d_dtb

    for i in range(small.stages):

        @pl.when(step == blocks + i)
        def _(i=i):
            small.stage(i)

    @pl.when((step >= n_out) & (step < chunks - 1))
    def _():
        dn[...] += mm_t(dp[step - n_out], w_ref[...])

    @pl.when(step == chunks - 1)
    def _():
        have = tail
        keep = iota((w_ref.shape[0], LANES), 1) < have % LANES
        full = have // LANES * LANES
        part = jnp.concatenate([w_ref[:, :full], jnp.where(keep, w_ref[:, full : full + LANES], 0)], axis=1)
        d_normed = dn[...] + mm_t(dp[step - n_out, :, : full + LANES], part)
        hid = hidden_ref[...].astype(F32)
        scale = lax.rsqrt(jnp.mean(hid * hid, axis=1, keepdims=True) + EPS)
        unit = hid * scale
        grad_norm = jnp.sum(d_normed * unit, axis=0, keepdims=True)
        for i in range(hid.shape[1] // LANES):
            norm_out[i : i + 1, :] = grad_norm[:, i * LANES : (i + 1) * LANES]
        du = d_normed * ngain_ref[...]
        gh_out[...] = cot_ref[...].astype(F32) + scale * (du - unit * jnp.mean(du * unit, axis=1, keepdims=True))

    for i in range(norm.stages):

        @pl.when(step == chunks - 1 + i)
        def _(i=i):
            norm.stage(i)


def mixer_backward_and_sums(
    proj, saved, dgn, rd, seg_col, seg_row, conv_w, conv_b, a_log, d_skip, dt_bias, gain,
    in_full, low, cotangent, normed, hidden, ngain, rep, shards,
):
    y, _, r, b, c, cbt, dt, cum, cumt, mask = saved
    rows, width = hidden.shape
    inner = low.shape[1]
    wide_block = 4 * LANES
    blocks = inner // wide_block
    n_out = width // (2 * LANES)
    n_in = -(-proj.shape[1] // wide_block)
    q = width // shards // 4
    chunks = n_out + n_in
    steps = chunks + 7
    n_small = SmallSum.count(rep, shards)
    n_extra = max(1, n_small - 3 - (shards - 1))
    mix = lambda offset: pl.BlockSpec((rows, wide_block), lambda i: (0, offset + jnp.minimum(i, blocks - 1)))
    lane = lambda n: pl.BlockSpec((n, wide_block), lambda i: (0, jnp.minimum(i, blocks - 1)))
    const = lambda shape, at=None: pl.BlockSpec(shape, lambda i: at or (0,) * len(shape), pipeline_mode=pl.Buffered(1))
    f = lambda *s: jax.ShapeDtypeStruct(s, F32)
    h = lambda *s: jax.ShapeDtypeStruct(s, BF)
    vm = pltpu.VMEM
    dma = lambda *s: pltpu.SemaphoreType.DMA(s)
    anywhere = pl.BlockSpec(memory_space=pl.ANY)
    pairs_bc = inner // LANES
    in_specs = [
        mix(0), mix(blocks), mix(0), mix(0), lane(CONV), lane(1), lane(1), lane(1),
        const((rows, 2 * LANES), (0, pairs_bc)), const((rows, LANES), (0, 2 * pairs_bc + 2)),
        const((rows, LANES)), const((rows, LANES)), const((rows, LANES)), const((rows, LANES)),
        const((rows, rows)), const((rows, LANES)), const((rows, LANES)), const((LANES, rows)),
        const((CONV - 1, rows, LANES)), const((rows, LANES)), const((1, rows)),
        const((CONV, 2 * LANES), (0, pairs_bc // 2)), const((1, 2 * LANES), (0, pairs_bc // 2)),
        const((1, LANES)), const((1, LANES)),
        pl.BlockSpec((width, wide_block), lambda i: (0, jnp.clip(i - n_out, 0, n_in - 1))),
        const((inner, rows)), const((rows, width)), const((width, rows)), const((rows, width)), const((1, width)),
    ]
    whole_out = lambda shape: pl.BlockSpec(shape, lambda i: (0,) * len(shape))
    small_shape, norm_shape = (8, conv_w.shape[1]), (16, LANES)
    kinds = [(2, 4 * q), (2, 2 * q), (2, q)]
    scratch = [
        vm((rows, 2 * LANES), BF), vm((rows, 3 * LANES), BF), vm((rows, rows), F32), vm((rows, LANES), F32),
        vm((rows, LANES), F32), vm((n_in, rows, wide_block), BF), vm((rows, width), F32),
    ]
    for o, height in kinds:
        shape = (2, o, shards, height, LANES)
        scratch += [vm(shape, F32), vm(shape, BF), vm(shape, BF)]
    scratch += [
        vm((2, 2, q, LANES), F32), vm((2, shards - 1, 2, q, LANES), BF), vm((2, shards - 1, 2, q, LANES), BF),
        vm((4, 2, 4 * q, LANES), BF), vm((n_small, *small_shape), F32), vm((n_small, *norm_shape), F32),
        dma(2), dma(2), dma(2, 2), dma(2, 2), dma(2, 2), dma(2, 2), dma(2, shards - 1), dma(2, shards - 1),
        dma(4, 2), dma(4, 2), dma(4, 2), dma(4, 2), dma(4, 2), dma(4, 2), dma(4, 2),
        vm((2, n_extra, 2, q, LANES), F32), dma(2, n_extra), dma(2, n_extra),
        dma(n_small), dma(n_small), dma(n_small), dma(n_small),
    ]
    return pl.pallas_call(
        functools.partial(
            reduce_kernel, rep=rep, shards=shards, q=q, blocks=blocks, n_out=n_out, n_in=n_in,
            tail=proj.shape[1] - (n_in - 1) * wide_block,
        ),
        grid=(steps,),
        in_specs=in_specs,
        out_specs=[anywhere, anywhere, whole_out((rows, width)), whole_out(small_shape), whole_out(norm_shape)],
        out_shape=[
            h(width // shards, n_in * wide_block), h(inner // shards, width), f(rows, width), f(*small_shape),
            f(*norm_shape),
        ],
        scratch_shapes=scratch,
        compiler_params=pltpu.CompilerParams(
            vmem_limit_bytes=VMEM_LIMIT, collective_id=2, has_side_effects=True
        ),
        name="mixer_backward_and_sums",
    )(
        proj, proj, y, dgn, conv_w, conv_b, d_skip, gain, proj, proj, r, rd, b, c, cbt, dt, cum, cumt, mask,
        seg_col, seg_row, conv_w, conv_b, a_log, dt_bias, in_full, low.T, cotangent, normed.T, hidden, ngain,
    )


def rows_scale(value):
    return lax.rsqrt(jnp.mean(value * value, axis=-1, keepdims=True) + EPS)


def per_device(
    hidden, seg_ids, cotangent, in_weight, out_weight, norm_gain, gated_gain, conv_weight, conv_bias, a_log, d_skip,
    dt_bias,
):
    rep, shards = lax.axis_size("rep"), lax.axis_size("shard")
    rows = hidden.shape[0]
    rep_at, shard_at = lax.axis_index("rep"), lax.axis_index("shard")

    def gather(weight):
        part = weight.shape[0] // rep
        mine = lax.dynamic_slice_in_dim(weight, rep_at * part, part, 0)
        return lax.all_gather(mine, ("shard", "rep"), axis=0, tiled=True)

    smalls = (norm_gain, gated_gain, conv_weight.reshape(-1), conv_bias, a_log, d_skip, dt_bias)
    sizes = [part.shape[0] for part in smalls]
    packed = lax.all_gather(jnp.concatenate(smalls), "shard", axis=0).astype(F32)
    starts = [sum(sizes[:i]) for i in range(len(sizes))]
    cuts = [packed[:, at : at + size] for at, size in zip(starts, sizes)]
    ngain, ggain, cb, alog, dskip, dtb = (cuts[i].reshape(1, -1) for i in (0, 1, 3, 4, 5, 6))
    cw = cuts[2].reshape(shards, CONV, -1).transpose(1, 0, 2).reshape(CONV, -1)
    pad = lambda v: jnp.pad(v, ((0, 0), (0, LANES - HEADS)))
    alog, dtb = pad(alog), pad(dtb)
    dskip = jnp.repeat(dskip, HEAD_DIM, axis=1)
    in_full, out_full = gather(in_weight), gather(out_weight)

    residual = hidden.astype(F32)
    scale = rows_scale(residual)
    unit = residual * scale
    normed = (unit * ngain).astype(BF)
    proj = mm(normed, in_full)
    seg_col = jnp.broadcast_to(seg_ids[0][:, None], (rows, LANES))
    shared = (seg_col, seg_ids, cw, cb, alog, dskip, dtb, ggain)
    saved = mixer_forward(proj, *shared)
    low, r = saved[1], saved[2]
    mixed = (residual + mm(low, out_full)).astype(BF)
    d_gated = mm_t(cotangent, out_full)
    rowdot = jnp.sum(d_gated * low.astype(F32), axis=1, keepdims=True)
    rd = r * r * (rowdot * (1.0 / INNER))
    g_in, g_out, grad_hidden, small, norm = mixer_backward_and_sums(
        proj, saved, d_gated, rd, *shared, in_full, low, cotangent, normed, hidden, ngain, rep, shards
    )
    g_in = g_in[:, : proj.shape[1]].astype(F32)
    g_out = g_out.astype(F32)

    def own(value, size):
        return lax.dynamic_slice_in_dim(value, shard_at * size, size, value.ndim - 1)

    heads = sizes[4]
    outs = (
        own(norm.reshape(-1), sizes[0]), own(small[5, :INNER], sizes[1]), own(small[:CONV], sizes[3]),
        own(small[4], sizes[3]), own(small[5, INNER : INNER + HEADS], heads),
        own(small[6, :INNER], sizes[1]).reshape(heads, HEAD_DIM).sum(1),
        own(small[5, INNER + LANES : INNER + LANES + HEADS], heads),
    )
    return (mixed, grad_hidden, g_in, g_out, *outs)


def solution(mesh):
    both = ("rep", "shard")
    shard = P("shard")
    placed = (P(both, None), P(both, None), P(both, None), P("shard", None), P("shard", None), shard, shard,
              P(None, "shard"), shard, shard, shard, shard)
    outs = (P(both, None), P(both, None), P("shard", None), P("shard", None), shard, shard, P(None, "shard"), shard,
            shard, shard, shard)
    return jax.shard_map(per_device, mesh=mesh, in_specs=placed, out_specs=outs, check_vma=False)
```

```python
import functools
import jax
import jax.numpy as jnp
from jax import lax
from jax.experimental import pallas as pl
from jax.experimental.pallas import tpu as pltpu
from jax.sharding import PartitionSpec as P

HEADS = 48
HEAD_DIM = 64
STATE = 128
CONV = 4
INNER = 3072
CONV_CH = 3328
LANES = 128
EPS = 1e-05
BF = jnp.bfloat16
F32 = jnp.float32
HIGH = lax.Precision.HIGHEST
VMEM_LIMIT = 63 * 2**20
MESH = pl.DeviceIdType.MESH


def mm(a, b):
    return jnp.dot(a, b, preferred_element_type=F32)


def mm_t(a, b):
    return lax.dot_general(a, b, (((1,), (1,)), ((), ())), preferred_element_type=F32)


def pieces(value, count):
    parts = []
    for _ in range(count):
        part = value.astype(BF)
        parts.append(part)
        value = value - part.astype(F32)
    return parts


def iota(shape, dim):
    return lax.broadcasted_iota(jnp.int32, shape, dim)


def head_of_lane(pair):
    heads, lanes = iota((LANES, LANES), 0), iota((LANES, LANES), 1)
    return (heads == 2 * pair + lanes // HEAD_DIM).astype(BF)


def one_head(head):
    return (iota((LANES, LANES), 0) == head).astype(BF)


def conv_shifts(value, masks):
    return [pltpu.roll(value, k, 0) * masks[k - 1] for k in range(1, CONV)]


def conv_apply(value, shifts, weight, bias):
    total = bias + weight[CONV - 1 : CONV] * value
    for k in range(1, CONV):
        total = total + weight[CONV - 1 - k : CONV - k] * shifts[k - 1]
    return total


def conv_back(d_pre, value, shifts, masks, weight):
    rows = d_pre.shape[0]
    d_value = weight[CONV - 1 : CONV] * d_pre
    d_weight = [jnp.sum(d_pre * value, axis=0, keepdims=True)]
    for k in range(1, CONV):
        d_weight.append(jnp.sum(d_pre * shifts[k - 1], axis=0, keepdims=True))
        d_value = d_value + weight[CONV - 1 - k : CONV - k] * pltpu.roll(
            d_pre * masks[k - 1], rows - k, 0
        )
    d_bias = jnp.sum(d_pre, axis=0, keepdims=True)
    return d_value, d_weight[::-1], d_bias


def silu_parts(value):
    sig = 1.0 / (1.0 + jnp.exp(-value))
    return sig, value * sig


def decay(col, row, clamp):
    gap = col - row
    return jnp.exp(jnp.minimum(gap, 0.0) if clamp else gap)


def wide(col, width):
    return jnp.concatenate([col] * (width // LANES), axis=1)


def backward_pair(
    pair, z, value, y, dgn, r, rd, cw, cb, skip, gain, masks, dt2, cum3, cumt_ref, cbt_ref, g_scr, dcum, ddt
):
    rows = z.shape[0]
    half = rows // 2
    shifts = conv_shifts(value, masks)
    pre = conv_apply(value, shifts, cw, cb)
    sp, x = silu_parts(pre)
    sg, sz = silu_parts(z)
    scanned = y + skip * x
    g = scanned * sz
    dgn_r = dgn * r
    d_gain = jnp.sum(dgn_r * g, axis=0, keepdims=True)
    dg = gain * dgn_r - g * rd
    dz = (dg * scanned * (sg * (1.0 + z * (1.0 - sg)))).astype(BF)
    dsc = dg * sz
    d_skip = jnp.sum(dsc * x, axis=0, keepdims=True)
    dy = dsc.astype(BF)
    spread = head_of_lane(pair)
    step = mm(dt2[...], jnp.concatenate([spread, spread], axis=0))
    xt = (x * step).astype(BF)
    first = iota((rows, LANES), 1) < HEAD_DIM
    zero = jnp.zeros_like(xt)
    dxts = []
    for side in range(2):
        head = 2 * pair + side
        pick = one_head(head)
        col = mm(cum3[...], jnp.concatenate([pick] * 3, axis=0))
        row = cumt_ref[pl.ds(head, 1), :]
        low_row, high_row = row[:, :half], row[:, half:]
        top, bottom = wide(col[:half], half), wide(col[half:], half)
        xs = jnp.where(first == (side == 0), xt, zero)
        parts = []
        for js, is_, jcol, irow, clamp in (
            (slice(0, half), slice(0, half), top, low_row, True),
            (slice(0, half), slice(half, rows), top, high_row, False),
            (slice(half, rows), slice(half, rows), bottom, high_row, True),
        ):
            e = decay(irow, jcol, clamp)
            parts.append(mm((e * cbt_ref[js, is_]).astype(BF), dy[is_]))
            g_scr[js, is_] += e * mm_t(xs[js], dy[is_])
        dxts.append(jnp.concatenate([parts[0] + parts[1], parts[2]], axis=0))
    dxt = jnp.where(first, dxts[0], dxts[1])
    for ref, term in ((dcum, dy.astype(F32) * y - xt.astype(F32) * dxt), (ddt, x * dxt)):
        hi, lo = pieces(term, 2)
        ref[...] += mm_t(hi, spread) + mm_t(lo, spread)
    dx = skip * dsc + step * dxt
    d_pre = dx * (sp * (1.0 + pre * (1.0 - sp)))
    d_value, d_weight, d_bias = conv_back(d_pre, value, shifts, masks, cw)
    return dz, d_value.astype(BF), d_gain, d_skip, d_weight, d_bias


def backward_tail(
    bc_ref, dtraw_ref, b_ref, c_ref, dt_ref, masks, seg_col, seg_row, cw_bc, cb_bc, alog_ref, bias_ref,
    g_scr, dcum, ddt
):
    rows = dt_ref.shape[0]
    same = wide(seg_col[...], rows) == seg_row[...]
    later = (iota((rows, rows), 0) <= iota((rows, rows), 1)) & same
    gt = jnp.where(later, g_scr[...], 0.0)
    db = jnp.dot(gt, c_ref[...], precision=HIGH, preferred_element_type=F32)
    dc = jnp.dot(gt.T, b_ref[...], precision=HIGH, preferred_element_type=F32)
    d_bc, d_weights, d_biases = [], [], []
    for i, d_out in enumerate((db, dc)):
        cols = slice(i * LANES, (i + 1) * LANES)
        value = bc_ref[:, cols]
        shifts = conv_shifts(value, masks)
        pre = conv_apply(value, shifts, cw_bc[:, cols], cb_bc[:, cols])
        sp, _ = silu_parts(pre)
        d_pre = d_out * (sp * (1.0 + pre * (1.0 - sp)))
        d_value, d_weight, d_bias = conv_back(d_pre, value, shifts, masks, cw_bc[:, cols])
        d_bc.append(d_value)
        d_weights.append(d_weight)
        d_biases.append(d_bias)
    step = dt_ref[...]
    live = iota((rows, LANES), 1) < HEADS
    rate = -jnp.exp(alog_ref)
    later_bf = later.astype(BF)
    dlog = sum(mm(later_bf, part) for part in pieces(dcum[...], 3)[::-1])
    dstep = ddt[...] + dlog * rate
    raw = jnp.where(live, dtraw_ref[...] + bias_ref, 0.0)
    d_raw = jnp.where(live, dstep / (1.0 + jnp.exp(-raw)), 0.0)
    d_alog = jnp.sum(dlog * step, axis=0, keepdims=True) * rate
    return d_bc, d_raw, d_weights, d_biases, d_alog, jnp.sum(d_raw, axis=0, keepdims=True)


class Place:
    def __init__(self, rep, shards):
        self.rep, self.shards = rep, shards
        r, self.me = lax.axis_index("rep"), lax.axis_index("shard")
        self.r = r
        self.core, self.a, self.b = r % 2, (r // 2) % 2, (r // 4) % 2
        self.core_peer = (r + 1 - 2 * self.core, self.me)
        self.a_peer = (r + 2 - 4 * self.a, self.me)
        self.b_peer = (r + 4 - 8 * self.b, self.me)
        self.extra = []
        stride = 8
        while stride < rep:
            bit = (r // stride) % 2
            self.extra.append((r + stride - 2 * stride * bit, self.me))
            stride *= 2
        self.quarter = 2 * self.a + self.b

    def shard_peer(self, distance):
        return (self.r, (self.me + distance) % self.shards)

    def partners(self):
        return [self.core_peer, self.a_peer, self.b_peer, *self.extra] + [
            self.shard_peer(d) for d in range(1, self.shards)
        ]

    def greet(self):
        barrier = pltpu.get_barrier_semaphore()
        partners = self.partners()
        for partner in partners:
            pl.semaphore_signal(barrier, inc=1, device_id=partner, device_id_type=MESH)
        pl.semaphore_wait(barrier, len(partners))


def remote(src, dst, send, recv, device):
    return pltpu.make_async_remote_copy(
        src_ref=src, dst_ref=dst, send_sem=send, recv_sem=recv, device_id=device, device_id_type=MESH
    )


class SmallSum:
    def __init__(self, place, buf, slots, sends, recvs):
        self.buf, self.slots, self.sends, self.recvs = buf, slots, sends, recvs
        pairs = [place.core_peer, place.a_peer, place.b_peer, *place.extra]
        self.groups = [[peer] for peer in pairs] + [[place.shard_peer(d) for d in range(1, place.shards)]]
        self.stages = len(self.groups) + 1

    @staticmethod
    def count(rep, shards):
        return rep.bit_length() - 1 + shards - 1

    def copies(self, group):
        at = sum(len(g) for g in self.groups[:group])
        return [
            remote(self.buf, self.slots.at[at + i], self.sends.at[at + i], self.recvs.at[at + i], peer)
            for i, peer in enumerate(self.groups[group])
        ]

    def stage(self, number):
        if number > 0:
            at = sum(len(g) for g in self.groups[: number - 1])
            copies = self.copies(number - 1)
            for copy in copies:
                copy.wait()
            total = self.buf[...]
            for i in range(len(copies)):
                total = total + self.slots[at + i]
            self.buf[...] = total
        if number < len(self.groups):
            for copy in self.copies(number):
                copy.start()


def forward_setup(
    bc, raw, seg_col, seg_row, cw, cb, alog, bias, outs, cb_scr, dt2, cum3
):
    b_out, c_out, cbt_out, dt_out, cum_out, cumt_out, mask_out = outs
    rows = raw.shape[0]
    at = iota((rows, LANES), 0)
    for k in range(1, CONV):
        same = (pltpu.roll(seg_col, k, 0) == seg_col) & (at >= k)
        mask_out[k - 1] = same.astype(F32)
    masks = [mask_out[k - 1] for k in range(1, CONV)]
    results = []
    for i in range(2):
        cols = slice(i * LANES, (i + 1) * LANES)
        value = bc[:, cols]
        pre = conv_apply(value, conv_shifts(value, masks), cw[:, cols], cb[:, cols])
        results.append(silu_parts(pre)[1])
    b_out[...] = results[0]
    c_out[...] = results[1]
    products = lax.dot_general(
        results[1], results[0], (((1,), (1,)), ((), ())), precision=HIGH, preferred_element_type=F32
    )
    lower = iota((rows, rows), 0) >= iota((rows, rows), 1)
    allowed = lower & (wide(seg_col, rows) == seg_row)
    products = jnp.where(allowed, products, 0.0)
    cb_scr[...] = products
    cbt_out[...] = products.T
    live = iota((rows, LANES), 1) < HEADS
    raw = jnp.where(live, raw + bias, 0.0)
    step = jnp.where(live, jnp.maximum(raw, 0.0) + jnp.log(1.0 + jnp.exp(-jnp.abs(raw))), 0.0)
    dt_out[...] = step
    hi, lo = pieces(step, 2)
    dt2[:, :LANES] = hi
    dt2[:, LANES:] = lo
    log_rate = step * -jnp.exp(alog)
    tri = lower.astype(BF)
    cum = sum(mm(tri, part) for part in pieces(log_rate, 3)[::-1])
    cum_out[...] = cum
    cumt_out[...] = cum.T
    for i, part in enumerate(pieces(cum, 3)):
        cum3[:, i * LANES : (i + 1) * LANES] = part


def skip_lanes(skip_row, spread):
    return mm(jnp.broadcast_to(skip_row, (8, LANES)).astype(BF), spread)[0:1]


def forward_pair(pair, z, value, cw, cb, skip_row, masks, dt2, cum3, cumt_ref, cb_scr):
    rows = z.shape[0]
    half = rows // 2
    pre = conv_apply(value, conv_shifts(value, masks), cw, cb)
    x = silu_parts(pre)[1]
    spread = head_of_lane(pair)
    step = mm(dt2[...], jnp.concatenate([spread, spread], axis=0))
    xt = (x * step).astype(BF)
    first = iota((rows, LANES), 1) < HEAD_DIM
    ys = []
    for side in range(2):
        head = 2 * pair + side
        pick = one_head(head)
        col = mm(cum3[...], jnp.concatenate([pick] * 3, axis=0))
        row = cumt_ref[pl.ds(head, 1), :]
        low_row, high_row = row[:, :half], row[:, half:]
        top, bottom = wide(col[:half], half), wide(col[half:], half)
        m00 = (decay(top, low_row, True) * cb_scr[:half, :half]).astype(BF)
        m10 = (decay(bottom, low_row, False) * cb_scr[half:, :half]).astype(BF)
        m11 = (decay(bottom, high_row, True) * cb_scr[half:, half:]).astype(BF)
        ys.append(
            jnp.concatenate([mm(m00, xt[:half]), mm(m10, xt[:half]) + mm(m11, xt[half:])], axis=0)
        )
    y = jnp.where(first, ys[0], ys[1])
    g = (y + skip_lanes(skip_row, spread) * x) * silu_parts(z)[1]
    return y, g


ROW_BIAS, ROW_GAIN, ROW_NORM, ROW_ALOG, ROW_SKIP, ROW_DTB = 4, 5, 6, 7, 8, 9


def forward_kernel(
    hidden_ref, cot_ref, seg_row, wt_ref, ow_ref, pack_ref,
    w3, ow3, proj_out, y_out, lowt_out, r_out, b_out, c_out, cbt_out, dt_out, cum_out, cumt_out, mask_out,
    normt_out, small_out, mixed_out, rd_out, segc_out,
    normed3, pk, wbuf, owbuf, xbuf, cb_scr, dt2, cum3, gated, ssq, low, acc,
    sz, rz, s2, r2, s3, r3, s4, r4, lw, st, rt, sp, rp, lc,
    *, rep, shards, blocks, n_out
):
    step = pl.program_id(0)
    place = Place(rep, shards)
    a, b, core, me, quarter = place.a, place.b, place.core, place.me, place.quarter
    rows, width = hidden_ref.shape
    depth = width // shards
    inner = blocks * 4 * LANES
    per = 4
    n_mix = 1 + 2 * blocks
    chunks = n_mix + n_out
    tail_at = 2 * inner + 2 * LANES
    tail = w3.shape[1] - tail_at
    total_rows = w3.shape[1]

    def rows_of(kind, c):
        if kind == "bc":
            return 2 * inner, 2 * LANES
        if kind == "in":
            j = (c - 1) // 2
            return ((c % 2) * inner + j * 4 * LANES), 4 * LANES
        return (c - n_mix) * LANES, LANES

    def view(kind, c, s, start, count, half=None):
        ref = ow3 if kind == "out" else w3
        base, _ = rows_of(kind, c)
        if half is not None and kind != "out":
            start, count = start + half * (count // 2), count // 2
        at = pl.ds(pl.multiple_of(base + start, 16), count)
        if half is not None and kind == "out":
            return ref.at[s, at, half * (width // 2) : (half + 1) * (width // 2)]
        return ref.at[s, at]

    def piece(kind, c, s, quarter, half=None):
        n = rows_of(kind, c)[1]
        return view(kind, c, s, core * (n // 2) + quarter * (n // 8), n // 8, half)

    def others():
        return [(d - 1, (me + d) % shards) for d in range(1, shards)]

    def copy1(kind, c):
        n = rows_of(kind, c)[1]
        base = rows_of(kind, c)[0]
        src = (ow_ref if kind == "out" else wt_ref).at[
            pl.ds(pl.multiple_of(base + core * (n // 2) + quarter * (n // 8), 16), n // 8)
        ]
        k = c % 8
        return [
            remote(src, piece(kind, c, me, quarter), sz.at[k, d - 1], rz.at[k, d - 1], place.shard_peer(d))
            for d in range(1, shards)
        ]

    def copy2(kind, c):
        k = c % 4
        return [
            remote(piece(kind, c, s, quarter), piece(kind, c, s, quarter), s2.at[k, i, d], r2.at[k, i, d], peer)
            for d, s in others()
            for i, peer in enumerate((place.a_peer, place.b_peer))
        ]

    def copy3(kind, c):
        k = c % 4
        from_a, from_b = 2 * (1 - a) + b, 2 * a + 1 - b
        return [
            remote(
                piece(kind, c, s, origin, i), piece(kind, c, s, origin, i), s3.at[k, i, d], r3.at[k, i, d], peer
            )
            for d, s in others()
            for i, (origin, peer) in enumerate(((from_a, place.b_peer), (from_b, place.a_peer)))
        ]

    def copy4(kind, c):
        k = c % 4
        n = rows_of(kind, c)[1]
        return [
            remote(
                view(kind, c, s, core * (n // 2), n // 2), view(kind, c, s, core * (n // 2), n // 2),
                s4.at[k, d], r4.at[k, d], place.core_peer,
            )
            for d, s in others()
        ]

    def load(kind, c, back=False):
        k = c % 2
        base, n = rows_of(kind, c)
        if kind == "bc":
            n = total_rows - base
        full, own, buf = (ow3, ow_ref, owbuf) if kind == "out" else (w3, wt_ref, wbuf)
        at = pl.ds(pl.multiple_of(base, LANES), n)
        mine = buf.at[k, me, pl.ds(0, n)]
        if back:
            return [pltpu.make_async_copy(mine, full.at[me, at], lc.at[k])]
        copies = [pltpu.make_async_copy(own.at[at], mine, lw.at[k, 0])]
        for d, s in others():
            copies.append(pltpu.make_async_copy(full.at[s, at], buf.at[k, s, pl.ds(0, n)], lw.at[k, 1 + d]))
        return copies

    def at_chunk(c, run):
        @pl.when(c == 0)
        def _():
            run("bc", 0)

        @pl.when((c >= 1) & (c < n_mix))
        def _():
            run("in", c)

        @pl.when((c >= n_mix) & (c < chunks))
        def _():
            run("out", c)

    def tails():
        return [
            remote(
                wt_ref.at[tail_at:total_rows], w3.at[me, tail_at:total_rows], st.at[d - 1], rt.at[d - 1],
                place.shard_peer(d),
            )
            for d in range(1, shards)
        ]

    def packs():
        return [
            remote(pack_ref, pk.at[me], sp.at[d - 1], rp.at[d - 1], place.shard_peer(d)) for d in range(1, shards)
        ]

    def start(copies):
        for copy in copies:
            copy.start()

    def finish(copies):
        for copy in copies:
            copy.wait()

    def stage5(kind, c):
        finish(copy4(kind, c))
        start(load(kind, c))

    def stage4(kind, c):
        finish(copy3(kind, c))
        start(copy4(kind, c))

    def stage3(kind, c):
        finish(copy2(kind, c))
        start(copy3(kind, c))

    def stage2(kind, c):
        finish(copy1(kind, c))
        start(copy2(kind, c))

    def stage1(kind, c):
        start(copy1(kind, c))

    @pl.when(step == 0)
    def _():
        place.greet()
        start(packs())
        stage1("bc", 0)
        start(tails())
        pk[me] = pack_ref[...]
        wbuf[0, :, total_rows - 2 * inner :] = jnp.zeros(
            (shards, 4 * LANES - (total_rows - 2 * inner), depth), BF
        )
        ssq[...] = jnp.zeros_like(ssq)
        acc[...] = jnp.zeros_like(acc)
        small_out[...] = jnp.zeros_like(small_out)

    @pl.when(step == 3)
    def _():
        finish(tails())

    at_chunk(step - 6, lambda kind, c: finish(load(kind, c, True)))
    for number, run in ((1, stage1), (2, stage2), (3, stage3), (4, stage4), (5, stage5)):
        at_chunk(step - (number - 1) if number > 1 else step + 1, run)

    @pl.when(step == 1)
    def _():
        finish(packs())
        conv_n, gain_n, heads_n = CONV_CH // shards, inner // shards, HEADS // shards
        for s in range(shards):
            part = pk[s].astype(F32)
            small_out[0 : CONV + 1, s * conv_n : (s + 1) * conv_n] = part[0 : CONV + 1, :conv_n]
            small_out[ROW_GAIN : ROW_GAIN + 1, s * gain_n : (s + 1) * gain_n] = part[5:6, :gain_n]
            small_out[ROW_NORM : ROW_NORM + 1, s * depth : (s + 1) * depth] = part[6:7, :depth]
            for i in range(3):
                small_out[ROW_ALOG + i : ROW_ALOG + i + 1, s * heads_n : (s + 1) * heads_n] = part[
                    7 + i : 8 + i, :heads_n
                ]
        hid = hidden_ref[...].astype(F32)
        scale = lax.rsqrt(jnp.mean(hid * hid, axis=1, keepdims=True) + EPS)
        normed = hid * scale * small_out[ROW_NORM : ROW_NORM + 1, :width]
        for s in range(shards):
            normed3[s] = normed[:, s * depth : (s + 1) * depth].astype(BF)
        normt_out[...] = normed.T.astype(BF)
        seg = jnp.broadcast_to(seg_row[...], (LANES, rows)).astype(F32)
        segc_out[...] = seg.T.astype(jnp.int32)

    def arrive(kind, c):
        finish(load(kind, c))
        start(load(kind, c, True))

    c = step - 5
    masks = lambda: [mask_out[k - 1] for k in range(1, CONV)]

    def project(k):
        return sum(mm_t(normed3[s], wbuf[k, s]) for s in range(shards))

    @pl.when(c == 0)
    def _():
        arrive("bc", 0)
        proj_out[...] = project(0)
        outs = (b_out, c_out, cbt_out, dt_out, cum_out, cumt_out, mask_out)
        end = slice(inner, inner + 2 * LANES)
        forward_setup(
            proj_out[:, : 2 * LANES], proj_out[:, 2 * LANES : 3 * LANES], segc_out[...], seg_row[...],
            small_out[:CONV, end], small_out[ROW_BIAS : ROW_BIAS + 1, end],
            small_out[ROW_ALOG : ROW_ALOG + 1, :LANES], small_out[ROW_DTB : ROW_DTB + 1, :LANES],
            outs, cb_scr, dt2, cum3,
        )

    is_in = (c >= 1) & (c < n_mix)

    @pl.when(is_in & (c % 2 == 1))
    def _():
        arrive("in", c)
        value = project(c % 2)
        proj_out[...] = value
        xbuf[...] = value

    @pl.when(is_in & (c % 2 == 0))
    def _():
        arrive("in", c)
        proj_out[...] = project(c % 2)
        j = (c - 1) // 2

        def one(p, carry):
            pair = j * per + p
            cols = pl.ds(pl.multiple_of(p * LANES, LANES), LANES)
            at = pl.ds(pl.multiple_of(pair * LANES, LANES), LANES)
            y, g = forward_pair(
                pair, proj_out[:, cols], xbuf[:, cols], small_out[:CONV, at], small_out[ROW_BIAS : ROW_BIAS + 1, at],
                small_out[ROW_SKIP : ROW_SKIP + 1, :LANES], masks(), dt2, cum3, cumt_out, cb_scr,
            )
            y_out[:, cols] = y
            gated[pair] = g
            ssq[...] += g * g
            return carry

        lax.fori_loop(0, per, one, 0)

    @pl.when(c == n_mix - 1)
    def _():
        mean = jnp.sum(ssq[...], axis=1, keepdims=True) * (1.0 / inner)
        r = jnp.broadcast_to(lax.rsqrt(mean + EPS), (rows, LANES))
        r_out[...] = r

        def write(i, carry):
            cols = pl.ds(pl.multiple_of(i * LANES, LANES), LANES)
            value = gated[i] * r * small_out[ROW_GAIN : ROW_GAIN + 1, cols]
            low[:, cols] = value.astype(BF)
            lowt_out[cols, :] = value.T.astype(BF)
            return carry

        lax.fori_loop(0, inner // LANES, write, 0)

    @pl.when((c >= n_mix) & (c < chunks))
    def _():
        arrive("out", c)
        for s in range(shards):
            cols = pl.ds(pl.multiple_of(s * (inner // shards) + (c - n_mix) * LANES, LANES), LANES)
            acc[...] += mm(low[:, cols], owbuf[c % 2, s])

    @pl.when(c == chunks - 1)
    def _():
        added = acc[...]
        mixed_out[...] = (hidden_ref[...].astype(F32) + added).astype(BF)
        dots = jnp.sum(cot_ref[...].astype(F32) * added, axis=1, keepdims=True)
        r = r_out[...]
        rd_out[...] = r * r * (dots * (1.0 / inner))


def mixer_forward(hidden, cotangent, seg_ids, wt, ow, pack, rep, shards):
    rows, width = hidden.shape
    depth = width // shards
    inner = ow.shape[0] * shards
    blocks = inner // (4 * LANES)
    n_out = ow.shape[0] // LANES
    n_mix = 1 + 2 * blocks
    n_in = -(-wt.shape[0] // (4 * LANES))
    steps = n_mix + n_out + 6
    f = lambda *s: jax.ShapeDtypeStruct(s, F32)
    h = lambda *s: jax.ShapeDtypeStruct(s, BF)
    vm = pltpu.VMEM
    dma = lambda *s: pltpu.SemaphoreType.DMA(s)
    anywhere = pl.BlockSpec(memory_space=pl.ANY)
    const = lambda shape: pl.BlockSpec(shape, lambda i: (0,) * len(shape), pipeline_mode=pl.Buffered(1))
    fixed = lambda shape: pl.BlockSpec(shape, lambda i: (0,) * len(shape))

    def proj_at(i):
        c = jnp.clip(i - 5, 0, n_mix - 1)
        return (0, jnp.where(c == 0, 2 * blocks, (c % 2) * blocks + (c - 1) // 2))

    def y_at(i):
        return (0, jnp.clip((i - 6) // 2, 0, blocks - 1))

    out_shape = [
        h(shards, wt.shape[0], depth), h(shards, *ow.shape), f(rows, n_in * 4 * LANES), f(rows, inner),
        h(inner, rows), f(rows, LANES), f(rows, LANES), f(rows, LANES), f(rows, rows), f(rows, LANES),
        f(rows, LANES), f(LANES, rows), f(CONV - 1, rows, LANES), h(width, rows), f(16, CONV_CH), h(rows, width),
        f(rows, LANES), jax.ShapeDtypeStruct((rows, LANES), jnp.int32),
    ]
    block = (rows, 4 * LANES)
    out_specs = [anywhere, anywhere, pl.BlockSpec(block, proj_at), pl.BlockSpec(block, y_at)] + [
        fixed(s.shape) for s in out_shape[4:]
    ]
    n = shards - 1
    return pl.pallas_call(
        functools.partial(forward_kernel, rep=rep, shards=shards, blocks=blocks, n_out=n_out),
        grid=(steps,),
        in_specs=[
            const((rows, width)), const((rows, width)), const((1, rows)), anywhere, anywhere, const(pack.shape),
        ],
        out_specs=out_specs,
        out_shape=out_shape,
        scratch_shapes=[
            vm((shards, rows, depth), BF), vm((shards, *pack.shape), BF), vm((2, shards, 4 * LANES, depth), BF),
            vm((2, shards, LANES, width), BF), vm(block, F32), vm((rows, rows), F32), vm((rows, 2 * LANES), BF),
            vm((rows, 3 * LANES), BF), vm((inner // LANES, rows, LANES), F32), vm((rows, LANES), F32),
            vm((rows, inner), BF), vm((rows, width), F32),
            dma(8, n), dma(8, n), dma(4, 2, n), dma(4, 2, n), dma(4, 2, n), dma(4, 2, n), dma(4, n), dma(4, n),
            dma(2, shards), dma(n), dma(n), dma(n), dma(n), dma(2),
        ],
        compiler_params=pltpu.CompilerParams(
            vmem_limit_bytes=VMEM_LIMIT, collective_id=1, has_side_effects=True
        ),
        name="mixer_forward",
    )(hidden, cotangent, seg_ids, wt, ow, pack)


def chunk_at(j, blocks):
    third = blocks // 2
    group = j // third
    return j + third * jnp.where(group == 1, 1, 0) - third * jnp.where(group == 2, 1, 0)


def reduce_kernel(
    z_ref, x_ref, y_ref, ow_ref, bc_ref, dtraw_ref, r_ref, rd_ref, b_ref, c_ref, cbt_ref, dt_ref, cum_ref, cumt_ref,
    mask_ref, seg_col, seg_row, par_ref, w_ref, low_t, cot_ref, normed_t, hidden_ref,
    gin_out, gout_out, gh_out, small_out, norm_out,
    dt2, cum3, g_scr, dcum, ddt, dp, dn, dgn,
    keep1, send1, recv1, keep2, send2, recv2, keep3, send3, recv3, keep4, send4, recv4, ag, agt,
    slots_small, slots_norm,
    s1, r1, s2, r2, s3, r3, s4, r4, s5, r5, s6, r6, l7, s7, r7, xtra, sx, rx, ss, rs, sn, rn,
    *, rep, shards, q, blocks, n_out, n_in, tail
):
    step = pl.program_id(0)
    place = Place(rep, shards)
    rows = z_ref.shape[0]
    per = 2
    mix_steps = blocks * 2
    chunks = n_out + n_in
    a, b, core, me, quarter = place.a, place.b, place.core, place.me, place.quarter

    small = SmallSum(place, small_out, slots_small, ss, rs)
    norm = SmallSum(place, norm_out, slots_norm, sn, rn)

    @pl.when(step == 0)
    def _():
        place.greet()
        small_out[...] = jnp.zeros_like(small_out)
        norm_out[...] = jnp.zeros_like(norm_out)
        dn[...] = jnp.zeros_like(dn)
        hi, lo = pieces(dt_ref[...], 2)
        dt2[:, :LANES] = hi
        dt2[:, LANES:] = lo
        for i, part in enumerate(pieces(cum_ref[...], 3)):
            cum3[:, i * LANES : (i + 1) * LANES] = part
        g_scr[...] = jnp.zeros_like(g_scr)
        dcum[...] = jnp.zeros_like(dcum)
        ddt[...] = jnp.zeros_like(ddt)

    def copy1(k, w):
        return [remote(send1.at[k], recv1.at[w], s1.at[k], r1.at[w], place.core_peer)]

    def copy2(k, w):
        return [
            remote(send2.at[k, o], recv2.at[w, o], s2.at[k, o], r2.at[w, o], peer)
            for o, peer in enumerate((place.a_peer, place.b_peer))
        ]

    def copy3(k, w):
        return [
            remote(send3.at[k, o], recv3.at[w, o], s3.at[k, o], r3.at[w, o], peer)
            for o, peer in enumerate((place.b_peer, place.a_peer))
        ]

    def copy4(k, w):
        return [
            remote(send4.at[k, d - 1], recv4.at[w, d - 1], s4.at[k, d - 1], r4.at[w, d - 1], place.shard_peer(d))
            for d in range(1, shards)
        ]

    def block(g, quarter):
        return ag.at[g, :, pl.ds(pl.multiple_of(quarter * q, q), q)]

    def half_block(g, o, quarter):
        return ag.at[g, o, pl.ds(pl.multiple_of(quarter * q, q), q)]

    def copy5(g):
        mine = block(g, quarter)
        return [
            remote(mine, mine, s5.at[g, i], r5.at[g, i], peer) for i, peer in enumerate((place.a_peer, place.b_peer))
        ]

    def copy6(g):
        from_a = half_block(g, 0, 2 * (1 - a) + b)
        from_b = half_block(g, 1, 2 * a + 1 - b)
        return [
            remote(from_a, from_a, s6.at[g, 0], r6.at[g, 0], place.b_peer),
            remote(from_b, from_b, s6.at[g, 1], r6.at[g, 1], place.a_peer),
        ]

    def targets(c, is_out):
        if is_out:
            cols = pl.ds(pl.multiple_of(c * 2 * LANES + core * LANES, LANES), LANES)
            return [gout_out.at[pl.ds(o * 4 * q, 4 * q), cols] for o in range(2)]
        base = chunk_at(c - n_out, blocks) * 4 * LANES + core * 2 * LANES
        return [gin_out.at[pl.ds(pl.multiple_of(base + o * LANES, LANES), LANES)] for o in range(2)]

    def copy7(g, c, is_out):
        ends = targets(c, is_out)
        ref = ag if is_out else agt
        local = [pltpu.make_async_copy(ref.at[g, o], ends[o], l7.at[g, o]) for o in range(2)]
        far = [remote(ref.at[g, o], ends[o], s7.at[g, o], r7.at[g, o], place.core_peer) for o in range(2)]
        return local + far

    def at_stage(number, run):
        c = step - (number - 1)

        @pl.when((c >= 0) & (c < chunks))
        def _():
            run(c, c % 2, c % 4, c % 8)

    def over_shards(body):
        def run(s, carry):
            body(s)
            return carry

        lax.fori_loop(0, shards, run, 0)

    def stage8(c, k, w, g):
        for is_out in (True, False):

            @pl.when((c < n_out) == is_out)
            def _():
                for copy in copy7(g, c, is_out):
                    copy.wait()

        for copy in copy5(g) + copy6(g):
            copy.wait_send()

    def stage7(c, k, w, g):
        for copy in copy6(g):
            copy.wait_recv()
        for is_out in (True, False):

            @pl.when((c < n_out) == is_out)
            def _(is_out=is_out):
                if not is_out:
                    for o in range(2):
                        agt[g, o] = ag[g, o].astype(F32).T.astype(BF)
                for copy in copy7(g, c, is_out):
                    copy.start()

    def stage6(c, k, w, g):
        for copy in copy5(g):
            copy.wait_recv()
        for copy in copy6(g):
            copy.start()

    def stage5(c, k, w, g):
        copies = copy4(k, w)
        for copy in copies:
            copy.wait()
        total = keep4[k]
        for d in range(1, shards):
            total = total + recv4[w, d - 1].astype(F32)
        for i, peer in enumerate(place.extra):
            keep4[k] = total
            copy = remote(keep4.at[k], xtra.at[k, i], sx.at[k, i], rx.at[k, i], peer)
            copy.start()
            copy.wait()
            total = total + xtra[k, i]
        for o in range(2):
            ag[g, o, pl.ds(pl.multiple_of(quarter * q, q), q)] = total[o].astype(BF)
        for copy in copy5(g):
            copy.start()

    def stage4(c, k, w, g):
        for copy in copy3(k, w):
            copy.wait()
        for o in range(2):
            keep4[k, o] = keep3[k, o, me] + recv3[w, o, me].astype(F32)
        for d in range(1, shards):
            s = (me + d) % shards
            for o in range(2):
                send4[k, d - 1, o] = (keep3[k, o, s] + recv3[w, o, s].astype(F32)).astype(BF)
        for copy in copy4(k, w):
            copy.start()

    def stage3(c, k, w, g):
        for copy in copy2(k, w):
            copy.wait()

        def part(s):
            for o, bit in enumerate((b, a)):
                own = pl.ds(pl.multiple_of(bit * q, q), q)
                other = pl.ds(pl.multiple_of((1 - bit) * q, q), q)
                keep3[k, o, s] = keep2[k, o, s, own] + recv2[w, o, s, own].astype(F32)
                send3[k, o, s] = (keep2[k, o, s, other] + recv2[w, o, s, other].astype(F32)).astype(BF)

        over_shards(part)
        for copy in copy3(k, w):
            copy.start()

    def stage2(c, k, w, g):
        for copy in copy1(k, w):
            copy.wait()

        def part(s):
            own = pl.ds(pl.multiple_of(a * 2 * q, 2 * q), 2 * q)
            other = pl.ds(pl.multiple_of((1 - a) * 2 * q, 2 * q), 2 * q)
            keep2[k, 0, s] = keep1[k, 0, s, own] + recv1[w, 0, s, own].astype(F32)
            send2[k, 0, s] = (keep1[k, 0, s, other] + recv1[w, 0, s, other].astype(F32)).astype(BF)
            for i in range(2):
                own = pl.ds(pl.multiple_of((2 * i + b) * q, q), q)
                other = pl.ds(pl.multiple_of((2 * i + 1 - b) * q, q), q)
                end = slice(i * q, (i + 1) * q)
                keep2[k, 1, s, end] = keep1[k, 1, s, own] + recv1[w, 1, s, own].astype(F32)
                send2[k, 1, s, end] = (keep1[k, 1, s, other] + recv1[w, 1, s, other].astype(F32)).astype(BF)

        over_shards(part)
        for copy in copy2(k, w):
            copy.start()

    def stage1(c, k, w, g):
        @pl.when(c < n_out)
        def _():
            base = c * 2 * LANES

            def part(s):
                lhs = low_t[pl.ds(pl.multiple_of(s * 8 * q, 8 * q), 8 * q), :]
                for side, ref in ((core, keep1), (1 - core, send1)):
                    cols = pl.ds(pl.multiple_of(base + side * LANES, LANES), LANES)
                    grad = mm(lhs, cot_ref[:, cols])
                    for o in range(2):
                        ref[k, o, s] = grad[o * 4 * q : (o + 1) * 4 * q].astype(ref.dtype)

            over_shards(part)

        @pl.when(c >= n_out)
        def _():
            def part(s):
                lhs = normed_t[pl.ds(pl.multiple_of(s * 4 * q, 4 * q), 4 * q), :]
                for side, ref in ((core, keep1), (1 - core, send1)):
                    cols = pl.ds(pl.multiple_of(side * 2 * LANES, 2 * LANES), 2 * LANES)
                    grad = mm(lhs, dp[chunk_at(c - n_out, blocks), :, cols])
                    for o in range(2):
                        ref[k, o, s] = grad[:, o * LANES : (o + 1) * LANES].astype(ref.dtype)

            over_shards(part)

        for copy in copy1(k, w):
            copy.start()

    for number, run in ((1, stage1), (2, stage2), (3, stage3), (4, stage4), (5, stage5), (6, stage6), (7, stage7), (8, stage8)):
        at_stage(number, run)

    masks = lambda: [mask_ref[k - 1] for k in range(1, CONV)]

    @pl.when(step < mix_steps)
    def _():
        dgn[...] = mm_t(cot_ref[...], ow_ref[...])

        def one(p, carry):
            pair = step * per + p
            cols = pl.ds(pl.multiple_of(p * LANES, LANES), LANES)
            at = pl.ds(pl.multiple_of(pair * LANES, LANES), LANES)
            skip = skip_lanes(par_ref[ROW_SKIP : ROW_SKIP + 1, :LANES], head_of_lane(pair))
            res = backward_pair(
                pair, z_ref[:, cols], x_ref[:, cols], y_ref[:, cols], dgn[:, cols], r_ref[...], rd_ref[...],
                par_ref[:CONV, at], par_ref[ROW_BIAS : ROW_BIAS + 1, at], skip, par_ref[ROW_GAIN : ROW_GAIN + 1, at],
                masks(), dt2, cum3, cumt_ref, cbt_ref, g_scr, dcum, ddt,
            )
            end = pl.ds(pl.multiple_of(step % 2 * per * LANES + p * LANES, LANES), LANES)
            dp[step // 2, :, end] = res[0]
            dp[blocks + step // 2, :, end] = res[1]
            for k in range(CONV):
                small_out[k : k + 1, at] = res[4][k]
            small_out[4:5, at] = res[5]
            small_out[5:6, at] = res[2]
            small_out[6:7, at] = res[3]
            return carry

        lax.fori_loop(0, per, one, 0)

    @pl.when(step == mix_steps - 1)
    def _():
        end = slice(INNER, INNER + 2 * LANES)
        d_bc, d_raw, d_weight, d_bias, d_alog, d_dtb = backward_tail(
            bc_ref, dtraw_ref, b_ref, c_ref, dt_ref, masks(), seg_col, seg_row, par_ref[:CONV, end],
            par_ref[ROW_BIAS : ROW_BIAS + 1, end], par_ref[ROW_ALOG : ROW_ALOG + 1, :LANES],
            par_ref[ROW_DTB : ROW_DTB + 1, :LANES],
            g_scr, dcum, ddt,
        )
        for i in range(2):
            cols = slice(i * LANES, (i + 1) * LANES)
            dp[2 * blocks, :, cols] = d_bc[i].astype(BF)
            end = slice(INNER + i * LANES, INNER + (i + 1) * LANES)
            for k in range(CONV):
                small_out[k : k + 1, end] = d_weight[i][k]
            small_out[4:5, end] = d_bias[i]
        dp[2 * blocks, :, 2 * LANES : 3 * LANES] = d_raw.astype(BF)
        dp[2 * blocks, :, 3 * LANES :] = jnp.zeros((rows, LANES), BF)
        small_out[5:6, INNER : INNER + LANES] = d_alog
        small_out[5:6, INNER + LANES :] = d_dtb

    for i in range(small.stages):

        @pl.when(step == mix_steps + i)
        def _(i=i):
            small.stage(i)

    @pl.when((step >= n_out) & (step < chunks - 1))
    def _():
        grad = dp[chunk_at(step - n_out, blocks)]
        for s in range(shards):
            dn[s] += mm(grad, w_ref[s])

    @pl.when(step == chunks - 1)
    def _():
        grad = dp[n_in - 1]
        keep = iota(w_ref.shape[1:], 0) < tail
        d_normed = jnp.concatenate(
            [dn[s] + mm(grad, jnp.where(keep, w_ref[s], 0)) for s in range(shards)], axis=1
        )
        hid = hidden_ref[...].astype(F32)
        scale = lax.rsqrt(jnp.mean(hid * hid, axis=1, keepdims=True) + EPS)
        unit = hid * scale
        grad_norm = jnp.sum(d_normed * unit, axis=0, keepdims=True)
        for i in range(hid.shape[1] // LANES):
            norm_out[i : i + 1, :] = grad_norm[:, i * LANES : (i + 1) * LANES]
        du = d_normed * par_ref[ROW_NORM : ROW_NORM + 1, : hid.shape[1]]
        gh_out[...] = cot_ref[...].astype(F32) + scale * (du - unit * jnp.mean(du * unit, axis=1, keepdims=True))

    for i in range(norm.stages):

        @pl.when(step == chunks - 1 + i)
        def _(i=i):
            norm.stage(i)


def mixer_backward_and_sums(saved, hidden, cotangent, seg_ids, rep, shards):
    (w3, ow3, proj, y, low_t, r, b, c, cbt, dt, cum, cumt, mask, normed_t, params, _, rd, seg_col) = saved
    rows, width = hidden.shape
    inner = low_t.shape[0]
    depth = width // shards
    wide_block = 4 * LANES
    blocks = inner // wide_block
    n_out = width // (2 * LANES)
    n_in = proj.shape[1] // wide_block
    q = depth // 4
    chunks = n_out + n_in
    steps = chunks + 7
    n_small = SmallSum.count(rep, shards)
    n_extra = max(1, n_small - 3 - (shards - 1))
    last = 2 * blocks - 1
    mix = lambda offset: pl.BlockSpec((rows, 2 * LANES), lambda i: (0, offset + jnp.minimum(i, last)))
    const = lambda shape, at=None: pl.BlockSpec(shape, lambda i: at or (0,) * len(shape), pipeline_mode=pl.Buffered(1))
    f = lambda *s: jax.ShapeDtypeStruct(s, F32)
    h = lambda *s: jax.ShapeDtypeStruct(s, BF)
    vm = pltpu.VMEM
    dma = lambda *s: pltpu.SemaphoreType.DMA(s)
    anywhere = pl.BlockSpec(memory_space=pl.ANY)
    pairs_bc = inner // LANES
    in_specs = [
        mix(0), mix(2 * blocks), mix(0),
        pl.BlockSpec((2 * LANES, width), lambda i: (jnp.minimum(i, last), 0)),
        const((rows, 2 * LANES), (0, pairs_bc)), const((rows, LANES), (0, 2 * pairs_bc + 2)),
        const((rows, LANES)), const((rows, LANES)), const((rows, LANES)), const((rows, LANES)),
        const((rows, rows)), const((rows, LANES)), const((rows, LANES)), const((LANES, rows)),
        const((CONV - 1, rows, LANES)), const((rows, LANES)), const((1, rows)), const(params.shape),
        pl.BlockSpec(
            (shards, wide_block, depth), lambda i: (0, chunk_at(jnp.clip(i - n_out, 0, n_in - 1), blocks), 0)
        ),
        const((inner, rows)), const((rows, width)), const((width, rows)), const((rows, width)),
    ]
    whole_out = lambda shape: pl.BlockSpec(shape, lambda i: (0,) * len(shape))
    small_shape, norm_shape = (8, CONV_CH), (16, LANES)
    kinds = [(2, 4 * q), (2, 2 * q), (2, q)]
    scratch = [
        vm((rows, 2 * LANES), BF), vm((rows, 3 * LANES), BF), vm((rows, rows), F32), vm((rows, LANES), F32),
        vm((rows, LANES), F32), vm((n_in, rows, wide_block), BF), vm((shards, rows, depth), F32),
        vm((rows, 2 * LANES), F32),
    ]
    for o, height in kinds:
        shape = (o, shards, height, LANES)
        scratch += [vm((2, *shape), F32), vm((2, *shape), BF), vm((4, *shape), BF)]
    scratch += [
        vm((2, 2, q, LANES), F32), vm((2, shards - 1, 2, q, LANES), BF), vm((4, shards - 1, 2, q, LANES), BF),
        vm((8, 2, 4 * q, LANES), BF), vm((8, 2, LANES, 4 * q), BF),
        vm((n_small, *small_shape), F32), vm((n_small, *norm_shape), F32),
        dma(2), dma(4), dma(2, 2), dma(4, 2), dma(2, 2), dma(4, 2), dma(2, shards - 1), dma(4, shards - 1),
        dma(8, 2), dma(8, 2), dma(8, 2), dma(8, 2), dma(8, 2), dma(8, 2), dma(8, 2),
        vm((2, n_extra, 2, q, LANES), F32), dma(2, n_extra), dma(2, n_extra),
        dma(n_small), dma(n_small), dma(n_small), dma(n_small),
    ]
    return pl.pallas_call(
        functools.partial(
            reduce_kernel, rep=rep, shards=shards, q=q, blocks=blocks, n_out=n_out, n_in=n_in,
            tail=w3.shape[1] - (n_in - 1) * wide_block,
        ),
        grid=(steps,),
        in_specs=in_specs,
        out_specs=[anywhere, anywhere, whole_out((rows, width)), whole_out(small_shape), whole_out(norm_shape)],
        out_shape=[
            h(n_in * wide_block, depth), h(inner // shards, width), f(rows, width), f(*small_shape), f(*norm_shape),
        ],
        scratch_shapes=scratch,
        compiler_params=pltpu.CompilerParams(
            vmem_limit_bytes=VMEM_LIMIT, collective_id=2, has_side_effects=True
        ),
        name="mixer_backward_and_sums",
    )(
        proj, proj, y, ow3.reshape(inner, width), proj, proj, r, rd, b, c, cbt, dt, cum, cumt, mask, seg_col, seg_ids,
        params, w3, low_t, cotangent, normed_t, hidden,
    )


def per_device(
    hidden, seg_ids, cotangent, in_weight, out_weight, norm_gain, gated_gain, conv_weight, conv_bias, a_log, d_skip,
    dt_bias,
):
    rep, shards = lax.axis_size("rep"), lax.axis_size("shard")
    shard_at = lax.axis_index("shard")
    wide_row = -(-conv_bias.shape[0] // LANES) * LANES
    row = lambda v: jnp.pad(v, ((0, 0), (0, wide_row - v.shape[1])))
    singles = (conv_bias, gated_gain, norm_gain, a_log, d_skip, dt_bias)
    pack = jnp.concatenate(
        [row(conv_weight), *(row(v[None]) for v in singles), jnp.zeros((16 - CONV - len(singles), wide_row), BF)], axis=0
    )
    wt = in_weight.T
    saved = mixer_forward(hidden, cotangent, seg_ids, wt, out_weight, pack, rep, shards)
    mixed = saved[15]
    g_in, g_out, grad_hidden, small, norm = mixer_backward_and_sums(saved, hidden, cotangent, seg_ids, rep, shards)
    g_in = g_in[: wt.shape[0]].astype(F32).T
    g_out = g_out.astype(F32)

    def own(value, size):
        return lax.dynamic_slice_in_dim(value, shard_at * size, size, value.ndim - 1)

    heads, gains, convs = a_log.shape[0], gated_gain.shape[0], conv_bias.shape[0]
    outs = (
        own(norm.reshape(-1), norm_gain.shape[0]), own(small[5, :INNER], gains), own(small[:CONV], convs),
        own(small[4], convs), own(small[5, INNER : INNER + HEADS], heads),
        own(small[6, :INNER], gains).reshape(heads, HEAD_DIM).sum(1),
        own(small[5, INNER + LANES : INNER + LANES + HEADS], heads),
    )
    return (mixed, grad_hidden, g_in, g_out, *outs)


def solution(mesh):
    both = ("rep", "shard")
    shard = P("shard")
    placed = (P(both, None), P(both, None), P(both, None), P("shard", None), P("shard", None), shard, shard,
              P(None, "shard"), shard, shard, shard, shard)
    outs = (P(both, None), P(both, None), P("shard", None), P("shard", None), shard, shard, P(None, "shard"), shard,
            shard, shard, shard)
    return jax.shard_map(per_device, mesh=mesh, in_specs=placed, out_specs=outs, check_vma=False)
```

```python
import functools
import jax
import jax.numpy as jnp
from jax import lax
from jax.experimental import pallas as pl
from jax.experimental.pallas import tpu as pltpu
from jax.sharding import PartitionSpec as P

HEADS = 48
HEAD_DIM = 64
STATE = 128
CONV = 4
INNER = 3072
CONV_CH = 3328
LANES = 128
EPS = 1e-05
BF = jnp.bfloat16
F32 = jnp.float32
HIGH = lax.Precision.HIGHEST
VMEM_LIMIT = 63 * 2**20
MESH = pl.DeviceIdType.MESH


def mm(a, b):
    return jnp.dot(a, b, preferred_element_type=F32)


def mm_t(a, b):
    return lax.dot_general(a, b, (((1,), (1,)), ((), ())), preferred_element_type=F32)


def pieces(value, count):
    parts = []
    for _ in range(count):
        part = value.astype(BF)
        parts.append(part)
        value = value - part.astype(F32)
    return parts


def iota(shape, dim):
    return lax.broadcasted_iota(jnp.int32, shape, dim)


def head_of_lane(pair):
    heads, lanes = iota((LANES, LANES), 0), iota((LANES, LANES), 1)
    return (heads == 2 * pair + lanes // HEAD_DIM).astype(BF)


def one_head(head):
    return (iota((LANES, LANES), 0) == head).astype(BF)


def conv_shifts(value, masks):
    return [pltpu.roll(value, k, 0) * masks[k - 1] for k in range(1, CONV)]


def conv_apply(value, shifts, weight, bias):
    total = bias + weight[CONV - 1 : CONV] * value
    for k in range(1, CONV):
        total = total + weight[CONV - 1 - k : CONV - k] * shifts[k - 1]
    return total


def conv_back(d_pre, value, shifts, masks, weight):
    rows = d_pre.shape[0]
    d_value = weight[CONV - 1 : CONV] * d_pre
    d_weight = [jnp.sum(d_pre * value, axis=0, keepdims=True)]
    for k in range(1, CONV):
        d_weight.append(jnp.sum(d_pre * shifts[k - 1], axis=0, keepdims=True))
        d_value = d_value + weight[CONV - 1 - k : CONV - k] * pltpu.roll(
            d_pre * masks[k - 1], rows - k, 0
        )
    d_bias = jnp.sum(d_pre, axis=0, keepdims=True)
    return d_value, d_weight[::-1], d_bias


def silu_parts(value):
    sig = 1.0 / (1.0 + jnp.exp(-value))
    return sig, value * sig


def decay(col, row, clamp):
    gap = col - row
    return jnp.exp(jnp.minimum(gap, 0.0) if clamp else gap)


def wide(col, width):
    return jnp.concatenate([col] * (width // LANES), axis=1)


def backward_pair(
    pair, z, value, y, dgn, r, rd, cw, cb, skip, gain, masks, dt2, cum3, cumt_ref, cbt_ref, g_scr, dcum, ddt
):
    rows = z.shape[0]
    half = rows // 2
    shifts = conv_shifts(value, masks)
    pre = conv_apply(value, shifts, cw, cb)
    sp, x = silu_parts(pre)
    sg, sz = silu_parts(z)
    scanned = y + skip * x
    g = scanned * sz
    dgn_r = dgn * r
    d_gain = jnp.sum(dgn_r * g, axis=0, keepdims=True)
    dg = gain * dgn_r - g * rd
    dz = (dg * scanned * (sg * (1.0 + z * (1.0 - sg)))).astype(BF)
    dsc = dg * sz
    d_skip = jnp.sum(dsc * x, axis=0, keepdims=True)
    dy = dsc.astype(BF)
    spread = head_of_lane(pair)
    step = mm(dt2[...], jnp.concatenate([spread, spread], axis=0))
    xt = (x * step).astype(BF)
    first = iota((rows, LANES), 1) < HEAD_DIM
    zero = jnp.zeros_like(xt)
    dxts = []
    for side in range(2):
        head = 2 * pair + side
        pick = one_head(head)
        col = mm(cum3[...], jnp.concatenate([pick] * 3, axis=0))
        row = cumt_ref[pl.ds(head, 1), :]
        low_row, high_row = row[:, :half], row[:, half:]
        top, bottom = wide(col[:half], half), wide(col[half:], half)
        xs = jnp.where(first == (side == 0), xt, zero)
        parts = []
        for js, is_, jcol, irow, clamp in (
            (slice(0, half), slice(0, half), top, low_row, True),
            (slice(0, half), slice(half, rows), top, high_row, False),
            (slice(half, rows), slice(half, rows), bottom, high_row, True),
        ):
            e = decay(irow, jcol, clamp)
            parts.append(mm((e * cbt_ref[js, is_]).astype(BF), dy[is_]))
            g_scr[js, is_] += e * mm_t(xs[js], dy[is_])
        dxts.append(jnp.concatenate([parts[0] + parts[1], parts[2]], axis=0))
    dxt = jnp.where(first, dxts[0], dxts[1])
    for ref, term in ((dcum, dy.astype(F32) * y - xt.astype(F32) * dxt), (ddt, x * dxt)):
        hi, lo = pieces(term, 2)
        ref[...] += mm_t(hi, spread) + mm_t(lo, spread)
    dx = skip * dsc + step * dxt
    d_pre = dx * (sp * (1.0 + pre * (1.0 - sp)))
    d_value, d_weight, d_bias = conv_back(d_pre, value, shifts, masks, cw)
    return dz, d_value.astype(BF), d_gain, d_skip, d_weight, d_bias


def backward_tail(
    bc_ref, dtraw_ref, b_ref, c_ref, dt_ref, masks, seg_col, seg_row, cw_bc, cb_bc, alog_ref, bias_ref,
    g_scr, dcum, ddt
):
    rows = dt_ref.shape[0]
    same = wide(seg_col[...], rows) == seg_row[...]
    later = (iota((rows, rows), 0) <= iota((rows, rows), 1)) & same
    gt = jnp.where(later, g_scr[...], 0.0)
    db = jnp.dot(gt, c_ref[...], precision=HIGH, preferred_element_type=F32)
    dc = jnp.dot(gt.T, b_ref[...], precision=HIGH, preferred_element_type=F32)
    d_bc, d_weights, d_biases = [], [], []
    for i, d_out in enumerate((db, dc)):
        cols = slice(i * LANES, (i + 1) * LANES)
        value = bc_ref[:, cols]
        shifts = conv_shifts(value, masks)
        pre = conv_apply(value, shifts, cw_bc[:, cols], cb_bc[:, cols])
        sp, _ = silu_parts(pre)
        d_pre = d_out * (sp * (1.0 + pre * (1.0 - sp)))
        d_value, d_weight, d_bias = conv_back(d_pre, value, shifts, masks, cw_bc[:, cols])
        d_bc.append(d_value)
        d_weights.append(d_weight)
        d_biases.append(d_bias)
    step = dt_ref[...]
    live = iota((rows, LANES), 1) < HEADS
    rate = -jnp.exp(alog_ref)
    later_bf = later.astype(BF)
    dlog = sum(mm(later_bf, part) for part in pieces(dcum[...], 3)[::-1])
    dstep = ddt[...] + dlog * rate
    raw = jnp.where(live, dtraw_ref[...] + bias_ref, 0.0)
    d_raw = jnp.where(live, dstep / (1.0 + jnp.exp(-raw)), 0.0)
    d_alog = jnp.sum(dlog * step, axis=0, keepdims=True) * rate
    return d_bc, d_raw, d_weights, d_biases, d_alog, jnp.sum(d_raw, axis=0, keepdims=True)


class Place:
    def __init__(self, rep, shards):
        self.rep, self.shards = rep, shards
        r, self.me = lax.axis_index("rep"), lax.axis_index("shard")
        self.r = r
        self.core, self.a, self.b = r % 2, (r // 2) % 2, (r // 4) % 2
        self.core_peer = (r + 1 - 2 * self.core, self.me)
        self.a_peer = (r + 2 - 4 * self.a, self.me)
        self.b_peer = (r + 4 - 8 * self.b, self.me)
        self.extra = []
        stride = 8
        while stride < rep:
            bit = (r // stride) % 2
            self.extra.append((r + stride - 2 * stride * bit, self.me))
            stride *= 2
        self.quarter = 2 * self.a + self.b

    def shard_bit(self, j):
        bit = (self.me // (1 << j)) % 2
        return bit, (self.r, self.me + (1 << j) - (2 << j) * bit)

    def shard_peer(self, distance):
        return (self.r, (self.me + distance) % self.shards)

    def partners(self):
        return [self.core_peer, self.a_peer, self.b_peer, *self.extra] + [
            self.shard_peer(d) for d in range(1, self.shards)
        ]

    def greet(self):
        barrier = pltpu.get_barrier_semaphore()
        partners = self.partners()
        for partner in partners:
            pl.semaphore_signal(barrier, inc=1, device_id=partner, device_id_type=MESH)
        pl.semaphore_wait(barrier, len(partners))


def remote(src, dst, send, recv, device):
    return pltpu.make_async_remote_copy(
        src_ref=src, dst_ref=dst, send_sem=send, recv_sem=recv, device_id=device, device_id_type=MESH
    )


class SmallSum:
    def __init__(self, place, buf, slots, sends, recvs):
        self.buf, self.slots, self.sends, self.recvs = buf, slots, sends, recvs
        pairs = [place.core_peer, place.a_peer, place.b_peer, *place.extra]
        self.groups = [[peer] for peer in pairs] + [[place.shard_peer(d) for d in range(1, place.shards)]]
        self.stages = len(self.groups) + 1

    @staticmethod
    def count(rep, shards):
        return rep.bit_length() - 1 + shards - 1

    def copies(self, group):
        at = sum(len(g) for g in self.groups[:group])
        return [
            remote(self.buf, self.slots.at[at + i], self.sends.at[at + i], self.recvs.at[at + i], peer)
            for i, peer in enumerate(self.groups[group])
        ]

    def stage(self, number):
        if number > 0:
            at = sum(len(g) for g in self.groups[: number - 1])
            copies = self.copies(number - 1)
            for copy in copies:
                copy.wait()
            total = self.buf[...]
            for i in range(len(copies)):
                total = total + self.slots[at + i]
            self.buf[...] = total
        if number < len(self.groups):
            for copy in self.copies(number):
                copy.start()


def small_tiles(s, shards):
    def span(total):
        size = total // shards
        return range(s * size // LANES * LANES, (s + 1) * size, LANES)

    tiles = [(row, lane) for row in range(CONV + 1) for lane in span(CONV_CH)]
    tiles += [(row, lane) for row in (5, 6) for lane in span(INNER)]
    return tiles + [(5, INNER), (5, INNER + LANES)]


def forward_setup(
    bc, raw, seg_col, seg_row, cw, cb, alog, bias, outs, cb_scr, dt2, cum3
):
    b_out, c_out, cbt_out, dt_out, cum_out, cumt_out, mask_out = outs
    rows = raw.shape[0]
    at = iota((rows, LANES), 0)
    for k in range(1, CONV):
        same = (pltpu.roll(seg_col, k, 0) == seg_col) & (at >= k)
        mask_out[k - 1] = same.astype(F32)
    masks = [mask_out[k - 1] for k in range(1, CONV)]
    results = []
    for i in range(2):
        cols = slice(i * LANES, (i + 1) * LANES)
        value = bc[:, cols]
        pre = conv_apply(value, conv_shifts(value, masks), cw[:, cols], cb[:, cols])
        results.append(silu_parts(pre)[1])
    b_out[...] = results[0]
    c_out[...] = results[1]
    products = lax.dot_general(
        results[1], results[0], (((1,), (1,)), ((), ())), precision=HIGH, preferred_element_type=F32
    )
    lower = iota((rows, rows), 0) >= iota((rows, rows), 1)
    allowed = lower & (wide(seg_col, rows) == seg_row)
    products = jnp.where(allowed, products, 0.0)
    cb_scr[...] = products
    cbt_out[...] = products.T
    live = iota((rows, LANES), 1) < HEADS
    raw = jnp.where(live, raw + bias, 0.0)
    step = jnp.where(live, jnp.maximum(raw, 0.0) + jnp.log(1.0 + jnp.exp(-jnp.abs(raw))), 0.0)
    dt_out[...] = step
    hi, lo = pieces(step, 2)
    dt2[:, :LANES] = hi
    dt2[:, LANES:] = lo
    log_rate = step * -jnp.exp(alog)
    tri = lower.astype(BF)
    cum = sum(mm(tri, part) for part in pieces(log_rate, 3)[::-1])
    cum_out[...] = cum
    cumt_out[...] = cum.T
    for i, part in enumerate(pieces(cum, 3)):
        cum3[:, i * LANES : (i + 1) * LANES] = part


def skip_lanes(skip_row, spread):
    return mm(jnp.broadcast_to(skip_row, (8, LANES)).astype(BF), spread)[0:1]


def forward_pair(pair, z, value, cw, cb, skip_row, masks, dt2, cum3, cumt_ref, cb_scr):
    rows = z.shape[0]
    half = rows // 2
    pre = conv_apply(value, conv_shifts(value, masks), cw, cb)
    x = silu_parts(pre)[1]
    spread = head_of_lane(pair)
    step = mm(dt2[...], jnp.concatenate([spread, spread], axis=0))
    xt = (x * step).astype(BF)
    first = iota((rows, LANES), 1) < HEAD_DIM
    ys = []
    for side in range(2):
        head = 2 * pair + side
        pick = one_head(head)
        col = mm(cum3[...], jnp.concatenate([pick] * 3, axis=0))
        row = cumt_ref[pl.ds(head, 1), :]
        low_row, high_row = row[:, :half], row[:, half:]
        top, bottom = wide(col[:half], half), wide(col[half:], half)
        m00 = (decay(top, low_row, True) * cb_scr[:half, :half]).astype(BF)
        m10 = (decay(bottom, low_row, False) * cb_scr[half:, :half]).astype(BF)
        m11 = (decay(bottom, high_row, True) * cb_scr[half:, half:]).astype(BF)
        ys.append(
            jnp.concatenate([mm(m00, xt[:half]), mm(m10, xt[:half]) + mm(m11, xt[half:])], axis=0)
        )
    y = jnp.where(first, ys[0], ys[1])
    g = (y + skip_lanes(skip_row, spread) * x) * silu_parts(z)[1]
    return y, g


ROW_BIAS, ROW_GAIN, ROW_NORM, ROW_ALOG, ROW_SKIP, ROW_DTB = 4, 5, 6, 7, 8, 9


def forward_kernel(
    hidden_ref, cot_ref, seg_row, wt_ref, ow_ref, pack_ref,
    w3, ow3, proj_out, y_out, lowt_out, r_out, b_out, c_out, cbt_out, dt_out, cum_out, cumt_out, mask_out,
    normt_out, small_out, mixed_out, rd_out, segc_out,
    normed3, pk, wbuf, owbuf, xbuf, zbuf, cb_scr, dt2, cum3, gated, ssq, low, acc,
    sz, rz, s2, r2, s3, r3, s4, r4, lw, st, rt, sp, rp, lc,
    *, rep, shards, blocks, n_out
):
    step = pl.program_id(0)
    place = Place(rep, shards)
    a, b, core, me, quarter = place.a, place.b, place.core, place.me, place.quarter
    rows, width = hidden_ref.shape
    depth = width // shards
    inner = blocks * 4 * LANES
    per = 4
    n_mix = 1 + 2 * blocks
    chunks = n_mix + n_out
    tail_at = 2 * inner + 2 * LANES
    tail = w3.shape[1] - tail_at
    total_rows = w3.shape[1]

    def rows_of(kind, c):
        if kind == "bc":
            return 2 * inner, 2 * LANES
        if kind == "in":
            j = (c - 1) // 2
            return ((c % 2) * inner + j * 4 * LANES), 4 * LANES
        return (c - n_mix) * LANES, LANES

    def view(kind, c, s, start, count, half=None):
        ref = ow3 if kind == "out" else w3
        base, _ = rows_of(kind, c)
        if half is not None and kind != "out":
            start, count = start + half * (count // 2), count // 2
        at = pl.ds(pl.multiple_of(base + start, 16), count)
        if half is not None and kind == "out":
            return ref.at[s, at, half * (width // 2) : (half + 1) * (width // 2)]
        return ref.at[s, at]

    def piece(kind, c, s, quarter, half=None):
        n = rows_of(kind, c)[1]
        return view(kind, c, s, core * (n // 2) + quarter * (n // 8), n // 8, half)

    def others():
        return [(d - 1, (me + d) % shards) for d in range(1, shards)]

    def copy1(kind, c):
        n = rows_of(kind, c)[1]
        base = rows_of(kind, c)[0]
        src = (ow_ref if kind == "out" else wt_ref).at[
            pl.ds(pl.multiple_of(base + core * (n // 2) + quarter * (n // 8), 16), n // 8)
        ]
        k = c % 8
        return [
            remote(src, piece(kind, c, me, quarter), sz.at[k, d - 1], rz.at[k, d - 1], place.shard_peer(d))
            for d in range(1, shards)
        ]

    def copy2(kind, c):
        k = c % 4
        return [
            remote(piece(kind, c, s, quarter), piece(kind, c, s, quarter), s2.at[k, i, d], r2.at[k, i, d], peer)
            for d, s in others()
            for i, peer in enumerate((place.a_peer, place.b_peer))
        ]

    def copy3(kind, c):
        k = c % 4
        from_a, from_b = 2 * (1 - a) + b, 2 * a + 1 - b
        return [
            remote(
                piece(kind, c, s, origin, i), piece(kind, c, s, origin, i), s3.at[k, i, d], r3.at[k, i, d], peer
            )
            for d, s in others()
            for i, (origin, peer) in enumerate(((from_a, place.b_peer), (from_b, place.a_peer)))
        ]

    def copy4(kind, c):
        k = c % 4
        n = rows_of(kind, c)[1]
        return [
            remote(
                view(kind, c, s, core * (n // 2), n // 2), view(kind, c, s, core * (n // 2), n // 2),
                s4.at[k, d], r4.at[k, d], place.core_peer,
            )
            for d, s in others()
        ]

    def load(kind, c, back=False):
        k = c % 2
        base, n = rows_of(kind, c)
        if kind == "bc":
            n = total_rows - base
        full, own, buf = (ow3, ow_ref, owbuf) if kind == "out" else (w3, wt_ref, wbuf)
        at = pl.ds(pl.multiple_of(base, LANES), n)
        mine = buf.at[k, me, pl.ds(0, n)]
        if back:
            return [pltpu.make_async_copy(mine, full.at[me, at], lc.at[k])]
        copies = [pltpu.make_async_copy(own.at[at], mine, lw.at[k, 0])]
        for d, s in others():
            copies.append(pltpu.make_async_copy(full.at[s, at], buf.at[k, s, pl.ds(0, n)], lw.at[k, 1 + d]))
        return copies

    def at_chunk(c, run):
        @pl.when(c == 0)
        def _():
            run("bc", 0)

        @pl.when((c >= 1) & (c < n_mix))
        def _():
            run("in", c)

        @pl.when((c >= n_mix) & (c < chunks))
        def _():
            run("out", c)

    def tails():
        return [
            remote(
                wt_ref.at[tail_at:total_rows], w3.at[me, tail_at:total_rows], st.at[d - 1], rt.at[d - 1],
                place.shard_peer(d),
            )
            for d in range(1, shards)
        ]

    def packs():
        return [
            remote(pack_ref, pk.at[me], sp.at[d - 1], rp.at[d - 1], place.shard_peer(d)) for d in range(1, shards)
        ]

    def start(copies):
        for copy in copies:
            copy.start()

    def finish(copies):
        for copy in copies:
            copy.wait()

    def stage5(kind, c):
        finish(copy4(kind, c))
        start(load(kind, c))

    def stage4(kind, c):
        finish(copy3(kind, c))
        start(copy4(kind, c))

    def stage3(kind, c):
        finish(copy2(kind, c))
        start(copy3(kind, c))

    def stage2(kind, c):
        finish(copy1(kind, c))
        start(copy2(kind, c))

    def stage1(kind, c):
        start(copy1(kind, c))

    @pl.when(step == 0)
    def _():
        place.greet()
        start(packs())
        stage1("bc", 0)
        start(tails())
        pk[me] = pack_ref[...]
        wbuf[0, :, total_rows - 2 * inner :] = jnp.zeros(
            (shards, 4 * LANES - (total_rows - 2 * inner), depth), BF
        )
        ssq[...] = jnp.zeros_like(ssq)
        acc[...] = jnp.zeros_like(acc)
        small_out[...] = jnp.zeros_like(small_out)

    @pl.when(step == 3)
    def _():
        finish(tails())

    at_chunk(step - 6, lambda kind, c: finish(load(kind, c, True)))
    for number, run in ((1, stage1), (2, stage2), (3, stage3), (4, stage4), (5, stage5)):
        at_chunk(step - (number - 1) if number > 1 else step + 1, run)

    @pl.when(step == 1)
    def _():
        finish(packs())
        conv_n, gain_n, heads_n = CONV_CH // shards, inner // shards, HEADS // shards
        for s in range(shards):
            part = pk[s].astype(F32)
            small_out[0 : CONV + 1, s * conv_n : (s + 1) * conv_n] = part[0 : CONV + 1, :conv_n]
            small_out[ROW_GAIN : ROW_GAIN + 1, s * gain_n : (s + 1) * gain_n] = part[5:6, :gain_n]
            small_out[ROW_NORM : ROW_NORM + 1, s * depth : (s + 1) * depth] = part[6:7, :depth]
            for i in range(3):
                small_out[ROW_ALOG + i : ROW_ALOG + i + 1, s * heads_n : (s + 1) * heads_n] = part[
                    7 + i : 8 + i, :heads_n
                ]
        hid = hidden_ref[...].astype(F32)
        scale = lax.rsqrt(jnp.mean(hid * hid, axis=1, keepdims=True) + EPS)
        normed = hid * scale * small_out[ROW_NORM : ROW_NORM + 1, :width]
        for s in range(shards):
            normed3[s] = normed[:, s * depth : (s + 1) * depth].astype(BF)
        normt_out[...] = normed.T.astype(BF)
        seg = jnp.broadcast_to(seg_row[...], (LANES, rows)).astype(F32)
        segc_out[...] = seg.T.astype(jnp.int32)

    def arrive(kind, c):
        finish(load(kind, c))
        start(load(kind, c, True))

    c = step - 5
    masks = lambda: [mask_out[k - 1] for k in range(1, CONV)]

    def project(k):
        return sum(mm_t(normed3[s], wbuf[k, s]) for s in range(shards))

    @pl.when(c == 0)
    def _():
        arrive("bc", 0)
        proj_out[...] = project(0)
        outs = (b_out, c_out, cbt_out, dt_out, cum_out, cumt_out, mask_out)
        end = slice(inner, inner + 2 * LANES)
        forward_setup(
            proj_out[:, : 2 * LANES], proj_out[:, 2 * LANES : 3 * LANES], segc_out[...], seg_row[...],
            small_out[:CONV, end], small_out[ROW_BIAS : ROW_BIAS + 1, end],
            small_out[ROW_ALOG : ROW_ALOG + 1, :LANES], small_out[ROW_DTB : ROW_DTB + 1, :LANES],
            outs, cb_scr, dt2, cum3,
        )

    def pairs(j, first):
        def one(p, carry):
            pair = j * per + p
            cols = pl.ds(pl.multiple_of(p * LANES, LANES), LANES)
            at = pl.ds(pl.multiple_of(pair * LANES, LANES), LANES)
            y, g = forward_pair(
                pair, zbuf[:, cols], xbuf[:, cols], small_out[:CONV, at], small_out[ROW_BIAS : ROW_BIAS + 1, at],
                small_out[ROW_SKIP : ROW_SKIP + 1, :LANES], masks(), dt2, cum3, cumt_out, cb_scr,
            )
            y_out[:, cols] = y
            gated[pair] = g
            ssq[...] += g * g
            return carry

        lax.fori_loop(first, first + per // 2, one, 0)

    @pl.when((c >= 3) & (c <= n_mix) & (c % 2 == 1))
    def _():
        pairs((c - 3) // 2, per // 2)

    is_in = (c >= 1) & (c < n_mix)

    @pl.when(is_in & (c % 2 == 1))
    def _():
        arrive("in", c)
        value = project(c % 2)
        proj_out[...] = value
        xbuf[...] = value

    @pl.when(is_in & (c % 2 == 0))
    def _():
        arrive("in", c)
        value = project(c % 2)
        proj_out[...] = value
        zbuf[...] = value
        pairs((c - 2) // 2, 0)

    @pl.when(c == n_mix)
    def _():
        mean = jnp.sum(ssq[...], axis=1, keepdims=True) * (1.0 / inner)
        r = jnp.broadcast_to(lax.rsqrt(mean + EPS), (rows, LANES))
        r_out[...] = r

        def write(i, carry):
            cols = pl.ds(pl.multiple_of(i * LANES, LANES), LANES)
            value = gated[i] * r * small_out[ROW_GAIN : ROW_GAIN + 1, cols]
            low[:, cols] = value.astype(BF)
            lowt_out[cols, :] = value.T.astype(BF)
            return carry

        lax.fori_loop(0, inner // LANES, write, 0)

    @pl.when((c >= n_mix) & (c < chunks))
    def _():
        arrive("out", c)
        for s in range(shards):
            cols = pl.ds(pl.multiple_of(s * (inner // shards) + (c - n_mix) * LANES, LANES), LANES)
            acc[...] += mm(low[:, cols], owbuf[c % 2, s])

    @pl.when(c == chunks - 1)
    def _():
        added = acc[...]
        mixed_out[...] = (hidden_ref[...].astype(F32) + added).astype(BF)
        dots = jnp.sum(cot_ref[...].astype(F32) * added, axis=1, keepdims=True)
        r = r_out[...]
        rd_out[...] = r * r * (dots * (1.0 / inner))


def mixer_forward(hidden, cotangent, seg_ids, wt, ow, pack, rep, shards):
    rows, width = hidden.shape
    depth = width // shards
    inner = ow.shape[0] * shards
    blocks = inner // (4 * LANES)
    n_out = ow.shape[0] // LANES
    n_mix = 1 + 2 * blocks
    n_in = -(-wt.shape[0] // (4 * LANES))
    steps = n_mix + n_out + 6
    f = lambda *s: jax.ShapeDtypeStruct(s, F32)
    h = lambda *s: jax.ShapeDtypeStruct(s, BF)
    vm = pltpu.VMEM
    dma = lambda *s: pltpu.SemaphoreType.DMA(s)
    anywhere = pl.BlockSpec(memory_space=pl.ANY)
    const = lambda shape: pl.BlockSpec(shape, lambda i: (0,) * len(shape), pipeline_mode=pl.Buffered(1))
    fixed = lambda shape: pl.BlockSpec(shape, lambda i: (0,) * len(shape))

    def proj_at(i):
        c = jnp.clip(i - 5, 0, n_mix - 1)
        return (0, jnp.where(c == 0, 2 * blocks, (c % 2) * blocks + (c - 1) // 2))

    def y_at(i):
        return (0, jnp.clip((i - 7) // 2, 0, blocks - 1))

    out_shape = [
        h(shards, wt.shape[0], depth), h(shards, *ow.shape), f(rows, n_in * 4 * LANES), f(rows, inner),
        h(inner, rows), f(rows, LANES), f(rows, LANES), f(rows, LANES), f(rows, rows), f(rows, LANES),
        f(rows, LANES), f(LANES, rows), f(CONV - 1, rows, LANES), h(width, rows), f(16, CONV_CH), h(rows, width),
        f(rows, LANES), jax.ShapeDtypeStruct((rows, LANES), jnp.int32),
    ]
    block = (rows, 4 * LANES)
    out_specs = [anywhere, anywhere, pl.BlockSpec(block, proj_at), pl.BlockSpec(block, y_at)] + [
        fixed(s.shape) for s in out_shape[4:]
    ]
    n = shards - 1
    return pl.pallas_call(
        functools.partial(forward_kernel, rep=rep, shards=shards, blocks=blocks, n_out=n_out),
        grid=(steps,),
        in_specs=[
            const((rows, width)), const((rows, width)), const((1, rows)), anywhere, anywhere, const(pack.shape),
        ],
        out_specs=out_specs,
        out_shape=out_shape,
        scratch_shapes=[
            vm((shards, rows, depth), BF), vm((shards, *pack.shape), BF), vm((2, shards, 4 * LANES, depth), BF),
            vm((2, shards, LANES, width), BF), vm(block, F32), vm(block, F32), vm((rows, rows), F32), vm((rows, 2 * LANES), BF),
            vm((rows, 3 * LANES), BF), vm((inner // LANES, rows, LANES), F32), vm((rows, LANES), F32),
            vm((rows, inner), BF), vm((rows, width), F32),
            dma(8, n), dma(8, n), dma(4, 2, n), dma(4, 2, n), dma(4, 2, n), dma(4, 2, n), dma(4, n), dma(4, n),
            dma(2, shards), dma(n), dma(n), dma(n), dma(n), dma(2),
        ],
        compiler_params=pltpu.CompilerParams(
            vmem_limit_bytes=VMEM_LIMIT, collective_id=1, has_side_effects=True
        ),
        name="mixer_forward",
    )(hidden, cotangent, seg_ids, wt, ow, pack)


def chunk_at(j, blocks):
    return jnp.where(j < 2 * blocks, j // 2 + blocks * (j % 2), j)


def first_over_shards(c):
    return c % 3 == 1


def stage_steps(bits):
    more = list(range(1, bits - 1))
    rep_first = [0, 1, 2, 4, 5] + [5 + i for i in more]
    shard_first = [0, 1, 3, 5, 6] + [6 + i for i in more]
    end = max(rep_first[-1] + 2, shard_first[-1] + 1)
    tail = [end, end + 1, end + 3, end + 4]
    return rep_first + tail, shard_first + tail


def reduce_kernel(*refs, rep, shards, q, blocks, n_out, n_in, tail):
    (
        z_ref, x_ref, y_ref, ow_ref, bc_ref, dtraw_ref, r_ref, rd_ref, b_ref, c_ref, cbt_ref, dt_ref, cum_ref,
        cumt_ref, mask_ref, seg_col, seg_row, par_ref, w_ref, low_t, cot_ref, normed_t, hidden_ref,
        gin_out, gout_out, gh_out, norm_out,
        dt2, cum3, g_scr, dcum, ddt, dp, dn, dgn, ag, agt, small, small_rows, slots_norm,
        s5, r5, s6, r6, l7, s7, r7, xtra, sx, rx, sn, rn, sgh,
    ) = refs[:53]
    levels = refs[53:]
    bits = shards.bit_length() - 1
    last = 3 + bits
    keep, send, land, ssem, rsem = (dict(zip(range(1, last + 1), levels[i::5])) for i in range(5))

    step = pl.program_id(0)
    place = Place(rep, shards)
    rows = z_ref.shape[0]
    tile = z_ref.shape[1]
    mix_steps = dp.shape[2] * blocks // tile * 2
    chunks = n_out + n_in
    a, b, core, me, quarter = place.a, place.b, place.core, place.me, place.quarter

    norm = SmallSum(place, norm_out, slots_norm, sn, rn)

    @pl.when(step == 0)
    def _():
        place.greet()
        norm_out[...] = jnp.zeros_like(norm_out)
        dn[...] = jnp.zeros_like(dn)
        hi, lo = pieces(dt_ref[...], 2)
        dt2[:, :LANES] = hi
        dt2[:, LANES:] = lo
        for i, part in enumerate(pieces(cum_ref[...], 3)):
            cum3[:, i * LANES : (i + 1) * LANES] = part
        g_scr[...] = jnp.zeros_like(g_scr)
        dcum[...] = jnp.zeros_like(dcum)
        ddt[...] = jnp.zeros_like(ddt)

    def halving(shard_first, level):
        at = level - 2
        if shard_first != (at >= 2):
            j = at if shard_first else at - 2
            if j < bits:
                bit, peer = place.shard_bit(j)
                return [(shards >> (j + 1), 4 * q if shard_first else q, bit, peer)] * 2
        n = 1 if shard_first else shards
        turn = at - bits if shard_first else at
        by_a, by_b = (a, place.a_peer), (b, place.b_peer)
        if turn == 0:
            return [(n, 2 * q, *by_a), (2 * n, q, *by_b)]
        return [(n, q, *by_b), (n, q, *by_a)]

    def copies(shard_first, level, c):
        k, w = c % keep[level].shape[0], c % land[level].shape[0]
        peers = [place.core_peer] * 2 if level == 1 else [part[3] for part in halving(shard_first, level)]
        return [
            remote(
                send[level].at[k, o], land[level].at[w, o], ssem[level].at[k, o], rsem[level].at[w, o], peers[o]
            )
            for o in range(2)
        ]

    def start(group):
        for copy in group:
            copy.start()

    def finish(group):
        for copy in group:
            copy.wait()

    def block(g, quarter):
        return ag.at[g, :, pl.ds(pl.multiple_of(quarter * q, q), q)]

    def half_block(g, o, quarter):
        return ag.at[g, o, pl.ds(pl.multiple_of(quarter * q, q), q)]

    def copy5(g):
        mine = block(g, quarter)
        return [
            remote(mine, mine, s5.at[g, i], r5.at[g, i], peer) for i, peer in enumerate((place.a_peer, place.b_peer))
        ]

    def copy6(g):
        from_a = half_block(g, 0, 2 * (1 - a) + b)
        from_b = half_block(g, 1, 2 * a + 1 - b)
        return [
            remote(from_a, from_a, s6.at[g, 0], r6.at[g, 0], place.b_peer),
            remote(from_b, from_b, s6.at[g, 1], r6.at[g, 1], place.a_peer),
        ]

    def targets(c, is_out):
        if is_out:
            cols = pl.ds(pl.multiple_of(c * 2 * LANES + core * LANES, LANES), LANES)
            return [gout_out.at[pl.ds(o * 4 * q, 4 * q), cols] for o in range(2)]
        base = chunk_at(c - n_out, blocks) * 4 * LANES + core * 2 * LANES
        return [gin_out.at[pl.ds(pl.multiple_of(base + o * LANES, LANES), LANES)] for o in range(2)]

    def copy7(c, is_out):
        g, t = c % ag.shape[0], c % agt.shape[0]
        ends = targets(c, is_out)
        own = [ag.at[g, o] if is_out else agt.at[t, o] for o in range(2)]
        local = [pltpu.make_async_copy(own[o], ends[o], l7.at[g, o]) for o in range(2)]
        return local + [remote(own[o], ends[o], s7.at[g, o], r7.at[g, o], place.core_peer) for o in range(2)]

    def by_target(c, run):
        for is_out in (True, False):

            @pl.when((c < n_out) == is_out)
            def _(is_out=is_out):
                run(is_out)

    def stage_first(c):
        @pl.when(c < n_out)
        def _():
            base = c * 2 * LANES
            for s in range(shards):
                lhs = low_t[s * 8 * q : (s + 1) * 8 * q, :]
                for side, ref in ((core, keep[1]), (1 - core, send[1])):
                    cols = pl.ds(pl.multiple_of(base + side * LANES, LANES), LANES)
                    grad = mm(lhs, cot_ref[:, cols])
                    for o in range(2):
                        ref[0, o, s * 4 * q : (s + 1) * 4 * q] = grad[o * 4 * q : (o + 1) * 4 * q].astype(ref.dtype)

        @pl.when(c >= n_out)
        def _():
            n = chunk_at(c - n_out, blocks)
            for s in range(shards):
                own = slice(s * 4 * q, (s + 1) * 4 * q)
                for side, ref in ((core, keep[1]), (1 - core, send[1])):
                    cols = pl.ds(pl.multiple_of(side * 2 * LANES, 2 * LANES), 2 * LANES)
                    grad = mm(normed_t[own, :], dp[n, :, cols])
                    for o in range(2):
                        ref[0, o, own] = grad[:, o * LANES : (o + 1) * LANES].astype(ref.dtype)

        for side, ref in ((1, keep[1]), (0, send[1])):

            @pl.when((c == chunks - 1) & (core == side))
            def _(ref=ref):
                for s in range(shards):
                    at = s * 4 * q
                    ref[0, 1, at : at + small_rows.shape[1]] = small_rows[s].astype(ref.dtype)

        start(copies(False, 1, c))

    def stage_halve(shard_first, level, c):
        finish(copies(shard_first, level - 1, c))
        k0, w0 = c % keep[level - 1].shape[0], c % land[level - 1].shape[0]
        k = c % keep[level].shape[0]
        for o, (runs, size, bit, _) in enumerate(halving(shard_first, level)):

            def part(u, carry, o=o, size=size, bit=bit):
                own = pl.ds(pl.multiple_of((2 * u + bit) * size, size), size)
                other = pl.ds(pl.multiple_of((2 * u + 1 - bit) * size, size), size)
                end = pl.ds(pl.multiple_of(u * size, size), size)
                keep[level][k, o, end] = keep[level - 1][k0, o, own] + land[level - 1][w0, o, own].astype(F32)
                send[level][k, o, end] = (
                    keep[level - 1][k0, o, other] + land[level - 1][w0, o, other].astype(F32)
                ).astype(BF)
                return carry

            if runs == 1:
                part(0, 0)
            else:
                lax.fori_loop(0, runs, part, 0)
        start(copies(shard_first, level, c))

    def stage_total(shard_first, c):
        finish(copies(shard_first, last, c))
        k, w, g = c % keep[last].shape[0], c % land[last].shape[0], c % ag.shape[0]
        total = keep[last][k] + land[last][w].astype(F32)
        for i, peer in enumerate(place.extra):
            keep[last][k] = total
            copy = remote(keep[last].at[k], xtra.at[c % 2, i], sx.at[c % 2, i], rx.at[c % 2, i], peer)
            copy.start()
            copy.wait()
            total = total + xtra[c % 2, i]
        for o in range(2):
            ag[g, o, pl.ds(pl.multiple_of(quarter * q, q), q)] = total[o].astype(BF)
        start(copy5(g))

    def stage_forward(c):
        g = c % ag.shape[0]
        for copy in copy5(g):
            copy.wait_recv()
        start(copy6(g))

    def stage_out(c):
        g, t = c % ag.shape[0], c % agt.shape[0]
        for copy in copy6(g):
            copy.wait_recv()

        def run(is_out):
            if not is_out:
                for o in range(2):
                    agt[t, o] = ag[g, o].astype(F32).T.astype(BF)
            start(copy7(c, is_out))

        by_target(c, run)

    def stage_end(c):
        by_target(c, lambda is_out: finish(copy7(c, is_out)))
        g = c % ag.shape[0]
        for copy in copy5(g) + copy6(g):
            copy.wait_send()

    plans = stage_steps(bits)

    def run_stage(number):
        for shard_first in (False, True):
            c = step - plans[shard_first][number - 1]

            @pl.when((c >= 0) & (c < chunks) & (first_over_shards(c) == shard_first))
            def _(c=c, shard_first=shard_first):
                if number == 1:
                    stage_first(c)
                elif number <= last:
                    stage_halve(shard_first, number, c)
                elif number == last + 1:
                    stage_total(shard_first, c)
                else:
                    (stage_forward, stage_out, stage_end)[number - last - 2](c)

    order = [4, 2, 8, 3, 1, 5, 6, 9, 7]
    for number in order + list(range(10, last + 5)):
        run_stage(number)

    masks = lambda: [mask_ref[k - 1] for k in range(1, CONV)]

    def pairs(first, count):
        def one(p, carry):
            pair = step // 2 * (tile // LANES) + p
            cols = pl.ds(pl.multiple_of(p * LANES, LANES), LANES)
            at = pl.ds(pl.multiple_of(pair * LANES, LANES), LANES)
            skip = skip_lanes(par_ref[ROW_SKIP : ROW_SKIP + 1, :LANES], head_of_lane(pair))
            res = backward_pair(
                pair, z_ref[:, cols], x_ref[:, cols], y_ref[:, cols], dgn[:, cols], r_ref[...], rd_ref[...],
                par_ref[:CONV, at], par_ref[ROW_BIAS : ROW_BIAS + 1, at], skip, par_ref[ROW_GAIN : ROW_GAIN + 1, at],
                masks(), dt2, cum3, cumt_ref, cbt_ref, g_scr, dcum, ddt,
            )
            end = pl.ds(pl.multiple_of(pair % 4 * LANES, LANES), LANES)
            dp[pair // 4, :, end] = res[0]
            dp[blocks + pair // 4, :, end] = res[1]
            for k in range(CONV):
                small[k : k + 1, at] = res[4][k]
            small[4:5, at] = res[5]
            small[5:6, at] = res[2]
            small[6:7, at] = res[3]
            return carry

        lax.fori_loop(first, first + count, one, 0)

    @pl.when((step < mix_steps) & (step % 2 == 0))
    def _():
        dgn[...] = mm_t(cot_ref[...], ow_ref[...])
        pairs(0, 1)

    @pl.when((step < mix_steps) & (step % 2 == 1))
    def _():
        pairs(1, tile // LANES - 1)

    @pl.when(step == mix_steps - 1)
    def _():
        end = slice(INNER, INNER + 2 * LANES)
        d_bc, d_raw, d_weight, d_bias, d_alog, d_dtb = backward_tail(
            bc_ref, dtraw_ref, b_ref, c_ref, dt_ref, masks(), seg_col, seg_row, par_ref[:CONV, end],
            par_ref[ROW_BIAS : ROW_BIAS + 1, end], par_ref[ROW_ALOG : ROW_ALOG + 1, :LANES],
            par_ref[ROW_DTB : ROW_DTB + 1, :LANES], g_scr, dcum, ddt,
        )
        for i in range(2):
            cols = slice(i * LANES, (i + 1) * LANES)
            dp[2 * blocks, :, cols] = d_bc[i].astype(BF)
            end = slice(INNER + i * LANES, INNER + (i + 1) * LANES)
            for k in range(CONV):
                small[k : k + 1, end] = d_weight[i][k]
            small[4:5, end] = d_bias[i]
        dp[2 * blocks, :, 2 * LANES : 3 * LANES] = d_raw.astype(BF)
        dp[2 * blocks, :, 3 * LANES :] = jnp.zeros((rows, LANES), BF)
        small[5:6, INNER : INNER + LANES] = d_alog
        small[5:6, INNER + LANES :] = d_dtb
        for s in range(shards):
            for at, (row, lane) in enumerate(small_tiles(s, shards)):
                small_rows[s, at : at + 1, :] = small[row : row + 1, lane : lane + LANES]

    @pl.when((step >= n_out) & (step < chunks - 1))
    def _():
        grad = dp[chunk_at(step - n_out, blocks)]
        for s in range(shards):
            dn[s] += mm(grad, w_ref[s])

    @pl.when(step == chunks - 1)
    def _():
        grad = dp[n_in - 1]
        keep_rows = iota(w_ref.shape[1:], 0) < tail
        hid = hidden_ref[...].astype(F32)
        scale = lax.rsqrt(jnp.mean(hid * hid, axis=1, keepdims=True) + EPS)
        wide_cols = dgn.shape[1]
        together = wide_cols // dn.shape[2]
        dots = jnp.zeros((rows, 1), F32)

        def part(i):
            cols = slice(i * wide_cols, (i + 1) * wide_cols)
            d_normed = jnp.concatenate([dn[s] for s in range(i * together, (i + 1) * together)], axis=1)
            unit = hidden_ref[:, cols].astype(F32) * scale
            return cols, d_normed, unit, d_normed * par_ref[ROW_NORM : ROW_NORM + 1, cols]

        for s in range(shards):
            dn[s] += mm(grad, jnp.where(keep_rows, w_ref[s], 0))
        for i in range(shards // together):
            cols, d_normed, unit, du = part(i)
            grad_norm = jnp.sum(d_normed * unit, axis=0, keepdims=True)
            for j in range(wide_cols // LANES):
                at = i * (wide_cols // LANES) + j
                norm_out[at : at + 1, :] = grad_norm[:, j * LANES : (j + 1) * LANES]
            dots += jnp.sum(du * unit, axis=1, keepdims=True)
        dots = dots * (1.0 / hid.shape[1])
        for i in range(shards // together):
            cols, _, unit, du = part(i)
            dgn[...] = cot_ref[:, cols].astype(F32) + scale * (du - unit * dots)
            copy = pltpu.make_async_copy(dgn, gh_out.at[:, cols], sgh)
            copy.start()
            copy.wait()

    for i in range(norm.stages):

        @pl.when(step == chunks - 1 + i)
        def _(i=i):
            norm.stage(i)


def mixer_backward_and_sums(saved, hidden, cotangent, seg_ids, rep, shards):
    (w3, ow3, proj, y, low_t, r, b, c, cbt, dt, cum, cumt, mask, normed_t, params, _, rd, seg_col) = saved
    rows, width = hidden.shape
    inner = low_t.shape[0]
    depth = width // shards
    wide_block = 4 * LANES
    blocks = inner // wide_block
    n_out = width // (2 * LANES)
    n_in = proj.shape[1] // wide_block
    q = depth // 4
    chunks = n_out + n_in
    bits = shards.bit_length() - 1
    steps = chunks + stage_steps(bits)[0][-1]
    n_small = SmallSum.count(rep, shards)
    n_extra = max(1, n_small - 3 - (shards - 1))
    tile = 3 * LANES
    tiles = inner // tile
    mix = lambda offset: pl.BlockSpec((rows, tile), lambda i: (0, offset + jnp.minimum(i // 2, tiles - 1)))
    const = lambda shape, at=None: pl.BlockSpec(shape, lambda i: at or (0,) * len(shape), pipeline_mode=pl.Buffered(1))
    f = lambda *s: jax.ShapeDtypeStruct(s, F32)
    h = lambda *s: jax.ShapeDtypeStruct(s, BF)
    vm = pltpu.VMEM
    dma = lambda *s: pltpu.SemaphoreType.DMA(s)
    anywhere = pl.BlockSpec(memory_space=pl.ANY)
    pairs_bc = inner // LANES
    in_specs = [
        mix(0), mix(tiles), mix(0),
        pl.BlockSpec((tile, width), lambda i: (jnp.minimum(i // 2, tiles - 1), 0)),
        const((rows, 2 * LANES), (0, pairs_bc)), const((rows, LANES), (0, 2 * pairs_bc + 2)),
        const((rows, LANES)), const((rows, LANES)), const((rows, LANES)), const((rows, LANES)),
        const((rows, rows)), const((rows, LANES)), const((rows, LANES)), const((LANES, rows)),
        const((CONV - 1, rows, LANES)), const((rows, LANES)), const((1, rows)), const(params.shape),
        pl.BlockSpec(
            (shards, wide_block, depth), lambda i: (0, chunk_at(jnp.clip(i - n_out, 0, n_in - 1), blocks), 0)
        ),
        const((inner, rows)), const((rows, width)), const((width, rows)), const((rows, width)),
    ]
    whole_out = lambda shape: pl.BlockSpec(shape, lambda i: (0,) * len(shape))
    norm_shape = (16, LANES)
    small_height = -(-max(len(small_tiles(s, shards)) for s in range(shards)) // 16) * 16
    scratch = [
        vm((rows, 2 * LANES), BF), vm((rows, 3 * LANES), BF), vm((rows, rows), F32), vm((rows, LANES), F32),
        vm((rows, LANES), F32), vm((n_in, rows, wide_block), BF), vm((shards, rows, depth), F32), vm((rows, tile), F32),
        vm((8, 2, 4 * q, LANES), BF), vm((4, 2, LANES, 4 * q), BF),
        vm((8, CONV_CH), F32), vm((shards, small_height, LANES), F32), vm((n_small, *norm_shape), F32),
        dma(8, 2), dma(8, 2), dma(8, 2), dma(8, 2), dma(8, 2), dma(8, 2), dma(8, 2),
        vm((2, n_extra, 2, q, LANES), F32), dma(2, n_extra), dma(2, n_extra),
        dma(n_small), dma(n_small), pltpu.SemaphoreType.DMA,
    ]
    for level in range(1, 4 + bits):
        own, landing = {1: (1, 2), 2: (3, 8)}.get(level, (4, 8))
        shape = (2, (shards * 4 * q) >> (level - 1), LANES)
        scratch += [
            vm((own, *shape), F32), vm((own, *shape), BF), vm((landing, *shape), BF), dma(own, 2), dma(landing, 2),
        ]
    return pl.pallas_call(
        functools.partial(
            reduce_kernel, rep=rep, shards=shards, q=q, blocks=blocks, n_out=n_out, n_in=n_in,
            tail=w3.shape[1] - (n_in - 1) * wide_block,
        ),
        grid=(steps,),
        in_specs=in_specs,
        out_specs=[anywhere, anywhere, anywhere, whole_out(norm_shape)],
        out_shape=[
            h(n_in * wide_block, depth), h(inner // shards, width), f(rows, width), f(*norm_shape),
        ],
        scratch_shapes=scratch,
        compiler_params=pltpu.CompilerParams(
            vmem_limit_bytes=VMEM_LIMIT, collective_id=2, has_side_effects=True
        ),
        name="mixer_backward_and_sums",
    )(
        proj, proj, y, ow3.reshape(inner, width), proj, proj, r, rd, b, c, cbt, dt, cum, cumt, mask, seg_col, seg_ids,
        params, w3, low_t, cotangent, normed_t, hidden,
    )


def per_device(
    hidden, seg_ids, cotangent, in_weight, out_weight, norm_gain, gated_gain, conv_weight, conv_bias, a_log, d_skip,
    dt_bias,
):
    rep, shards = lax.axis_size("rep"), lax.axis_size("shard")
    shard_at = lax.axis_index("shard")
    wide_row = -(-conv_bias.shape[0] // LANES) * LANES
    row = lambda v: jnp.pad(v, ((0, 0), (0, wide_row - v.shape[1])))
    singles = (conv_bias, gated_gain, norm_gain, a_log, d_skip, dt_bias)
    pack = jnp.concatenate(
        [row(conv_weight), *(row(v[None]) for v in singles), jnp.zeros((16 - CONV - len(singles), wide_row), BF)], axis=0
    )
    wt = in_weight.T
    saved = mixer_forward(hidden, cotangent, seg_ids, wt, out_weight, pack, rep, shards)
    mixed = saved[15]
    g_in, g_out, grad_hidden, norm = mixer_backward_and_sums(saved, hidden, cotangent, seg_ids, rep, shards)
    heads, gains, convs = a_log.shape[0], gated_gain.shape[0], conv_bias.shape[0]
    tiles = [small_tiles(s, shards) for s in range(shards)]
    height = max(len(t) for t in tiles)
    small = g_in[g_in.shape[0] - LANES :, :height].astype(F32).T
    g_in = g_in[: wt.shape[0]].astype(F32).T
    g_out = g_out.astype(F32)

    n_gain = gains // LANES if gains % LANES == 0 else None
    n_conv = sum(1 for row, _ in tiles[0] if row == 0)

    def flat(first, count, start, size):
        return lax.dynamic_slice_in_dim(small[first : first + count].reshape(-1), start, size, 0)

    conv_start = shard_at * convs % LANES
    taps = jnp.stack([flat(k * n_conv, n_conv, conv_start, convs) for k in range(CONV + 1)])
    first = (CONV + 1) * n_conv
    outs = (
        lax.dynamic_slice_in_dim(norm.reshape(-1), shard_at * norm_gain.shape[0], norm_gain.shape[0], 0),
        small[first : first + n_gain].reshape(-1), taps[:CONV], taps[CONV],
        flat(first + 2 * n_gain, 1, shard_at * heads, heads),
        small[first + n_gain : first + 2 * n_gain].reshape(heads, HEAD_DIM).sum(1),
        flat(first + 2 * n_gain + 1, 1, shard_at * heads, heads),
    )
    return (mixed, grad_hidden, g_in, g_out, *outs)


def solution(mesh):
    both = ("rep", "shard")
    shard = P("shard")
    placed = (P(both, None), P(both, None), P(both, None), P("shard", None), P("shard", None), shard, shard,
              P(None, "shard"), shard, shard, shard, shard)
    outs = (P(both, None), P(both, None), P("shard", None), P("shard", None), shard, shard, P(None, "shard"), shard,
            shard, shard, shard)
    return jax.shard_map(per_device, mesh=mesh, in_specs=placed, out_specs=outs, check_vma=False)
```

```python
import functools
import jax
import jax.numpy as jnp
from jax import lax
from jax.experimental import pallas as pl
from jax.experimental.pallas import tpu as pltpu
from jax.sharding import PartitionSpec as P

HEADS = 48
HEAD_DIM = 64
STATE = 128
CONV = 4
INNER = 3072
CONV_CH = 3328
LANES = 128
EPS = 1e-05
LOG2E = 1.4426950408889634
BF = jnp.bfloat16
F32 = jnp.float32
HIGH = lax.Precision.HIGHEST
VMEM_LIMIT = 63 * 2**20
MESH = pl.DeviceIdType.MESH


def mm(a, b):
    return jnp.dot(a, b, preferred_element_type=F32)


def mm_t(a, b):
    return lax.dot_general(a, b, (((1,), (1,)), ((), ())), preferred_element_type=F32)


def pieces(value, count):
    parts = []
    for _ in range(count):
        part = value.astype(BF)
        parts.append(part)
        value = value - part.astype(F32)
    return parts


def iota(shape, dim):
    return lax.broadcasted_iota(jnp.int32, shape, dim)


def head_of_lane(pair):
    heads, lanes = iota((LANES, LANES), 0), iota((LANES, LANES), 1)
    return (heads == 2 * pair + lanes // HEAD_DIM).astype(BF)


def head_columns(cum3, pair):
    heads, lanes = iota((LANES, 2 * LANES), 0), iota((LANES, 2 * LANES), 1)
    pick = (heads == 2 * pair + lanes // LANES).astype(BF)
    cols = mm(cum3[...], jnp.concatenate([pick] * 3, axis=0))
    return cols[:, :LANES], cols[:, LANES:]


def conv_shifts(value, masks):
    return [pltpu.roll(value, k, 0) * masks[k - 1] for k in range(1, CONV)]


def conv_apply(value, shifts, weight, bias):
    total = bias + weight[CONV - 1 : CONV] * value
    for k in range(1, CONV):
        total = total + weight[CONV - 1 - k : CONV - k] * shifts[k - 1]
    return total


def conv_back(d_pre, value, shifts, masks, weight):
    rows = d_pre.shape[0]
    d_value = weight[CONV - 1 : CONV] * d_pre
    d_weight = [jnp.sum(d_pre * value, axis=0, keepdims=True)]
    for k in range(1, CONV):
        d_weight.append(jnp.sum(d_pre * shifts[k - 1], axis=0, keepdims=True))
        d_value = d_value + weight[CONV - 1 - k : CONV - k] * pltpu.roll(
            d_pre * masks[k - 1], rows - k, 0
        )
    d_bias = jnp.sum(d_pre, axis=0, keepdims=True)
    return d_value, d_weight[::-1], d_bias


def silu_parts(value):
    sig = 0.5 * jnp.tanh(0.5 * value) + 0.5
    return sig, value * sig


def silu_slope(sig, silu):
    return sig + silu - silu * sig


def decay(col, row, clamp):
    gap = col - row
    return jnp.exp2(jnp.minimum(gap, 0.0) if clamp else gap)


def wide(col, width):
    return jnp.concatenate([col] * (width // LANES), axis=1)


def backward_pair(
    pair, z, value, y, dgn, r, rd, cw, cb, skip, gain, masks, dt2, cum3, cumt_ref, cbt_ref, g_scr, dcum, ddt
):
    rows = z.shape[0]
    half = rows // 2
    shifts = conv_shifts(value, masks)
    pre = conv_apply(value, shifts, cw, cb)
    sp, x = silu_parts(pre)
    sg, sz = silu_parts(z)
    scanned = y + skip * x
    g = scanned * sz
    dgn_r = dgn * r
    d_gain = jnp.sum(dgn_r * g, axis=0, keepdims=True)
    dg = gain * dgn_r - g * rd
    dz = (dg * scanned * silu_slope(sg, sz)).astype(BF)
    dsc = dg * sz
    d_skip = jnp.sum(dsc * x, axis=0, keepdims=True)
    dy = dsc.astype(BF)
    spread = head_of_lane(pair)
    step = mm(dt2[...], jnp.concatenate([spread, spread], axis=0))
    both = jnp.concatenate([spread, spread], axis=1)
    xt = (x * step).astype(BF)
    first = iota((rows, LANES), 1) < HEAD_DIM
    zero = jnp.zeros_like(xt)
    columns = head_columns(cum3, pair)
    blocks = (
        (slice(0, half), slice(0, half), True),
        (slice(0, half), slice(half, rows), False),
        (slice(half, rows), slice(half, rows), True),
    )
    rows_of = [cumt_ref[pl.ds(2 * pair + side, 1), :] for side in range(2)]
    sides = [jnp.where(first == (side == 0), xt, zero) for side in range(2)]
    parts = [[], []]
    for js, is_, clamp in blocks:
        total = g_scr[js, is_]
        for side in range(2):
            e = decay(rows_of[side][:, is_], wide(columns[side][js], half), clamp)
            parts[side].append(mm((e * cbt_ref[js, is_]).astype(BF), dy[is_]))
            total = total + e * mm_t(sides[side][js], dy[is_])
        g_scr[js, is_] = total
    dxts = [jnp.concatenate([p[0] + p[1], p[2]], axis=0) for p in parts]
    dxt = jnp.where(first, dxts[0], dxts[1])
    for ref, term in ((dcum, dy.astype(F32) * y - xt.astype(F32) * dxt), (ddt, x * dxt)):
        ref[...] += mm_t(jnp.concatenate(pieces(term, 2), axis=1), both)
    dx = skip * dsc + step * dxt
    d_pre = dx * silu_slope(sp, x)
    d_value, d_weight, d_bias = conv_back(d_pre, value, shifts, masks, cw)
    return dz, d_value.astype(BF), d_gain, d_skip, d_weight, d_bias


def backward_tail(
    bc_ref, dtraw_ref, b_ref, c_ref, dt_ref, masks, seg_col, seg_row, cw_bc, cb_bc, alog_ref, bias_ref,
    g_scr, dcum, ddt
):
    rows = dt_ref.shape[0]
    same = wide(seg_col[...], rows) == seg_row[...]
    later = (iota((rows, rows), 0) <= iota((rows, rows), 1)) & same
    gt = jnp.where(later, g_scr[...], 0.0)
    db = jnp.dot(gt, c_ref[...], precision=HIGH, preferred_element_type=F32)
    dc = jnp.dot(gt.T, b_ref[...], precision=HIGH, preferred_element_type=F32)
    d_bc, d_weights, d_biases = [], [], []
    for i, d_out in enumerate((db, dc)):
        cols = slice(i * LANES, (i + 1) * LANES)
        value = bc_ref[:, cols]
        shifts = conv_shifts(value, masks)
        pre = conv_apply(value, shifts, cw_bc[:, cols], cb_bc[:, cols])
        sp, value_out = silu_parts(pre)
        d_pre = d_out * silu_slope(sp, value_out)
        d_value, d_weight, d_bias = conv_back(d_pre, value, shifts, masks, cw_bc[:, cols])
        d_bc.append(d_value)
        d_weights.append(d_weight)
        d_biases.append(d_bias)
    step = dt_ref[...]
    live = iota((rows, LANES), 1) < HEADS
    rate = -jnp.exp(alog_ref)
    later_bf = later.astype(BF)
    dlog = sum(mm(later_bf, part) for part in pieces(dcum[...], 3)[::-1])
    dstep = ddt[...] + dlog * rate
    raw = jnp.where(live, dtraw_ref[...] + bias_ref, 0.0)
    d_raw = jnp.where(live, dstep / (1.0 + jnp.exp(-raw)), 0.0)
    d_alog = jnp.sum(dlog * step, axis=0, keepdims=True) * rate
    return d_bc, d_raw, d_weights, d_biases, d_alog, jnp.sum(d_raw, axis=0, keepdims=True)


class Place:
    def __init__(self, rep, shards):
        self.rep, self.shards = rep, shards
        r, self.me = lax.axis_index("rep"), lax.axis_index("shard")
        self.r = r
        self.core, self.a, self.b = r % 2, (r // 2) % 2, (r // 4) % 2
        self.core_peer = (r + 1 - 2 * self.core, self.me)
        self.a_peer = (r + 2 - 4 * self.a, self.me)
        self.b_peer = (r + 4 - 8 * self.b, self.me)
        self.extra = []
        stride = 8
        while stride < rep:
            bit = (r // stride) % 2
            self.extra.append((r + stride - 2 * stride * bit, self.me))
            stride *= 2
        self.quarter = 2 * self.a + self.b

    def shard_bit(self, j):
        bit = (self.me // (1 << j)) % 2
        return bit, (self.r, self.me + (1 << j) - (2 << j) * bit)

    def shard_peer(self, distance):
        return (self.r, (self.me + distance) % self.shards)

    def partners(self):
        return [self.core_peer, self.a_peer, self.b_peer, *self.extra] + [
            self.shard_peer(d) for d in range(1, self.shards)
        ]

    def greet(self):
        barrier = pltpu.get_barrier_semaphore()
        partners = self.partners()
        for partner in partners:
            pl.semaphore_signal(barrier, inc=1, device_id=partner, device_id_type=MESH)
        pl.semaphore_wait(barrier, len(partners))


def remote(src, dst, send, recv, device):
    return pltpu.make_async_remote_copy(
        src_ref=src, dst_ref=dst, send_sem=send, recv_sem=recv, device_id=device, device_id_type=MESH
    )


class SmallSum:
    def __init__(self, place, buf, slots, sends, recvs):
        self.buf, self.slots, self.sends, self.recvs = buf, slots, sends, recvs
        pairs = [place.core_peer, place.a_peer, place.b_peer, *place.extra]
        self.groups = [[peer] for peer in pairs] + [[place.shard_peer(d) for d in range(1, place.shards)]]
        self.stages = len(self.groups) + 1

    @staticmethod
    def count(rep, shards):
        return rep.bit_length() - 1 + shards - 1

    def copies(self, group):
        at = sum(len(g) for g in self.groups[:group])
        return [
            remote(self.buf, self.slots.at[at + i], self.sends.at[at + i], self.recvs.at[at + i], peer)
            for i, peer in enumerate(self.groups[group])
        ]

    def stage(self, number):
        if number > 0:
            at = sum(len(g) for g in self.groups[: number - 1])
            copies = self.copies(number - 1)
            for copy in copies:
                copy.wait()
            total = self.buf[...]
            for i in range(len(copies)):
                total = total + self.slots[at + i]
            self.buf[...] = total
        if number < len(self.groups):
            for copy in self.copies(number):
                copy.start()


def small_tiles(s, shards):
    def span(total):
        size = total // shards
        return range(s * size // LANES * LANES, (s + 1) * size, LANES)

    tiles = [(row, lane) for row in range(CONV + 1) for lane in span(CONV_CH)]
    tiles += [(5, lane) for lane in span(INNER)]
    return tiles + [(5, INNER), (5, INNER + LANES), (6, 0)]


def forward_setup(
    bc, raw, seg_col, seg_row, cw, cb, alog, bias, outs, cb_scr, dt2, cum3
):
    b_out, c_out, cbt_out, dt_out, cum_out, cumt_out, mask_out = outs
    rows = raw.shape[0]
    at = iota((rows, LANES), 0)
    for k in range(1, CONV):
        same = (pltpu.roll(seg_col, k, 0) == seg_col) & (at >= k)
        mask_out[k - 1] = same.astype(F32)
    masks = [mask_out[k - 1] for k in range(1, CONV)]
    results = []
    for i in range(2):
        cols = slice(i * LANES, (i + 1) * LANES)
        value = bc[:, cols]
        pre = conv_apply(value, conv_shifts(value, masks), cw[:, cols], cb[:, cols])
        results.append(silu_parts(pre)[1])
    b_out[...] = results[0]
    c_out[...] = results[1]
    products = lax.dot_general(
        results[1], results[0], (((1,), (1,)), ((), ())), precision=HIGH, preferred_element_type=F32
    )
    lower = iota((rows, rows), 0) >= iota((rows, rows), 1)
    allowed = lower & (wide(seg_col, rows) == seg_row)
    products = jnp.where(allowed, products, 0.0)
    cb_scr[...] = products
    cbt_out[...] = products.T
    live = iota((rows, LANES), 1) < HEADS
    raw = jnp.where(live, raw + bias, 0.0)
    step = jnp.where(live, jnp.maximum(raw, 0.0) + jnp.log(1.0 + jnp.exp(-jnp.abs(raw))), 0.0)
    dt_out[...] = step
    hi, lo = pieces(step, 2)
    dt2[:, :LANES] = hi
    dt2[:, LANES:] = lo
    log_rate = step * (-LOG2E * jnp.exp(alog))
    tri = lower.astype(BF)
    cum = sum(mm(tri, part) for part in pieces(log_rate, 3)[::-1])
    cum_out[...] = cum
    cumt_out[...] = cum.T
    for i, part in enumerate(pieces(cum, 3)):
        cum3[:, i * LANES : (i + 1) * LANES] = part


def skip_lanes(skip_row, spread):
    return mm(jnp.broadcast_to(skip_row, (8, LANES)).astype(BF), spread)[0:1]


def forward_pair(pair, z, value, cw, cb, skip_row, masks, dt2, cum3, cumt_ref, cb_scr):
    rows = z.shape[0]
    half = rows // 2
    pre = conv_apply(value, conv_shifts(value, masks), cw, cb)
    x = silu_parts(pre)[1]
    spread = head_of_lane(pair)
    step = mm(dt2[...], jnp.concatenate([spread, spread], axis=0))
    xt = (x * step).astype(BF)
    first = iota((rows, LANES), 1) < HEAD_DIM
    ys = []
    columns = head_columns(cum3, pair)
    for side in range(2):
        head = 2 * pair + side
        col = columns[side]
        row = cumt_ref[pl.ds(head, 1), :]
        low_row, high_row = row[:, :half], row[:, half:]
        top, bottom = wide(col[:half], half), wide(col[half:], half)
        m00 = (decay(top, low_row, True) * cb_scr[:half, :half]).astype(BF)
        m10 = (decay(bottom, low_row, False) * cb_scr[half:, :half]).astype(BF)
        m11 = (decay(bottom, high_row, True) * cb_scr[half:, half:]).astype(BF)
        ys.append(
            jnp.concatenate([mm(m00, xt[:half]), mm(m10, xt[:half]) + mm(m11, xt[half:])], axis=0)
        )
    y = jnp.where(first, ys[0], ys[1])
    g = (y + skip_lanes(skip_row, spread) * x) * silu_parts(z)[1]
    return y, g


ROW_BIAS, ROW_GAIN, ROW_NORM, ROW_ALOG, ROW_SKIP, ROW_DTB = 4, 5, 6, 7, 8, 9


def forward_kernel(
    hidden_ref, cot_ref, seg_row, wt_ref, ow_ref, cw_ref, cb_ref, gain_ref, ngain_ref, alog_ref, skip_ref, dtb_ref,
    w3, ow3, proj_out, y_out, lowt_out, r_out, b_out, c_out, cbt_out, dt_out, cum_out, cumt_out, mask_out,
    normt_out, small_out, mixed_out, rd_out, segc_out, dg_out,
    normed3, pack32, pack_ref, pk, wbuf, owbuf, xbuf, zbuf, cb_scr, dt2, cum3, gated, ssq, low, acc,
    sz, rz, s2, r2, s3, r3, s4, r4, lw, st, rt, sp, rp, lc,
    *, rep, shards, blocks, n_out
):
    step = pl.program_id(0)
    place = Place(rep, shards)
    a, b, core, me, quarter = place.a, place.b, place.core, place.me, place.quarter
    rows, width = hidden_ref.shape
    depth = width // shards
    inner = blocks * 4 * LANES
    per = 4
    n_mix = 1 + 2 * blocks
    chunks = n_mix + n_out
    tail_at = 2 * inner + 2 * LANES
    tail = w3.shape[1] - tail_at
    total_rows = w3.shape[1]

    def rows_of(kind, c):
        if kind == "bc":
            return 2 * inner, 2 * LANES
        if kind == "in":
            j = (c - 1) // 2
            return ((c % 2) * inner + j * 4 * LANES), 4 * LANES
        return (c - n_mix) * LANES, LANES

    def view(kind, c, s, start, count, half=None):
        ref = ow3 if kind == "out" else w3
        base, _ = rows_of(kind, c)
        if half is not None and kind != "out":
            start, count = start + half * (count // 2), count // 2
        at = pl.ds(pl.multiple_of(base + start, 16), count)
        if half is not None and kind == "out":
            return ref.at[s, at, half * (width // 2) : (half + 1) * (width // 2)]
        return ref.at[s, at]

    def piece(kind, c, s, quarter, half=None):
        n = rows_of(kind, c)[1]
        return view(kind, c, s, core * (n // 2) + quarter * (n // 8), n // 8, half)

    def others():
        return [(d - 1, (me + d) % shards) for d in range(1, shards)]

    def copy1(kind, c):
        n = rows_of(kind, c)[1]
        base = rows_of(kind, c)[0]
        src = (ow_ref if kind == "out" else wt_ref).at[
            pl.ds(pl.multiple_of(base + core * (n // 2) + quarter * (n // 8), 16), n // 8)
        ]
        k = c % 8
        return [
            remote(src, piece(kind, c, me, quarter), sz.at[k, d - 1], rz.at[k, d - 1], place.shard_peer(d))
            for d in range(1, shards)
        ]

    def copy2(kind, c):
        k = c % 4
        return [
            remote(piece(kind, c, s, quarter), piece(kind, c, s, quarter), s2.at[k, i, d], r2.at[k, i, d], peer)
            for d, s in others()
            for i, peer in enumerate((place.a_peer, place.b_peer))
        ]

    def copy3(kind, c):
        k = c % 4
        from_a, from_b = 2 * (1 - a) + b, 2 * a + 1 - b
        return [
            remote(
                piece(kind, c, s, origin, i), piece(kind, c, s, origin, i), s3.at[k, i, d], r3.at[k, i, d], peer
            )
            for d, s in others()
            for i, (origin, peer) in enumerate(((from_a, place.b_peer), (from_b, place.a_peer)))
        ]

    def copy4(kind, c):
        k = c % 4
        n = rows_of(kind, c)[1]
        return [
            remote(
                view(kind, c, s, core * (n // 2), n // 2), view(kind, c, s, core * (n // 2), n // 2),
                s4.at[k, d], r4.at[k, d], place.core_peer,
            )
            for d, s in others()
        ]

    def load(kind, c, back=False):
        k = c % 2
        base, n = rows_of(kind, c)
        if kind == "bc":
            n = total_rows - base
        full, own, buf = (ow3, ow_ref, owbuf) if kind == "out" else (w3, wt_ref, wbuf)
        at = pl.ds(pl.multiple_of(base, LANES), n)
        mine = buf.at[k, me, pl.ds(0, n)]
        if back:
            return [pltpu.make_async_copy(mine, full.at[me, at], lc.at[k])]
        copies = [pltpu.make_async_copy(own.at[at], mine, lw.at[k, 0])]
        for d, s in others():
            copies.append(pltpu.make_async_copy(full.at[s, at], buf.at[k, s, pl.ds(0, n)], lw.at[k, 1 + d]))
        return copies

    def at_chunk(c, run):
        @pl.when(c == 0)
        def _():
            run("bc", 0)

        @pl.when((c >= 1) & (c < n_mix))
        def _():
            run("in", c)

        @pl.when((c >= n_mix) & (c < chunks))
        def _():
            run("out", c)

    def tails():
        return [
            remote(
                wt_ref.at[tail_at:total_rows], w3.at[me, tail_at:total_rows], st.at[d - 1], rt.at[d - 1],
                place.shard_peer(d),
            )
            for d in range(1, shards)
        ]

    def packs():
        return [
            remote(pack_ref, pk.at[me], sp.at[d - 1], rp.at[d - 1], place.shard_peer(d)) for d in range(1, shards)
        ]

    def start(copies):
        for copy in copies:
            copy.start()

    def finish(copies):
        for copy in copies:
            copy.wait()

    def stage5(kind, c):
        finish(copy4(kind, c))
        start(load(kind, c))

    def stage4(kind, c):
        finish(copy3(kind, c))
        start(copy4(kind, c))

    def stage3(kind, c):
        finish(copy2(kind, c))
        start(copy3(kind, c))

    def stage2(kind, c):
        finish(copy1(kind, c))
        start(copy2(kind, c))

    def stage1(kind, c):
        start(copy1(kind, c))

    @pl.when(step == 0)
    def _():
        place.greet()
        stage1("bc", 0)
        pack32[...] = jnp.zeros_like(pack32)
        pack32[:CONV, : cw_ref.shape[1]] = cw_ref[...].astype(F32)
        for i, ref in enumerate((cb_ref, gain_ref, ngain_ref, alog_ref, skip_ref, dtb_ref)):
            n = ref.shape[0]
            pack32[CONV + i : CONV + i + 1, :n] = ref[...].astype(F32).reshape(1, n)
        pack_ref[...] = pack32[...].astype(BF)
        pk[me] = pack_ref[...]
        wbuf[0, :, total_rows - 2 * inner :] = jnp.zeros(
            (shards, 4 * LANES - (total_rows - 2 * inner), depth), BF
        )
        ssq[...] = jnp.zeros_like(ssq)
        acc[...] = jnp.zeros_like(acc)
        small_out[...] = jnp.zeros_like(small_out)

    @pl.when(step == 4)
    def _():
        finish(tails())

    at_chunk(step - 6, lambda kind, c: finish(load(kind, c, True)))
    for number, run in ((1, stage1), (2, stage2), (3, stage3), (4, stage4), (5, stage5)):
        at_chunk(step - (number - 1) if number > 1 else step + 1, run)

    @pl.when(step == 1)
    def _():
        start(packs())

    @pl.when(step == 2)
    def _():
        start(tails())

    @pl.when(step == 3)
    def _():
        finish(packs())
        conv_n, gain_n, heads_n = CONV_CH // shards, inner // shards, HEADS // shards
        for s in range(shards):
            part = pk[s].astype(F32)
            small_out[0 : CONV + 1, s * conv_n : (s + 1) * conv_n] = part[0 : CONV + 1, :conv_n]
            small_out[ROW_GAIN : ROW_GAIN + 1, s * gain_n : (s + 1) * gain_n] = part[5:6, :gain_n]
            small_out[ROW_NORM : ROW_NORM + 1, s * depth : (s + 1) * depth] = part[6:7, :depth]
            for i in range(3):
                small_out[ROW_ALOG + i : ROW_ALOG + i + 1, s * heads_n : (s + 1) * heads_n] = part[
                    7 + i : 8 + i, :heads_n
                ]
        hid = hidden_ref[...].astype(F32)
        scale = lax.rsqrt(jnp.mean(hid * hid, axis=1, keepdims=True) + EPS)
        normed = hid * scale * small_out[ROW_NORM : ROW_NORM + 1, :width]
        for s in range(shards):
            normed3[s] = normed[:, s * depth : (s + 1) * depth].astype(BF)
        normt_out[...] = normed.T.astype(BF)
        seg = jnp.broadcast_to(seg_row[...], (LANES, rows)).astype(F32)
        segc_out[...] = seg.T.astype(jnp.int32)

    def arrive(kind, c):
        finish(load(kind, c))
        start(load(kind, c, True))

    c = step - 5
    masks = lambda: [mask_out[k - 1] for k in range(1, CONV)]

    def project(k):
        return sum(mm_t(normed3[s], wbuf[k, s]) for s in range(shards))

    @pl.when(c == 0)
    def _():
        arrive("bc", 0)
        proj_out[...] = project(0)
        outs = (b_out, c_out, cbt_out, dt_out, cum_out, cumt_out, mask_out)
        end = slice(inner, inner + 2 * LANES)
        forward_setup(
            proj_out[:, : 2 * LANES], proj_out[:, 2 * LANES : 3 * LANES], segc_out[...], seg_row[...],
            small_out[:CONV, end], small_out[ROW_BIAS : ROW_BIAS + 1, end],
            small_out[ROW_ALOG : ROW_ALOG + 1, :LANES], small_out[ROW_DTB : ROW_DTB + 1, :LANES],
            outs, cb_scr, dt2, cum3,
        )

    def pairs(j, first):
        def one(p, carry):
            pair = j * per + p
            cols = pl.ds(pl.multiple_of(p * LANES, LANES), LANES)
            at = pl.ds(pl.multiple_of(pair * LANES, LANES), LANES)
            y, g = forward_pair(
                pair, zbuf[:, cols], xbuf[:, cols], small_out[:CONV, at], small_out[ROW_BIAS : ROW_BIAS + 1, at],
                small_out[ROW_SKIP : ROW_SKIP + 1, :LANES], masks(), dt2, cum3, cumt_out, cb_scr,
            )
            y_out[:, cols] = y
            gated[pair] = g
            ssq[...] += g * g
            return carry

        lax.fori_loop(first, first + per // 2, one, 0)

    @pl.when((c >= 3) & (c <= n_mix) & (c % 2 == 1))
    def _():
        pairs((c - 3) // 2, per // 2)

    is_in = (c >= 1) & (c < n_mix)

    @pl.when(is_in & (c % 2 == 1))
    def _():
        arrive("in", c)
        value = project(c % 2)
        proj_out[...] = value
        xbuf[...] = value

    @pl.when(is_in & (c % 2 == 0))
    def _():
        arrive("in", c)
        value = project(c % 2)
        proj_out[...] = value
        zbuf[...] = value
        pairs((c - 2) // 2, 0)

    @pl.when(c == n_mix)
    def _():
        mean = jnp.sum(ssq[...], axis=1, keepdims=True) * (1.0 / inner)
        r = jnp.broadcast_to(lax.rsqrt(mean + EPS), (rows, LANES))
        r_out[...] = r

        def write(i, carry):
            cols = pl.ds(pl.multiple_of(i * LANES, LANES), LANES)
            value = gated[i] * r * small_out[ROW_GAIN : ROW_GAIN + 1, cols]
            low[:, cols] = value.astype(BF)
            lowt_out[cols, :] = value.T.astype(BF)
            return carry

        lax.fori_loop(0, inner // LANES, write, 0)

    @pl.when((c >= n_mix) & (c < chunks))
    def _():
        arrive("out", c)
        part = owbuf[c % 2].reshape(shards * LANES, width)
        lows = [
            low[:, pl.ds(pl.multiple_of(s * (inner // shards) + (c - n_mix) * LANES, LANES), LANES)]
            for s in range(shards)
        ]
        acc[...] += mm(jnp.concatenate(lows, axis=1), part)
        grads = mm_t(cot_ref[...], part)
        for s in range(shards):
            dg_out[s] = grads[:, s * LANES : (s + 1) * LANES]

    @pl.when(c == chunks - 1)
    def _():
        added = acc[...]
        mixed_out[...] = (hidden_ref[...].astype(F32) + added).astype(BF)
        dots = jnp.sum(cot_ref[...].astype(F32) * added, axis=1, keepdims=True)
        r = r_out[...]
        rd_out[...] = r * r * (dots * (1.0 / inner))


def mixer_forward(hidden, cotangent, seg_ids, wt, ow, singles, rep, shards):
    rows, width = hidden.shape
    depth = width // shards
    inner = ow.shape[0] * shards
    blocks = inner // (4 * LANES)
    n_out = ow.shape[0] // LANES
    n_mix = 1 + 2 * blocks
    n_in = -(-wt.shape[0] // (4 * LANES))
    steps = n_mix + n_out + 6
    pack = (16, -(-singles[1].shape[0] // LANES) * LANES)
    f = lambda *s: jax.ShapeDtypeStruct(s, F32)
    h = lambda *s: jax.ShapeDtypeStruct(s, BF)
    vm = pltpu.VMEM
    dma = lambda *s: pltpu.SemaphoreType.DMA(s)
    anywhere = pl.BlockSpec(memory_space=pl.ANY)
    const = lambda shape: pl.BlockSpec(shape, lambda i: (0,) * len(shape), pipeline_mode=pl.Buffered(1))
    fixed = lambda shape: pl.BlockSpec(shape, lambda i: (0,) * len(shape))

    def proj_at(i):
        c = jnp.clip(i - 5, 0, n_mix - 1)
        return (0, jnp.where(c == 0, 2 * blocks, (c % 2) * blocks + (c - 1) // 2))

    def y_at(i):
        return (0, jnp.clip((i - 7) // 2, 0, blocks - 1))

    out_shape = [
        h(shards, wt.shape[0], depth), h(shards, *ow.shape), f(rows, n_in * 4 * LANES), f(rows, inner),
        h(inner, rows), f(rows, LANES), f(rows, LANES), f(rows, LANES), f(rows, rows), f(rows, LANES),
        f(rows, LANES), f(LANES, rows), f(CONV - 1, rows, LANES), h(width, rows), f(16, CONV_CH), h(rows, width),
        f(rows, LANES), jax.ShapeDtypeStruct((rows, LANES), jnp.int32), f(shards, rows, inner // shards),
    ]
    block = (rows, 4 * LANES)
    out_specs = [anywhere, anywhere, pl.BlockSpec(block, proj_at), pl.BlockSpec(block, y_at)] + [
        fixed(s.shape) for s in out_shape[4:-1]
    ]
    out_specs.append(pl.BlockSpec((shards, rows, LANES), lambda i: (0, 0, jnp.clip(i - 5 - n_mix, 0, n_out - 1))))
    n = shards - 1
    return pl.pallas_call(
        functools.partial(forward_kernel, rep=rep, shards=shards, blocks=blocks, n_out=n_out),
        grid=(steps,),
        in_specs=[
            const((rows, width)), const((rows, width)), const((1, rows)), anywhere, anywhere, *(const(v.shape) for v in singles),
        ],
        out_specs=out_specs,
        out_shape=out_shape,
        scratch_shapes=[
            vm((shards, rows, depth), BF), vm(pack, F32), vm(pack, BF), vm((shards, *pack), BF), vm((2, shards, 4 * LANES, depth), BF),
            vm((2, shards, LANES, width), BF), vm(block, F32), vm(block, F32), vm((rows, rows), F32), vm((rows, 2 * LANES), BF),
            vm((rows, 3 * LANES), BF), vm((inner // LANES, rows, LANES), F32), vm((rows, LANES), F32),
            vm((rows, inner), BF), vm((rows, width), F32),
            dma(8, n), dma(8, n), dma(4, 2, n), dma(4, 2, n), dma(4, 2, n), dma(4, 2, n), dma(4, n), dma(4, n),
            dma(2, shards), dma(n), dma(n), dma(n), dma(n), dma(2),
        ],
        compiler_params=pltpu.CompilerParams(
            vmem_limit_bytes=VMEM_LIMIT, collective_id=1, has_side_effects=True
        ),
        name="mixer_forward",
    )(hidden, cotangent, seg_ids, wt, ow, *singles)


def chunk_at(j, blocks):
    return jnp.where(j < 2 * blocks, j // 2 + blocks * (j % 2), j)


def first_over_shards(c):
    return c % 3 == 1


def stage_steps(bits):
    more = list(range(1, bits - 1))
    n = len(more)
    rep_first = [0, 1, 2, 4, 6] + [6 + i for i in more] + [8 + n, 9 + n, 11 + n, 12 + n]
    shard_first = [0, 1, 3, 5, 7] + [7 + i for i in more] + [8 + n, 9 + n, 10 + n, 12 + n]
    return rep_first, shard_first


def reduce_kernel(*refs, rep, shards, q, blocks, n_out, n_in, tail):
    (
        z_ref, x_ref, y_ref, dgn_ref, bc_ref, dtraw_ref, r_ref, rd_ref, b_ref, c_ref, cbt_ref, dt_ref, cum_ref,
        cumt_ref, mask_ref, seg_col, seg_row, par_ref, w_ref, low_t, cot_ref, normed_t, hidden_ref,
        gin_out, gout_out, gh_out, norm_out,
        dt2, cum3, g_scr, dcum, ddt, dp, dn, gh_buf, inv, dots, ag, agt, small, small_rows, slots_norm,
        s5, r5, s6, r6, l7, s7, r7, xtra, sx, rx, sn, rn, sgh,
    ) = refs[:55]
    levels = refs[55:]
    bits = shards.bit_length() - 1
    last = 3 + bits
    keep, send, land, ssem, rsem = (dict(zip(range(1, last + 1), levels[i::5])) for i in range(5))

    step = pl.program_id(0)
    place = Place(rep, shards)
    rows = z_ref.shape[0]
    tile = z_ref.shape[1]
    mix_steps = dp.shape[2] * blocks // tile * 2
    chunks = n_out + n_in
    a, b, core, me, quarter = place.a, place.b, place.core, place.me, place.quarter

    norm = SmallSum(place, norm_out, slots_norm, sn, rn)

    @pl.when(step == 0)
    def _():
        place.greet()
        norm_out[...] = jnp.zeros_like(norm_out)
        small[6:7, :LANES] = jnp.zeros((1, LANES), F32)
        dn[...] = jnp.zeros_like(dn)
        hi, lo = pieces(dt_ref[...], 2)
        dt2[:, :LANES] = hi
        dt2[:, LANES:] = lo
        for i, part in enumerate(pieces(cum_ref[...], 3)):
            cum3[:, i * LANES : (i + 1) * LANES] = part
        g_scr[...] = jnp.zeros_like(g_scr)
        dcum[...] = jnp.zeros_like(dcum)
        ddt[...] = jnp.zeros_like(ddt)

    def halving(shard_first, level):
        at = level - 2
        if shard_first != (at >= 2):
            j = at if shard_first else at - 2
            if j < bits:
                bit, peer = place.shard_bit(j)
                return [(shards >> (j + 1), 4 * q if shard_first else q, bit, peer)] * 2
        n = 1 if shard_first else shards
        turn = at - bits if shard_first else at
        by_a, by_b = (a, place.a_peer), (b, place.b_peer)
        if turn == 0:
            return [(n, 2 * q, *by_a), (2 * n, q, *by_b)]
        return [(n, q, *by_b), (n, q, *by_a)]

    def copies(shard_first, level, c):
        k, w = c % keep[level].shape[0], c % land[level].shape[0]
        peers = [place.core_peer] * 2 if level == 1 else [part[3] for part in halving(shard_first, level)]
        return [
            remote(
                send[level].at[k, o], land[level].at[w, o], ssem[level].at[k, o], rsem[level].at[w, o], peers[o]
            )
            for o in range(2)
        ]

    def start(group):
        for copy in group:
            copy.start()

    def finish(group):
        for copy in group:
            copy.wait()

    def block(g, quarter):
        return ag.at[g, :, pl.ds(pl.multiple_of(quarter * q, q), q)]

    def half_block(g, o, quarter):
        return ag.at[g, o, pl.ds(pl.multiple_of(quarter * q, q), q)]

    def copy5(g):
        mine = block(g, quarter)
        return [
            remote(mine, mine, s5.at[g, i], r5.at[g, i], peer) for i, peer in enumerate((place.a_peer, place.b_peer))
        ]

    def copy6(g):
        from_a = half_block(g, 0, 2 * (1 - a) + b)
        from_b = half_block(g, 1, 2 * a + 1 - b)
        return [
            remote(from_a, from_a, s6.at[g, 0], r6.at[g, 0], place.b_peer),
            remote(from_b, from_b, s6.at[g, 1], r6.at[g, 1], place.a_peer),
        ]

    def targets(c, is_out):
        if is_out:
            cols = pl.ds(pl.multiple_of(c * 2 * LANES + core * LANES, LANES), LANES)
            return [gout_out.at[pl.ds(o * 4 * q, 4 * q), cols] for o in range(2)]
        base = chunk_at(c - n_out, blocks) * 4 * LANES + core * 2 * LANES
        return [gin_out.at[pl.ds(pl.multiple_of(base + o * LANES, LANES), LANES)] for o in range(2)]

    def copy7(c, is_out):
        g, t = c % ag.shape[0], c % agt.shape[0]
        ends = targets(c, is_out)
        own = [ag.at[g, o] if is_out else agt.at[t, o] for o in range(2)]
        local = [pltpu.make_async_copy(own[o], ends[o], l7.at[g, o]) for o in range(2)]
        return local + [remote(own[o], ends[o], s7.at[g, o], r7.at[g, o], place.core_peer) for o in range(2)]

    def by_target(c, run):
        for is_out in (True, False):

            @pl.when((c < n_out) == is_out)
            def _(is_out=is_out):
                run(is_out)

    def stage_first(c):
        @pl.when(c < n_out)
        def _():
            base = c * 2 * LANES
            for s in range(shards):
                lhs = low_t[s * 8 * q : (s + 1) * 8 * q, :]
                for side, ref in ((core, keep[1]), (1 - core, send[1])):
                    cols = pl.ds(pl.multiple_of(base + side * LANES, LANES), LANES)
                    grad = mm(lhs, cot_ref[:, cols])
                    for o in range(2):
                        ref[0, o, s * 4 * q : (s + 1) * 4 * q] = grad[o * 4 * q : (o + 1) * 4 * q].astype(ref.dtype)

        @pl.when(c >= n_out)
        def _():
            n = chunk_at(c - n_out, blocks)
            for s in range(shards):
                own = slice(s * 4 * q, (s + 1) * 4 * q)
                for side, ref in ((core, keep[1]), (1 - core, send[1])):
                    cols = pl.ds(pl.multiple_of(side * 2 * LANES, 2 * LANES), 2 * LANES)
                    grad = mm(normed_t[own, :], dp[n, :, cols])
                    for o in range(2):
                        ref[0, o, own] = grad[:, o * LANES : (o + 1) * LANES].astype(ref.dtype)

        for side, ref in ((1, keep[1]), (0, send[1])):

            @pl.when((c == chunks - 1) & (core == side))
            def _(ref=ref):
                for s in range(shards):
                    at = s * 4 * q
                    ref[0, 1, at : at + small_rows.shape[1]] = small_rows[s].astype(ref.dtype)

        start(copies(False, 1, c))

    def stage_halve(shard_first, level, c):
        finish(copies(shard_first, level - 1, c))
        k0, w0 = c % keep[level - 1].shape[0], c % land[level - 1].shape[0]
        k = c % keep[level].shape[0]
        for o, (runs, size, bit, _) in enumerate(halving(shard_first, level)):

            def part(u, carry, o=o, size=size, bit=bit):
                own = pl.ds(pl.multiple_of((2 * u + bit) * size, size), size)
                other = pl.ds(pl.multiple_of((2 * u + 1 - bit) * size, size), size)
                end = pl.ds(pl.multiple_of(u * size, size), size)
                keep[level][k, o, end] = keep[level - 1][k0, o, own] + land[level - 1][w0, o, own].astype(F32)
                send[level][k, o, end] = (
                    keep[level - 1][k0, o, other] + land[level - 1][w0, o, other].astype(F32)
                ).astype(BF)
                return carry

            if runs == 1:
                part(0, 0)
            else:
                lax.fori_loop(0, runs, part, 0)
        start(copies(shard_first, level, c))

    def stage_total(shard_first, c):
        finish(copies(shard_first, last, c))
        k, w, g = c % keep[last].shape[0], c % land[last].shape[0], c % ag.shape[0]
        total = keep[last][k] + land[last][w].astype(F32)
        for i, peer in enumerate(place.extra):
            keep[last][k] = total
            copy = remote(keep[last].at[k], xtra.at[c % 2, i], sx.at[c % 2, i], rx.at[c % 2, i], peer)
            copy.start()
            copy.wait()
            total = total + xtra[c % 2, i]
        for o in range(2):
            ag[g, o, pl.ds(pl.multiple_of(quarter * q, q), q)] = total[o].astype(BF)
        start(copy5(g))

    def stage_forward(c):
        g = c % ag.shape[0]
        for copy in copy5(g):
            copy.wait_recv()
        start(copy6(g))

    def stage_out(c):
        g, t = c % ag.shape[0], c % agt.shape[0]
        for copy in copy6(g):
            copy.wait_recv()

        def run(is_out):
            if not is_out:
                for o in range(2):
                    agt[t, o] = ag[g, o].astype(F32).T.astype(BF)
            start(copy7(c, is_out))

        by_target(c, run)

    def stage_end(c):
        by_target(c, lambda is_out: finish(copy7(c, is_out)))
        g = c % ag.shape[0]
        for copy in copy5(g) + copy6(g):
            copy.wait_send()

    plans = stage_steps(bits)

    def run_stage(number):
        for shard_first in (False, True):
            c = step - plans[shard_first][number - 1]

            @pl.when((c >= 0) & (c < chunks) & (first_over_shards(c) == shard_first))
            def _(c=c, shard_first=shard_first):
                if number == 1:
                    stage_first(c)
                elif number <= last:
                    stage_halve(shard_first, number, c)
                elif number == last + 1:
                    stage_total(shard_first, c)
                else:
                    (stage_forward, stage_out, stage_end)[number - last - 2](c)

    order = [5, 6, 8, 9, 7, 2, 4, 1, 3]
    for number in order + list(range(10, last + 5)):
        run_stage(number)

    masks = lambda: [mask_ref[k - 1] for k in range(1, CONV)]

    def pairs(first, count):
        def one(p, carry):
            pair = step // 2 * (tile // LANES) + p
            cols = pl.ds(pl.multiple_of(p * LANES, LANES), LANES)
            at = pl.ds(pl.multiple_of(pair * LANES, LANES), LANES)
            skip = skip_lanes(par_ref[ROW_SKIP : ROW_SKIP + 1, :LANES], head_of_lane(pair))
            res = backward_pair(
                pair, z_ref[:, cols], x_ref[:, cols], y_ref[:, cols], dgn_ref[0, :, cols], r_ref[...], rd_ref[...],
                par_ref[:CONV, at], par_ref[ROW_BIAS : ROW_BIAS + 1, at], skip, par_ref[ROW_GAIN : ROW_GAIN + 1, at],
                masks(), dt2, cum3, cumt_ref, cbt_ref, g_scr, dcum, ddt,
            )
            end = pl.ds(pl.multiple_of(pair % 4 * LANES, LANES), LANES)
            dp[pair // 4, :, end] = res[0]
            dp[blocks + pair // 4, :, end] = res[1]
            for k in range(CONV):
                small[k : k + 1, at] = res[4][k]
            small[4:5, at] = res[5]
            small[5:6, at] = res[2]
            per_head = jnp.concatenate(pieces(jnp.broadcast_to(res[3], (8, LANES)), 3), axis=1)
            small[6:7, :LANES] += mm_t(per_head, jnp.concatenate([head_of_lane(pair)] * 3, axis=1))[0:1]
            return carry

        lax.fori_loop(first, first + count, one, 0)

    @pl.when((step < mix_steps) & (step % 2 == 0))
    def _():
        pairs(0, 1)

    @pl.when((step < mix_steps) & (step % 2 == 1))
    def _():
        pairs(1, tile // LANES - 1)

    @pl.when(step == mix_steps - 1)
    def _():
        end = slice(INNER, INNER + 2 * LANES)
        d_bc, d_raw, d_weight, d_bias, d_alog, d_dtb = backward_tail(
            bc_ref, dtraw_ref, b_ref, c_ref, dt_ref, masks(), seg_col, seg_row, par_ref[:CONV, end],
            par_ref[ROW_BIAS : ROW_BIAS + 1, end], par_ref[ROW_ALOG : ROW_ALOG + 1, :LANES],
            par_ref[ROW_DTB : ROW_DTB + 1, :LANES], g_scr, dcum, ddt,
        )
        for i in range(2):
            cols = slice(i * LANES, (i + 1) * LANES)
            dp[2 * blocks, :, cols] = d_bc[i].astype(BF)
            end = slice(INNER + i * LANES, INNER + (i + 1) * LANES)
            for k in range(CONV):
                small[k : k + 1, end] = d_weight[i][k]
            small[4:5, end] = d_bias[i]
        dp[2 * blocks, :, 2 * LANES : 3 * LANES] = d_raw.astype(BF)
        dp[2 * blocks, :, 3 * LANES :] = jnp.zeros((rows, LANES), BF)
        small[5:6, INNER : INNER + LANES] = d_alog
        small[5:6, INNER + LANES :] = d_dtb
        for s in range(shards):
            for at, (row, lane) in enumerate(small_tiles(s, shards)):
                small_rows[s, at : at + 1, :] = small[row : row + 1, lane : lane + LANES]

    @pl.when((step >= n_out) & (step < chunks - 1))
    def _():
        grad = dp[chunk_at(step - n_out, blocks)]
        for s in range(shards):
            dn[s] += mm(grad, w_ref[s])

    @pl.when(step == chunks - 1)
    def _():
        grad = dp[n_in - 1]
        keep_rows = iota(w_ref.shape[1:], 0) < tail
        for s in range(shards):
            dn[s] += mm(grad, jnp.where(keep_rows, w_ref[s], 0))

    wide_cols = gh_buf.shape[2]
    together = wide_cols // dn.shape[2]
    n_parts = shards // together

    def norm_part(i):
        cols = slice(i * wide_cols, (i + 1) * wide_cols)
        d_normed = jnp.concatenate([dn[s] for s in range(i * together, (i + 1) * together)], axis=1)
        unit = hidden_ref[:, cols].astype(F32) * inv[:, :1]
        return cols, d_normed, unit, d_normed * par_ref[ROW_NORM : ROW_NORM + 1, cols]

    def first_pass(i):
        cols, d_normed, unit, du = norm_part(i)
        grad_norm = jnp.sum(d_normed * unit, axis=0, keepdims=True)
        for j in range(wide_cols // LANES):
            at = i * (wide_cols // LANES) + j
            norm_out[at : at + 1, :] = grad_norm[:, j * LANES : (j + 1) * LANES]
        dots[...] += jnp.sum(du * unit, axis=1, keepdims=True) * (1.0 / hidden_ref.shape[1])

    def gh_copy(i):
        return pltpu.make_async_copy(
            gh_buf.at[i % 2], gh_out.at[:, i * wide_cols : (i + 1) * wide_cols], sgh.at[i % 2]
        )

    def second_pass(i):
        if i >= 2:
            gh_copy(i - 2).wait()
        cols, _, unit, du = norm_part(i)
        gh_buf[i % 2] = cot_ref[:, cols].astype(F32) + inv[:, :1] * (du - unit * dots[:, :1])
        gh_copy(i).start()

    @pl.when(step == chunks)
    def _():
        hid = hidden_ref[...].astype(F32)
        scale = lax.rsqrt(jnp.mean(hid * hid, axis=1, keepdims=True) + EPS)
        inv[...] = jnp.broadcast_to(scale, inv.shape)
        dots[...] = jnp.zeros_like(dots)
        first_pass(0)

    for i in range(1, n_parts):

        @pl.when(step == chunks + (i + 1) // 2)
        def _(i=i):
            first_pass(i)

    norm_from = chunks + n_parts // 2

    for i in range(n_parts):

        @pl.when(step == norm_from + 1 + i)
        def _(i=i):
            second_pass(i)

    @pl.when(step == norm_from + 1 + n_parts)
    def _():
        for i in range(max(0, n_parts - 2), n_parts):
            gh_copy(i).wait()

    for i in range(norm.stages):

        @pl.when(step == norm_from + i)
        def _(i=i):
            norm.stage(i)


def results_kernel(
    gin_ref, gout_ref, gh_ref, mixed_ref, norm_ref,
    gin_out, gout_out, gh_out, mixed_out, ngain_out, gain_out, cw_out, cb_out, alog_out, skip_out, dtb_out, *, shards
):
    step = pl.program_id(0)
    me = lax.axis_index("shard")
    gin_out[...] = gin_ref[...].astype(F32)
    gout_out[...] = gout_ref[...].astype(F32)
    gh_out[...] = gh_ref[...]
    mixed_out[...] = mixed_ref[...]

    @pl.when(step == pl.num_programs(0) - 1)
    def _():
        conv, gain, heads, ngain = cb_out.shape[0], gain_out.shape[0], alog_out.shape[0], ngain_out.shape[0]
        rows = gin_ref.shape[0]
        small = gin_ref[rows - LANES :, :].astype(F32).T
        norm = jnp.concatenate([norm_ref[i : i + 1, :] for i in range(norm_ref.shape[0])], axis=1)
        for s in range(shards):

            @pl.when(me == s)
            def _(s=s):
                tiles = small_tiles(s, shards)

                def part(row, base, size):
                    at = [i for i, (r, lane) in enumerate(tiles) if r == row and base <= lane < base + max(size, LANES) * shards]
                    flat = jnp.concatenate([small[i : i + 1, :] for i in at], axis=1)
                    first = s * size - (tiles[at[0]][1] - base)
                    return flat[:, first : first + size]

                for k in range(CONV):
                    cw_out[k : k + 1, :] = part(k, 0, conv)
                cb_out[...] = part(CONV, 0, conv).reshape(conv)
                gain_out[...] = part(5, 0, gain).reshape(gain)
                for ref, row, base in ((alog_out, 5, INNER), (dtb_out, 5, INNER + LANES), (skip_out, 6, 0)):
                    i = tiles.index((row, base))
                    ref[...] = small[i : i + 1, s * heads : (s + 1) * heads].reshape(heads)
                ngain_out[...] = norm[:, s * ngain : (s + 1) * ngain].reshape(ngain)


def results(g_in, g_out, grad_hidden, mixed, norm, columns, singles, shards):
    conv_w, conv_b, gain, ngain, a_log = singles[:5]
    depth, width = g_in.shape[1], g_out.shape[1]
    steps = g_in.shape[0] // (4 * LANES)
    f = lambda *s: jax.ShapeDtypeStruct(s, F32)
    some = steps // 4 * 4
    strip = lambda v: pl.BlockSpec((v.shape[0] // some, v.shape[1]), lambda i: (jnp.minimum(i, some - 1), 0))
    eighth = lambda v: pl.BlockSpec((v.shape[0] // 8, v.shape[1]), lambda i: (jnp.minimum(i, 7), 0))
    block = pl.BlockSpec((4 * LANES, depth), lambda i: (i, 0))
    whole = lambda s: pl.BlockSpec(s, lambda i: (0,) * len(s))
    small = [ngain.shape, gain.shape, conv_w.shape, conv_b.shape, a_log.shape, a_log.shape, a_log.shape]
    return pl.pallas_call(
        functools.partial(results_kernel, shards=shards),
        grid=(steps,),
        in_specs=[block, strip(g_out), eighth(grad_hidden), eighth(mixed), whole(norm.shape)],
        out_specs=[block, strip(g_out), eighth(grad_hidden), eighth(mixed), *(whole(s) for s in small)],
        out_shape=[
            f(columns, depth), f(*g_out.shape), f(*grad_hidden.shape), jax.ShapeDtypeStruct(mixed.shape, BF),
            *(f(*s) for s in small),
        ],
        name="results",
    )(g_in, g_out, grad_hidden, mixed, norm)


def mixer_backward_and_sums(saved, hidden, cotangent, seg_ids, rep, shards):
    (w3, ow3, proj, y, low_t, r, b, c, cbt, dt, cum, cumt, mask, normed_t, params, _, rd, seg_col, d_gated) = saved
    rows, width = hidden.shape
    inner = low_t.shape[0]
    depth = width // shards
    wide_block = 4 * LANES
    blocks = inner // wide_block
    n_out = width // (2 * LANES)
    n_in = proj.shape[1] // wide_block
    q = depth // 4
    chunks = n_out + n_in
    bits = shards.bit_length() - 1
    steps = chunks + stage_steps(bits)[0][-1]
    n_small = SmallSum.count(rep, shards)
    n_extra = max(1, n_small - 3 - (shards - 1))
    tile = 3 * LANES
    tiles = inner // tile
    mix = lambda offset: pl.BlockSpec((rows, tile), lambda i: (0, offset + jnp.minimum(i // 2, tiles - 1)))
    a_shard = inner // shards // tile

    def d_gated_at(i):
        at = jnp.minimum(i // 2, tiles - 1)
        return at // a_shard, 0, at % a_shard

    const = lambda shape, at=None: pl.BlockSpec(shape, lambda i: at or (0,) * len(shape), pipeline_mode=pl.Buffered(1))
    f = lambda *s: jax.ShapeDtypeStruct(s, F32)
    h = lambda *s: jax.ShapeDtypeStruct(s, BF)
    vm = pltpu.VMEM
    dma = lambda *s: pltpu.SemaphoreType.DMA(s)
    anywhere = pl.BlockSpec(memory_space=pl.ANY)
    pairs_bc = inner // LANES
    in_specs = [
        mix(0), mix(tiles), mix(0),
        pl.BlockSpec((1, rows, tile), d_gated_at),
        const((rows, 2 * LANES), (0, pairs_bc)), const((rows, LANES), (0, 2 * pairs_bc + 2)),
        const((rows, LANES)), const((rows, LANES)), const((rows, LANES)), const((rows, LANES)),
        const((rows, rows)), const((rows, LANES)), const((rows, LANES)), const((LANES, rows)),
        const((CONV - 1, rows, LANES)), const((rows, LANES)), const((1, rows)), const(params.shape),
        pl.BlockSpec(
            (shards, wide_block, depth), lambda i: (0, chunk_at(jnp.clip(i - n_out, 0, n_in - 1), blocks), 0)
        ),
        const((inner, rows)), const((rows, width)), const((width, rows)), const((rows, width)),
    ]
    whole_out = lambda shape: pl.BlockSpec(shape, lambda i: (0,) * len(shape))
    norm_shape = (16, LANES)
    small_height = -(-max(len(small_tiles(s, shards)) for s in range(shards)) // 16) * 16
    scratch = [
        vm((rows, 2 * LANES), BF), vm((rows, 3 * LANES), BF), vm((rows, rows), F32), vm((rows, LANES), F32),
        vm((rows, LANES), F32), vm((n_in, rows, wide_block), BF), vm((shards, rows, depth), F32), vm((2, rows, tile), F32), vm((rows, LANES), F32), vm((rows, LANES), F32),
        vm((8, 2, 4 * q, LANES), BF), vm((4, 2, LANES, 4 * q), BF),
        vm((8, CONV_CH), F32), vm((shards, small_height, LANES), F32), vm((n_small, *norm_shape), F32),
        dma(8, 2), dma(8, 2), dma(8, 2), dma(8, 2), dma(8, 2), dma(8, 2), dma(8, 2),
        vm((2, n_extra, 2, q, LANES), F32), dma(2, n_extra), dma(2, n_extra),
        dma(n_small), dma(n_small), dma(2),
    ]
    for level in range(1, 4 + bits):
        own, landing = {1: (1, 2), 2: (3, 8)}.get(level, (4, 8))
        shape = (2, (shards * 4 * q) >> (level - 1), LANES)
        scratch += [
            vm((own, *shape), F32), vm((own, *shape), BF), vm((landing, *shape), BF), dma(own, 2), dma(landing, 2),
        ]
    return pl.pallas_call(
        functools.partial(
            reduce_kernel, rep=rep, shards=shards, q=q, blocks=blocks, n_out=n_out, n_in=n_in,
            tail=w3.shape[1] - (n_in - 1) * wide_block,
        ),
        grid=(steps,),
        in_specs=in_specs,
        out_specs=[anywhere, anywhere, anywhere, whole_out(norm_shape)],
        out_shape=[
            h(n_in * wide_block, depth), h(inner // shards, width), f(rows, width), f(*norm_shape),
        ],
        scratch_shapes=scratch,
        compiler_params=pltpu.CompilerParams(
            vmem_limit_bytes=VMEM_LIMIT, collective_id=2, has_side_effects=True
        ),
        name="mixer_backward_and_sums",
    )(
        proj, proj, y, d_gated, proj, proj, r, rd, b, c, cbt, dt, cum, cumt, mask, seg_col, seg_ids,
        params, w3, low_t, cotangent, normed_t, hidden,
    )


def per_device(
    hidden, seg_ids, cotangent, in_weight, out_weight, norm_gain, gated_gain, conv_weight, conv_bias, a_log, d_skip,
    dt_bias,
):
    rep, shards = lax.axis_size("rep"), lax.axis_size("shard")
    singles = (conv_weight, conv_bias, gated_gain, norm_gain, a_log, d_skip, dt_bias)
    wt = in_weight.T
    saved = mixer_forward(hidden, cotangent, seg_ids, wt, out_weight, singles, rep, shards)
    mixed = saved[15]
    g_in, g_out, grad_hidden, norm = mixer_backward_and_sums(saved, hidden, cotangent, seg_ids, rep, shards)
    g_in, g_out, grad_hidden, mixed, *small = results(
        g_in, g_out, grad_hidden, mixed, norm, wt.shape[0], singles, shards
    )
    return (mixed, grad_hidden, g_in.T, g_out, *small)


def solution(mesh):
    both = ("rep", "shard")
    shard = P("shard")
    placed = (P(both, None), P(both, None), P(both, None), P("shard", None), P("shard", None), shard, shard,
              P(None, "shard"), shard, shard, shard, shard)
    outs = (P(both, None), P(both, None), P("shard", None), P("shard", None), shard, shard, P(None, "shard"), shard,
            shard, shard, shard)
    return jax.shard_map(per_device, mesh=mesh, in_specs=placed, out_specs=outs, check_vma=False)
```

```python
import functools
import jax
import jax.numpy as jnp
from jax import lax
from jax.experimental import pallas as pl
from jax.experimental.pallas import tpu as pltpu
from jax.sharding import PartitionSpec as P

HEADS = 48
HEAD_DIM = 64
STATE = 128
CONV = 4
INNER = 3072
CONV_CH = 3328
LANES = 128
EPS = 1e-05
LOG2E = 1.4426950408889634
BF = jnp.bfloat16
F32 = jnp.float32
HIGH = lax.Precision.HIGHEST
VMEM_LIMIT = 63 * 2**20
MESH = pl.DeviceIdType.MESH


def mm(a, b):
    return jnp.dot(a, b, preferred_element_type=F32)


def mm_t(a, b):
    return lax.dot_general(a, b, (((1,), (1,)), ((), ())), preferred_element_type=F32)


def pieces(value, count):
    parts = []
    for _ in range(count):
        part = value.astype(BF)
        parts.append(part)
        value = value - part.astype(F32)
    return parts


def iota(shape, dim):
    return lax.broadcasted_iota(jnp.int32, shape, dim)


def head_of_lane(pair):
    heads, lanes = iota((LANES, LANES), 0), iota((LANES, LANES), 1)
    return (heads == 2 * pair + lanes // HEAD_DIM).astype(BF)


def head_columns(cum3, pair):
    heads, lanes = iota((LANES, 2 * LANES), 0), iota((LANES, 2 * LANES), 1)
    pick = (heads == 2 * pair + lanes // LANES).astype(BF)
    cols = mm(cum3[...], jnp.concatenate([pick] * 3, axis=0))
    return cols[:, :LANES], cols[:, LANES:]


def conv_shifts(value, masks):
    return [pltpu.roll(value, k, 0) * masks[k - 1] for k in range(1, CONV)]


def conv_apply(value, shifts, weight, bias):
    total = bias + weight[CONV - 1 : CONV] * value
    for k in range(1, CONV):
        total = total + weight[CONV - 1 - k : CONV - k] * shifts[k - 1]
    return total


def conv_back(d_pre, value, shifts, masks, weight):
    rows = d_pre.shape[0]
    d_value = weight[CONV - 1 : CONV] * d_pre
    d_weight = [jnp.sum(d_pre * value, axis=0, keepdims=True)]
    for k in range(1, CONV):
        d_weight.append(jnp.sum(d_pre * shifts[k - 1], axis=0, keepdims=True))
        d_value = d_value + weight[CONV - 1 - k : CONV - k] * pltpu.roll(
            d_pre * masks[k - 1], rows - k, 0
        )
    d_bias = jnp.sum(d_pre, axis=0, keepdims=True)
    return d_value, d_weight[::-1], d_bias


def silu_parts(value):
    sig = 0.5 * jnp.tanh(0.5 * value) + 0.5
    return sig, value * sig


def silu_slope(sig, silu):
    return sig + silu - silu * sig


def decay(col, row, clamp):
    gap = col - row
    return jnp.exp2(jnp.minimum(gap, 0.0) if clamp else gap)


def wide(col, width):
    return jnp.concatenate([col] * (width // LANES), axis=1)


def backward_pair(
    pair, z, value, y, dgn, r, rd, cw, cb, skip, gain, masks, dt2, cum3, cumt_ref, cbt_ref, g_scr, dcum, ddt
):
    rows = z.shape[0]
    half = rows // 2
    shifts = conv_shifts(value, masks)
    pre = conv_apply(value, shifts, cw, cb)
    sp, x = silu_parts(pre)
    sg, sz = silu_parts(z)
    scanned = y + skip * x
    g = scanned * sz
    dgn_r = dgn * r
    d_gain = jnp.sum(dgn_r * g, axis=0, keepdims=True)
    dg = gain * dgn_r - g * rd
    dz = (dg * scanned * silu_slope(sg, sz)).astype(BF)
    dsc = dg * sz
    d_skip = jnp.sum(dsc * x, axis=0, keepdims=True)
    dy = dsc.astype(BF)
    spread = head_of_lane(pair)
    step = mm(dt2[...], jnp.concatenate([spread, spread], axis=0))
    both = jnp.concatenate([spread, spread], axis=1)
    xt = (x * step).astype(BF)
    first = iota((rows, LANES), 1) < HEAD_DIM
    zero = jnp.zeros_like(xt)
    columns = head_columns(cum3, pair)
    blocks = (
        (slice(0, half), slice(0, half), True),
        (slice(0, half), slice(half, rows), False),
        (slice(half, rows), slice(half, rows), True),
    )
    rows_of = [cumt_ref[pl.ds(2 * pair + side, 1), :] for side in range(2)]
    sides = [jnp.where(first == (side == 0), xt, zero) for side in range(2)]
    parts = [[], []]
    for js, is_, clamp in blocks:
        total = g_scr[js, is_]
        for side in range(2):
            e = decay(rows_of[side][:, is_], wide(columns[side][js], half), clamp)
            parts[side].append(mm((e * cbt_ref[js, is_]).astype(BF), dy[is_]))
            total = total + e * mm_t(sides[side][js], dy[is_])
        g_scr[js, is_] = total
    dxts = [jnp.concatenate([p[0] + p[1], p[2]], axis=0) for p in parts]
    dxt = jnp.where(first, dxts[0], dxts[1])
    for ref, term in ((dcum, dy.astype(F32) * y - xt.astype(F32) * dxt), (ddt, x * dxt)):
        ref[...] += mm_t(jnp.concatenate(pieces(term, 2), axis=1), both)
    dx = skip * dsc + step * dxt
    d_pre = dx * silu_slope(sp, x)
    d_value, d_weight, d_bias = conv_back(d_pre, value, shifts, masks, cw)
    return dz, d_value.astype(BF), d_gain, d_skip, d_weight, d_bias


def backward_tail(
    bc_ref, dtraw_ref, b_ref, c_ref, dt_ref, masks, seg_col, seg_row, cw_bc, cb_bc, alog_ref, bias_ref,
    g_scr, dcum, ddt
):
    rows = dt_ref.shape[0]
    same = wide(seg_col[...], rows) == seg_row[...]
    later = (iota((rows, rows), 0) <= iota((rows, rows), 1)) & same
    gt = jnp.where(later, g_scr[...], 0.0)
    db = jnp.dot(gt, c_ref[...], precision=HIGH, preferred_element_type=F32)
    dc = jnp.dot(gt.T, b_ref[...], precision=HIGH, preferred_element_type=F32)
    d_bc, d_weights, d_biases = [], [], []
    for i, d_out in enumerate((db, dc)):
        cols = slice(i * LANES, (i + 1) * LANES)
        value = bc_ref[:, cols]
        shifts = conv_shifts(value, masks)
        pre = conv_apply(value, shifts, cw_bc[:, cols], cb_bc[:, cols])
        sp, value_out = silu_parts(pre)
        d_pre = d_out * silu_slope(sp, value_out)
        d_value, d_weight, d_bias = conv_back(d_pre, value, shifts, masks, cw_bc[:, cols])
        d_bc.append(d_value)
        d_weights.append(d_weight)
        d_biases.append(d_bias)
    step = dt_ref[...]
    live = iota((rows, LANES), 1) < HEADS
    rate = -jnp.exp(alog_ref)
    later_bf = later.astype(BF)
    dlog = sum(mm(later_bf, part) for part in pieces(dcum[...], 3)[::-1])
    dstep = ddt[...] + dlog * rate
    raw = jnp.where(live, dtraw_ref[...] + bias_ref, 0.0)
    d_raw = jnp.where(live, dstep / (1.0 + jnp.exp(-raw)), 0.0)
    d_alog = jnp.sum(dlog * step, axis=0, keepdims=True) * rate
    return d_bc, d_raw, d_weights, d_biases, d_alog, jnp.sum(d_raw, axis=0, keepdims=True)


class Place:
    def __init__(self, rep, shards):
        self.rep, self.shards = rep, shards
        r, self.me = lax.axis_index("rep"), lax.axis_index("shard")
        self.r = r
        self.core, self.a, self.b = r % 2, (r // 2) % 2, (r // 4) % 2
        self.core_peer = (r + 1 - 2 * self.core, self.me)
        self.a_peer = (r + 2 - 4 * self.a, self.me)
        self.b_peer = (r + 4 - 8 * self.b, self.me)
        self.extra = []
        stride = 8
        while stride < rep:
            bit = (r // stride) % 2
            self.extra.append((r + stride - 2 * stride * bit, self.me))
            stride *= 2
        self.quarter = 2 * self.a + self.b

    def shard_bit(self, j):
        bit = (self.me // (1 << j)) % 2
        return bit, (self.r, self.me + (1 << j) - (2 << j) * bit)

    def shard_peer(self, distance):
        return (self.r, (self.me + distance) % self.shards)

    def partners(self):
        return [self.core_peer, self.a_peer, self.b_peer, *self.extra] + [
            self.shard_peer(d) for d in range(1, self.shards)
        ]

    def greet(self):
        barrier = pltpu.get_barrier_semaphore()
        partners = self.partners()
        for partner in partners:
            pl.semaphore_signal(barrier, inc=1, device_id=partner, device_id_type=MESH)
        pl.semaphore_wait(barrier, len(partners))


def remote(src, dst, send, recv, device):
    return pltpu.make_async_remote_copy(
        src_ref=src, dst_ref=dst, send_sem=send, recv_sem=recv, device_id=device, device_id_type=MESH
    )


class SmallSum:
    def __init__(self, place, buf, slots, sends, recvs):
        self.buf, self.slots, self.sends, self.recvs = buf, slots, sends, recvs
        pairs = [place.core_peer, place.a_peer, place.b_peer, *place.extra]
        self.groups = [[peer] for peer in pairs] + [[place.shard_peer(d) for d in range(1, place.shards)]]
        self.stages = len(self.groups) + 1

    @staticmethod
    def count(rep, shards):
        return rep.bit_length() - 1 + shards - 1

    def copies(self, group):
        at = sum(len(g) for g in self.groups[:group])
        return [
            remote(self.buf, self.slots.at[at + i], self.sends.at[at + i], self.recvs.at[at + i], peer)
            for i, peer in enumerate(self.groups[group])
        ]

    def stage(self, number):
        if number > 0:
            at = sum(len(g) for g in self.groups[: number - 1])
            copies = self.copies(number - 1)
            for copy in copies:
                copy.wait()
            total = self.buf[...]
            for i in range(len(copies)):
                total = total + self.slots[at + i]
            self.buf[...] = total
        if number < len(self.groups):
            for copy in self.copies(number):
                copy.start()


def small_tiles(s, shards):
    def span(total):
        size = total // shards
        return range(s * size // LANES * LANES, (s + 1) * size, LANES)

    tiles = [(row, lane) for row in range(CONV + 1) for lane in span(CONV_CH)]
    tiles += [(5, lane) for lane in span(INNER)]
    return tiles + [(5, INNER), (5, INNER + LANES), (6, 0)]


def forward_setup(
    bc, raw, seg_col, seg_row, cw, cb, alog, bias, outs, cb_scr, dt2, cum3
):
    b_out, c_out, cbt_out, dt_out, cum_out, cumt_out, mask_out = outs
    rows = raw.shape[0]
    at = iota((rows, LANES), 0)
    for k in range(1, CONV):
        same = (pltpu.roll(seg_col, k, 0) == seg_col) & (at >= k)
        mask_out[k - 1] = same.astype(F32)
    masks = [mask_out[k - 1] for k in range(1, CONV)]
    results = []
    for i in range(2):
        cols = slice(i * LANES, (i + 1) * LANES)
        value = bc[:, cols]
        pre = conv_apply(value, conv_shifts(value, masks), cw[:, cols], cb[:, cols])
        results.append(silu_parts(pre)[1])
    b_out[...] = results[0]
    c_out[...] = results[1]
    products = lax.dot_general(
        results[1], results[0], (((1,), (1,)), ((), ())), precision=HIGH, preferred_element_type=F32
    )
    lower = iota((rows, rows), 0) >= iota((rows, rows), 1)
    allowed = lower & (wide(seg_col, rows) == seg_row)
    products = jnp.where(allowed, products, 0.0)
    cb_scr[...] = products
    cbt_out[...] = products.T
    live = iota((rows, LANES), 1) < HEADS
    raw = jnp.where(live, raw + bias, 0.0)
    step = jnp.where(live, jnp.maximum(raw, 0.0) + jnp.log(1.0 + jnp.exp(-jnp.abs(raw))), 0.0)
    dt_out[...] = step
    hi, lo = pieces(step, 2)
    dt2[:, :LANES] = hi
    dt2[:, LANES:] = lo
    log_rate = step * (-LOG2E * jnp.exp(alog))
    tri = lower.astype(BF)
    cum = sum(mm(tri, part) for part in pieces(log_rate, 3)[::-1])
    cum_out[...] = cum
    cumt_out[...] = cum.T
    for i, part in enumerate(pieces(cum, 3)):
        cum3[:, i * LANES : (i + 1) * LANES] = part


def skip_lanes(skip_row, spread):
    return mm(jnp.broadcast_to(skip_row, (8, LANES)).astype(BF), spread)[0:1]


def forward_pair(pair, z, value, cw, cb, skip_row, masks, dt2, cum3, cumt_ref, cb_scr):
    rows = z.shape[0]
    half = rows // 2
    pre = conv_apply(value, conv_shifts(value, masks), cw, cb)
    x = silu_parts(pre)[1]
    spread = head_of_lane(pair)
    step = mm(dt2[...], jnp.concatenate([spread, spread], axis=0))
    xt = (x * step).astype(BF)
    first = iota((rows, LANES), 1) < HEAD_DIM
    ys = []
    columns = head_columns(cum3, pair)
    for side in range(2):
        head = 2 * pair + side
        col = columns[side]
        row = cumt_ref[pl.ds(head, 1), :]
        low_row, high_row = row[:, :half], row[:, half:]
        top, bottom = wide(col[:half], half), wide(col[half:], half)
        m00 = (decay(top, low_row, True) * cb_scr[:half, :half]).astype(BF)
        m10 = (decay(bottom, low_row, False) * cb_scr[half:, :half]).astype(BF)
        m11 = (decay(bottom, high_row, True) * cb_scr[half:, half:]).astype(BF)
        ys.append(
            jnp.concatenate([mm(m00, xt[:half]), mm(m10, xt[:half]) + mm(m11, xt[half:])], axis=0)
        )
    y = jnp.where(first, ys[0], ys[1])
    g = (y + skip_lanes(skip_row, spread) * x) * silu_parts(z)[1]
    return y, g


ROW_BIAS, ROW_GAIN, ROW_NORM, ROW_ALOG, ROW_SKIP, ROW_DTB = 4, 5, 6, 7, 8, 9


def forward_kernel(
    hidden_ref, cot_ref, seg_row, wt_ref, ow_ref, cw_ref, cb_ref, gain_ref, ngain_ref, alog_ref, skip_ref, dtb_ref,
    w3, ow3, proj_out, y_out, lowt_out, r_out, b_out, c_out, cbt_out, dt_out, cum_out, cumt_out, mask_out,
    normt_out, small_out, mixed_out, rd_out, segc_out, dg_out,
    normed3, normt, lowt, pack32, pack_ref, pk, wbuf, owbuf, xbuf, zbuf, cb_scr, dt2, cum3, gated, ssq, low, acc,
    sz, rz, s2, r2, s3, r3, s4, r4, lw, st, rt, sp, rp, lc, se,
    *, rep, shards, blocks, n_out
):
    step = pl.program_id(0)
    place = Place(rep, shards)
    a, b, core, me, quarter = place.a, place.b, place.core, place.me, place.quarter
    rows, width = hidden_ref.shape
    depth = width // shards
    inner = blocks * 4 * LANES
    per = 4
    n_mix = 1 + 2 * blocks
    chunks = n_mix + n_out
    tail_at = 2 * inner + 2 * LANES
    tail = w3.shape[1] - tail_at
    total_rows = w3.shape[1]

    def rows_of(kind, c):
        if kind == "bc":
            return 2 * inner, 2 * LANES
        if kind == "in":
            j = (c - 1) // 2
            return ((c % 2) * inner + j * 4 * LANES), 4 * LANES
        return (c - n_mix) * LANES, LANES

    def view(kind, c, s, start, count, half=None):
        ref = ow3 if kind == "out" else w3
        base, _ = rows_of(kind, c)
        if half is not None and kind != "out":
            start, count = start + half * (count // 2), count // 2
        at = pl.ds(pl.multiple_of(base + start, 16), count)
        if half is not None and kind == "out":
            return ref.at[s, at, half * (width // 2) : (half + 1) * (width // 2)]
        return ref.at[s, at]

    def piece(kind, c, s, quarter, half=None):
        n = rows_of(kind, c)[1]
        return view(kind, c, s, core * (n // 2) + quarter * (n // 8), n // 8, half)

    def others():
        return [(d - 1, (me + d) % shards) for d in range(1, shards)]

    def copy1(kind, c):
        n = rows_of(kind, c)[1]
        base = rows_of(kind, c)[0]
        src = (ow_ref if kind == "out" else wt_ref).at[
            pl.ds(pl.multiple_of(base + core * (n // 2) + quarter * (n // 8), 16), n // 8)
        ]
        k = c % 8
        return [
            remote(src, piece(kind, c, me, quarter), sz.at[k, d - 1], rz.at[k, d - 1], place.shard_peer(d))
            for d in range(1, shards)
        ]

    def copy2(kind, c):
        k = c % 8
        return [
            remote(piece(kind, c, s, quarter), piece(kind, c, s, quarter), s2.at[k, i, d], r2.at[k, i, d], peer)
            for d, s in others()
            for i, peer in enumerate((place.a_peer, place.b_peer))
        ]

    def copy3(kind, c):
        k = c % 8
        from_a, from_b = 2 * (1 - a) + b, 2 * a + 1 - b
        return [
            remote(
                piece(kind, c, s, origin, i), piece(kind, c, s, origin, i), s3.at[k, i, d], r3.at[k, i, d], peer
            )
            for d, s in others()
            for i, (origin, peer) in enumerate(((from_a, place.b_peer), (from_b, place.a_peer)))
        ]

    def copy4(kind, c):
        k = c % 8
        n = rows_of(kind, c)[1]
        return [
            remote(
                view(kind, c, s, core * (n // 2), n // 2), view(kind, c, s, core * (n // 2), n // 2),
                s4.at[k, d], r4.at[k, d], place.core_peer,
            )
            for d, s in others()
        ]

    def load(kind, c, back=False):
        k = c % 2
        base, n = rows_of(kind, c)
        if kind == "bc":
            n = total_rows - base
        full, own, buf = (ow3, ow_ref, owbuf) if kind == "out" else (w3, wt_ref, wbuf)
        at = pl.ds(pl.multiple_of(base, LANES), n)
        mine = buf.at[k, me, pl.ds(0, n)]
        if back:
            return [pltpu.make_async_copy(mine, full.at[me, at], lc.at[k])]
        copies = [pltpu.make_async_copy(own.at[at], mine, lw.at[k, 0])]
        for d, s in others():
            copies.append(pltpu.make_async_copy(full.at[s, at], buf.at[k, s, pl.ds(0, n)], lw.at[k, 1 + d]))
        return copies

    def at_chunk(c, run):
        @pl.when(c == 0)
        def _():
            run("bc", 0)

        @pl.when((c >= 1) & (c < n_mix))
        def _():
            run("in", c)

        @pl.when((c >= n_mix) & (c < chunks))
        def _():
            run("out", c)

    def tails():
        return [
            remote(
                wt_ref.at[tail_at:total_rows], w3.at[me, tail_at:total_rows], st.at[d - 1], rt.at[d - 1],
                place.shard_peer(d),
            )
            for d in range(1, shards)
        ]

    def packs():
        return [
            remote(pack_ref, pk.at[me], sp.at[d - 1], rp.at[d - 1], place.shard_peer(d)) for d in range(1, shards)
        ]

    def early(i):
        src, dst = ((normt, normt_out), (lowt, lowt_out))[i]
        return [pltpu.make_async_copy(src, dst, se.at[i])]

    def start(copies):
        for copy in copies:
            copy.start()

    def finish(copies):
        for copy in copies:
            copy.wait()

    def stage5(kind, c):
        finish(copy4(kind, c))
        start(load(kind, c))

    def stage4(kind, c):
        finish(copy3(kind, c))
        start(copy4(kind, c))

    def stage3(kind, c):
        finish(copy2(kind, c))
        start(copy3(kind, c))

    def stage2(kind, c):
        finish(copy1(kind, c))
        start(copy2(kind, c))

    def stage1(kind, c):
        start(copy1(kind, c))

    @pl.when(step == 0)
    def _():
        place.greet()
        stage1("bc", 0)
        pack32[...] = jnp.zeros_like(pack32)
        pack32[:CONV, : cw_ref.shape[1]] = cw_ref[...].astype(F32)
        for i, ref in enumerate((cb_ref, gain_ref, ngain_ref, alog_ref, skip_ref, dtb_ref)):
            n = ref.shape[0]
            pack32[CONV + i : CONV + i + 1, :n] = ref[...].astype(F32).reshape(1, n)
        pack_ref[...] = pack32[...].astype(BF)
        pk[me] = pack_ref[...]
        wbuf[0, :, total_rows - 2 * inner :] = jnp.zeros(
            (shards, 4 * LANES - (total_rows - 2 * inner), depth), BF
        )
        ssq[...] = jnp.zeros_like(ssq)
        acc[...] = jnp.zeros_like(acc)
        small_out[...] = jnp.zeros_like(small_out)

    @pl.when(step == 4)
    def _():
        finish(tails())

    at_chunk(step - 7, lambda kind, c: finish(load(kind, c, True)))
    for run, after in ((stage3, 3), (stage4, 4), (stage2, 1), (stage1, -1), (stage5, 5)):
        at_chunk(step - after, run)

    @pl.when(step == 1)
    def _():
        start(packs())

    @pl.when(step == 2)
    def _():
        start(tails())

    @pl.when(step == 3)
    def _():
        finish(packs())
        conv_n, gain_n, heads_n = CONV_CH // shards, inner // shards, HEADS // shards
        for s in range(shards):
            part = pk[s].astype(F32)
            small_out[0 : CONV + 1, s * conv_n : (s + 1) * conv_n] = part[0 : CONV + 1, :conv_n]
            small_out[ROW_GAIN : ROW_GAIN + 1, s * gain_n : (s + 1) * gain_n] = part[5:6, :gain_n]
            small_out[ROW_NORM : ROW_NORM + 1, s * depth : (s + 1) * depth] = part[6:7, :depth]
            for i in range(3):
                small_out[ROW_ALOG + i : ROW_ALOG + i + 1, s * heads_n : (s + 1) * heads_n] = part[
                    7 + i : 8 + i, :heads_n
                ]
        hid = hidden_ref[...].astype(F32)
        scale = lax.rsqrt(jnp.mean(hid * hid, axis=1, keepdims=True) + EPS)
        normed = hid * scale * small_out[ROW_NORM : ROW_NORM + 1, :width]
        for s in range(shards):
            normed3[s] = normed[:, s * depth : (s + 1) * depth].astype(BF)
        normt[...] = normed.T.astype(BF)
        start(early(0))
        seg = jnp.broadcast_to(seg_row[...], (LANES, rows)).astype(F32)
        segc_out[...] = seg.T.astype(jnp.int32)

    def arrive(kind, c):
        finish(load(kind, c))
        start(load(kind, c, True))

    c = step - 6
    masks = lambda: [mask_out[k - 1] for k in range(1, CONV)]

    def project(k):
        return sum(mm_t(normed3[s], wbuf[k, s]) for s in range(shards))

    @pl.when(c == 0)
    def _():
        arrive("bc", 0)
        proj_out[...] = project(0)
        outs = (b_out, c_out, cbt_out, dt_out, cum_out, cumt_out, mask_out)
        end = slice(inner, inner + 2 * LANES)
        forward_setup(
            proj_out[:, : 2 * LANES], proj_out[:, 2 * LANES : 3 * LANES], segc_out[...], seg_row[...],
            small_out[:CONV, end], small_out[ROW_BIAS : ROW_BIAS + 1, end],
            small_out[ROW_ALOG : ROW_ALOG + 1, :LANES], small_out[ROW_DTB : ROW_DTB + 1, :LANES],
            outs, cb_scr, dt2, cum3,
        )

    def pairs(j, first):
        def one(p, carry):
            pair = j * per + p
            cols = pl.ds(pl.multiple_of(p * LANES, LANES), LANES)
            at = pl.ds(pl.multiple_of(pair * LANES, LANES), LANES)
            y, g = forward_pair(
                pair, zbuf[:, cols], xbuf[:, cols], small_out[:CONV, at], small_out[ROW_BIAS : ROW_BIAS + 1, at],
                small_out[ROW_SKIP : ROW_SKIP + 1, :LANES], masks(), dt2, cum3, cumt_out, cb_scr,
            )
            y_out[:, cols] = y
            gated[pair] = g
            ssq[...] += g * g
            return carry

        lax.fori_loop(first, first + per // 2, one, 0)

    @pl.when((c >= 3) & (c <= n_mix) & (c % 2 == 1))
    def _():
        pairs((c - 3) // 2, per // 2)

    is_in = (c >= 1) & (c < n_mix)

    @pl.when(is_in & (c % 2 == 1))
    def _():
        arrive("in", c)
        value = project(c % 2)
        proj_out[...] = value
        xbuf[...] = value

    @pl.when(is_in & (c % 2 == 0))
    def _():
        arrive("in", c)
        value = project(c % 2)
        proj_out[...] = value
        zbuf[...] = value
        pairs((c - 2) // 2, 0)

    @pl.when(c == n_mix)
    def _():
        mean = jnp.sum(ssq[...], axis=1, keepdims=True) * (1.0 / inner)
        r = jnp.broadcast_to(lax.rsqrt(mean + EPS), (rows, LANES))
        r_out[...] = r

        def write(i, carry):
            cols = pl.ds(pl.multiple_of(i * LANES, LANES), LANES)
            value = gated[i] * r * small_out[ROW_GAIN : ROW_GAIN + 1, cols]
            low[:, cols] = value.astype(BF)
            lowt[cols, :] = value.T.astype(BF)
            return carry

        lax.fori_loop(0, inner // LANES, write, 0)
        start(early(1))

    @pl.when((c >= n_mix) & (c < chunks))
    def _():
        arrive("out", c)
        part = owbuf[c % 2].reshape(shards * LANES, width)
        lows = [
            low[:, pl.ds(pl.multiple_of(s * (inner // shards) + (c - n_mix) * LANES, LANES), LANES)]
            for s in range(shards)
        ]
        acc[...] += mm(jnp.concatenate(lows, axis=1), part)
        grads = mm_t(cot_ref[...], part)
        for s in range(shards):
            dg_out[s] = grads[:, s * LANES : (s + 1) * LANES]

    @pl.when(c == chunks - 1)
    def _():
        added = acc[...]
        mixed_out[...] = (hidden_ref[...].astype(F32) + added).astype(BF)
        dots = jnp.sum(cot_ref[...].astype(F32) * added, axis=1, keepdims=True)
        r = r_out[...]
        rd_out[...] = r * r * (dots * (1.0 / inner))
        finish(early(0) + early(1))


def mixer_forward(hidden, cotangent, seg_ids, wt, ow, singles, rep, shards):
    rows, width = hidden.shape
    depth = width // shards
    inner = ow.shape[0] * shards
    blocks = inner // (4 * LANES)
    n_out = ow.shape[0] // LANES
    n_mix = 1 + 2 * blocks
    n_in = -(-wt.shape[0] // (4 * LANES))
    steps = n_mix + n_out + 7
    pack = (16, -(-singles[1].shape[0] // LANES) * LANES)
    f = lambda *s: jax.ShapeDtypeStruct(s, F32)
    h = lambda *s: jax.ShapeDtypeStruct(s, BF)
    vm = pltpu.VMEM
    dma = lambda *s: pltpu.SemaphoreType.DMA(s)
    anywhere = pl.BlockSpec(memory_space=pl.ANY)
    const = lambda shape: pl.BlockSpec(shape, lambda i: (0,) * len(shape), pipeline_mode=pl.Buffered(1))
    fixed = lambda shape: pl.BlockSpec(shape, lambda i: (0,) * len(shape))

    def proj_at(i):
        c = jnp.clip(i - 6, 0, n_mix - 1)
        return (0, jnp.where(c == 0, 2 * blocks, (c % 2) * blocks + (c - 1) // 2))

    def y_at(i):
        return (0, jnp.clip((i - 8) // 2, 0, blocks - 1))

    out_shape = [
        h(shards, wt.shape[0], depth), h(shards, *ow.shape), f(rows, n_in * 4 * LANES), f(rows, inner),
        h(inner, rows), f(rows, LANES), f(rows, LANES), f(rows, LANES), f(rows, rows), f(rows, LANES),
        f(rows, LANES), f(LANES, rows), f(CONV - 1, rows, LANES), h(width, rows), f(16, CONV_CH), h(rows, width),
        f(rows, LANES), jax.ShapeDtypeStruct((rows, LANES), jnp.int32), f(shards, rows, inner // shards),
    ]
    block = (rows, 4 * LANES)
    out_specs = [anywhere, anywhere, pl.BlockSpec(block, proj_at), pl.BlockSpec(block, y_at)] + [
        anywhere if s.dtype == BF and s.shape[1] == rows else fixed(s.shape) for s in out_shape[4:-1]
    ]
    out_specs.append(pl.BlockSpec((shards, rows, LANES), lambda i: (0, 0, jnp.clip(i - 6 - n_mix, 0, n_out - 1))))
    n = shards - 1
    return pl.pallas_call(
        functools.partial(forward_kernel, rep=rep, shards=shards, blocks=blocks, n_out=n_out),
        grid=(steps,),
        in_specs=[
            const((rows, width)), const((rows, width)), const((1, rows)), anywhere, anywhere, *(const(v.shape) for v in singles),
        ],
        out_specs=out_specs,
        out_shape=out_shape,
        scratch_shapes=[
            vm((shards, rows, depth), BF), vm((width, rows), BF), vm((inner, rows), BF), vm(pack, F32), vm(pack, BF), vm((shards, *pack), BF), vm((2, shards, 4 * LANES, depth), BF),
            vm((2, shards, LANES, width), BF), vm(block, F32), vm(block, F32), vm((rows, rows), F32), vm((rows, 2 * LANES), BF),
            vm((rows, 3 * LANES), BF), vm((inner // LANES, rows, LANES), F32), vm((rows, LANES), F32),
            vm((rows, inner), BF), vm((rows, width), F32),
            dma(8, n), dma(8, n), dma(8, 2, n), dma(8, 2, n), dma(8, 2, n), dma(8, 2, n), dma(8, n), dma(8, n),
            dma(2, shards), dma(n), dma(n), dma(n), dma(n), dma(2), dma(2),
        ],
        compiler_params=pltpu.CompilerParams(
            vmem_limit_bytes=VMEM_LIMIT, collective_id=1, has_side_effects=True
        ),
        name="mixer_forward",
    )(hidden, cotangent, seg_ids, wt, ow, *singles)


def chunk_at(j, blocks):
    return jnp.where(j < 2 * blocks, j // 2 + blocks * (j % 2), j)


def first_over_shards(c):
    return c % 3 == 1


def stage_steps(bits):
    more = list(range(1, bits - 1))
    n = len(more)
    rep_first = [0, 1, 2, 4, 6] + [6 + i for i in more] + [8 + n, 9 + n, 11 + n, 12 + n]
    shard_first = [0, 1, 3, 5, 7] + [7 + i for i in more] + [8 + n, 9 + n, 10 + n, 12 + n]
    return rep_first, shard_first


def reduce_kernel(*refs, rep, shards, q, blocks, n_out, n_in, tail):
    (
        z_ref, x_ref, y_ref, dgn_ref, bc_ref, dtraw_ref, r_ref, rd_ref, b_ref, c_ref, cbt_ref, dt_ref, cum_ref,
        cumt_ref, mask_ref, seg_col, seg_row, par_ref, w_ref, low_t, cot_ref, normed_t, hidden_ref,
        gin_out, gout_out, gh_out, norm_out,
        dt2, cum3, g_scr, dcum, ddt, dp, dn, gh_buf, inv, dots, ag, agt, small, small_rows, slots_norm,
        s5, r5, s6, r6, l7, s7, r7, xtra, sx, rx, sn, rn, sgh,
    ) = refs[:55]
    levels = refs[55:]
    bits = shards.bit_length() - 1
    last = 3 + bits
    keep, send, land, ssem, rsem = (dict(zip(range(1, last + 1), levels[i::5])) for i in range(5))

    step = pl.program_id(0)
    place = Place(rep, shards)
    rows = z_ref.shape[0]
    tile = z_ref.shape[1]
    mix_steps = dp.shape[2] * blocks // tile * 2
    chunks = n_out + n_in
    a, b, core, me, quarter = place.a, place.b, place.core, place.me, place.quarter

    norm = SmallSum(place, norm_out, slots_norm, sn, rn)

    @pl.when(step == 0)
    def _():
        place.greet()
        norm_out[...] = jnp.zeros_like(norm_out)
        small[6:7, :LANES] = jnp.zeros((1, LANES), F32)
        dn[...] = jnp.zeros_like(dn)
        hi, lo = pieces(dt_ref[...], 2)
        dt2[:, :LANES] = hi
        dt2[:, LANES:] = lo
        for i, part in enumerate(pieces(cum_ref[...], 3)):
            cum3[:, i * LANES : (i + 1) * LANES] = part
        g_scr[...] = jnp.zeros_like(g_scr)
        dcum[...] = jnp.zeros_like(dcum)
        ddt[...] = jnp.zeros_like(ddt)

    def halving(shard_first, level):
        at = level - 2
        if shard_first != (at >= 2):
            j = at if shard_first else at - 2
            if j < bits:
                bit, peer = place.shard_bit(j)
                return [(shards >> (j + 1), 4 * q if shard_first else q, bit, peer)] * 2
        n = 1 if shard_first else shards
        turn = at - bits if shard_first else at
        by_a, by_b = (a, place.a_peer), (b, place.b_peer)
        if turn == 0:
            return [(n, 2 * q, *by_a), (2 * n, q, *by_b)]
        return [(n, q, *by_b), (n, q, *by_a)]

    def copies(shard_first, level, c):
        k, w = c % keep[level].shape[0], c % land[level].shape[0]
        peers = [place.core_peer] * 2 if level == 1 else [part[3] for part in halving(shard_first, level)]
        return [
            remote(
                send[level].at[k, o], land[level].at[w, o], ssem[level].at[k, o], rsem[level].at[w, o], peers[o]
            )
            for o in range(2)
        ]

    def start(group):
        for copy in group:
            copy.start()

    def finish(group):
        for copy in group:
            copy.wait()

    def block(g, quarter):
        return ag.at[g, :, pl.ds(pl.multiple_of(quarter * q, q), q)]

    def half_block(g, o, quarter):
        return ag.at[g, o, pl.ds(pl.multiple_of(quarter * q, q), q)]

    def copy5(g):
        mine = block(g, quarter)
        return [
            remote(mine, mine, s5.at[g, i], r5.at[g, i], peer) for i, peer in enumerate((place.a_peer, place.b_peer))
        ]

    def copy6(g):
        from_a = half_block(g, 0, 2 * (1 - a) + b)
        from_b = half_block(g, 1, 2 * a + 1 - b)
        return [
            remote(from_a, from_a, s6.at[g, 0], r6.at[g, 0], place.b_peer),
            remote(from_b, from_b, s6.at[g, 1], r6.at[g, 1], place.a_peer),
        ]

    def targets(c, is_out):
        if is_out:
            cols = pl.ds(pl.multiple_of(c * 2 * LANES + core * LANES, LANES), LANES)
            return [gout_out.at[pl.ds(o * 4 * q, 4 * q), cols] for o in range(2)]
        base = chunk_at(c - n_out, blocks) * 4 * LANES + core * 2 * LANES
        return [gin_out.at[pl.ds(pl.multiple_of(base + o * LANES, LANES), LANES)] for o in range(2)]

    def copy7(c, is_out):
        g, t = c % ag.shape[0], c % agt.shape[0]
        ends = targets(c, is_out)
        own = [ag.at[g, o] if is_out else agt.at[t, o] for o in range(2)]
        local = [pltpu.make_async_copy(own[o], ends[o], l7.at[g, o]) for o in range(2)]
        return local + [remote(own[o], ends[o], s7.at[g, o], r7.at[g, o], place.core_peer) for o in range(2)]

    def by_target(c, run):
        for is_out in (True, False):

            @pl.when((c < n_out) == is_out)
            def _(is_out=is_out):
                run(is_out)

    def stage_first(c):
        @pl.when(c < n_out)
        def _():
            base = c * 2 * LANES
            for s in range(shards):
                lhs = low_t[s * 8 * q : (s + 1) * 8 * q, :]
                for side, ref in ((core, keep[1]), (1 - core, send[1])):
                    cols = pl.ds(pl.multiple_of(base + side * LANES, LANES), LANES)
                    grad = mm(lhs, cot_ref[:, cols])
                    for o in range(2):
                        ref[0, o, s * 4 * q : (s + 1) * 4 * q] = grad[o * 4 * q : (o + 1) * 4 * q].astype(ref.dtype)

        @pl.when(c >= n_out)
        def _():
            n = chunk_at(c - n_out, blocks)
            for s in range(shards):
                own = slice(s * 4 * q, (s + 1) * 4 * q)
                for side, ref in ((core, keep[1]), (1 - core, send[1])):
                    cols = pl.ds(pl.multiple_of(side * 2 * LANES, 2 * LANES), 2 * LANES)
                    grad = mm(normed_t[own, :], dp[n, :, cols])
                    for o in range(2):
                        ref[0, o, own] = grad[:, o * LANES : (o + 1) * LANES].astype(ref.dtype)

        for side, ref in ((1, keep[1]), (0, send[1])):

            @pl.when((c == chunks - 1) & (core == side))
            def _(ref=ref):
                for s in range(shards):
                    at = s * 4 * q
                    ref[0, 1, at : at + small_rows.shape[1]] = small_rows[s].astype(ref.dtype)

        start(copies(False, 1, c))

    def stage_halve(shard_first, level, c):
        finish(copies(shard_first, level - 1, c))
        k0, w0 = c % keep[level - 1].shape[0], c % land[level - 1].shape[0]
        k = c % keep[level].shape[0]
        for o, (runs, size, bit, _) in enumerate(halving(shard_first, level)):

            def part(u, carry, o=o, size=size, bit=bit):
                own = pl.ds(pl.multiple_of((2 * u + bit) * size, size), size)
                other = pl.ds(pl.multiple_of((2 * u + 1 - bit) * size, size), size)
                end = pl.ds(pl.multiple_of(u * size, size), size)
                keep[level][k, o, end] = keep[level - 1][k0, o, own] + land[level - 1][w0, o, own].astype(F32)
                send[level][k, o, end] = (
                    keep[level - 1][k0, o, other] + land[level - 1][w0, o, other].astype(F32)
                ).astype(BF)
                return carry

            if runs == 1:
                part(0, 0)
            else:
                lax.fori_loop(0, runs, part, 0)
        start(copies(shard_first, level, c))

    def stage_total(shard_first, c):
        finish(copies(shard_first, last, c))
        k, w, g = c % keep[last].shape[0], c % land[last].shape[0], c % ag.shape[0]
        total = keep[last][k] + land[last][w].astype(F32)
        for i, peer in enumerate(place.extra):
            keep[last][k] = total
            copy = remote(keep[last].at[k], xtra.at[c % 2, i], sx.at[c % 2, i], rx.at[c % 2, i], peer)
            copy.start()
            copy.wait()
            total = total + xtra[c % 2, i]
        for o in range(2):
            ag[g, o, pl.ds(pl.multiple_of(quarter * q, q), q)] = total[o].astype(BF)
        start(copy5(g))

    def stage_forward(c):
        g = c % ag.shape[0]
        for copy in copy5(g):
            copy.wait_recv()
        start(copy6(g))

    def stage_out(c):
        g, t = c % ag.shape[0], c % agt.shape[0]
        for copy in copy6(g):
            copy.wait_recv()

        def run(is_out):
            if not is_out:
                for o in range(2):
                    agt[t, o] = ag[g, o].astype(F32).T.astype(BF)
            start(copy7(c, is_out))

        by_target(c, run)

    def stage_end(c):
        by_target(c, lambda is_out: finish(copy7(c, is_out)))
        g = c % ag.shape[0]
        for copy in copy5(g) + copy6(g):
            copy.wait_send()

    plans = stage_steps(bits)

    def run_stage(number):
        for shard_first in (False, True):
            c = step - plans[shard_first][number - 1]

            @pl.when((c >= 0) & (c < chunks) & (first_over_shards(c) == shard_first))
            def _(c=c, shard_first=shard_first):
                if number == 1:
                    stage_first(c)
                elif number <= last:
                    stage_halve(shard_first, number, c)
                elif number == last + 1:
                    stage_total(shard_first, c)
                else:
                    (stage_forward, stage_out, stage_end)[number - last - 2](c)

    order = [5, 6, 8, 9, 7, 2, 4, 1, 3]
    for number in order + list(range(10, last + 5)):
        run_stage(number)

    masks = lambda: [mask_ref[k - 1] for k in range(1, CONV)]

    def pairs(first, count):
        def one(p, carry):
            pair = step // 2 * (tile // LANES) + p
            cols = pl.ds(pl.multiple_of(p * LANES, LANES), LANES)
            at = pl.ds(pl.multiple_of(pair * LANES, LANES), LANES)
            skip = skip_lanes(par_ref[ROW_SKIP : ROW_SKIP + 1, :LANES], head_of_lane(pair))
            res = backward_pair(
                pair, z_ref[:, cols], x_ref[:, cols], y_ref[:, cols], dgn_ref[0, :, cols], r_ref[...], rd_ref[...],
                par_ref[:CONV, at], par_ref[ROW_BIAS : ROW_BIAS + 1, at], skip, par_ref[ROW_GAIN : ROW_GAIN + 1, at],
                masks(), dt2, cum3, cumt_ref, cbt_ref, g_scr, dcum, ddt,
            )
            end = pl.ds(pl.multiple_of(pair % 4 * LANES, LANES), LANES)
            dp[pair // 4, :, end] = res[0]
            dp[blocks + pair // 4, :, end] = res[1]
            for k in range(CONV):
                small[k : k + 1, at] = res[4][k]
            small[4:5, at] = res[5]
            small[5:6, at] = res[2]
            per_head = jnp.concatenate(pieces(jnp.broadcast_to(res[3], (8, LANES)), 3), axis=1)
            small[6:7, :LANES] += mm_t(per_head, jnp.concatenate([head_of_lane(pair)] * 3, axis=1))[0:1]
            return carry

        lax.fori_loop(first, first + count, one, 0)

    @pl.when((step < mix_steps) & (step % 2 == 0))
    def _():
        pairs(0, 1)

    @pl.when((step < mix_steps) & (step % 2 == 1))
    def _():
        pairs(1, tile // LANES - 1)

    @pl.when(step == mix_steps - 1)
    def _():
        end = slice(INNER, INNER + 2 * LANES)
        d_bc, d_raw, d_weight, d_bias, d_alog, d_dtb = backward_tail(
            bc_ref, dtraw_ref, b_ref, c_ref, dt_ref, masks(), seg_col, seg_row, par_ref[:CONV, end],
            par_ref[ROW_BIAS : ROW_BIAS + 1, end], par_ref[ROW_ALOG : ROW_ALOG + 1, :LANES],
            par_ref[ROW_DTB : ROW_DTB + 1, :LANES], g_scr, dcum, ddt,
        )
        for i in range(2):
            cols = slice(i * LANES, (i + 1) * LANES)
            dp[2 * blocks, :, cols] = d_bc[i].astype(BF)
            end = slice(INNER + i * LANES, INNER + (i + 1) * LANES)
            for k in range(CONV):
                small[k : k + 1, end] = d_weight[i][k]
            small[4:5, end] = d_bias[i]
        dp[2 * blocks, :, 2 * LANES : 3 * LANES] = d_raw.astype(BF)
        dp[2 * blocks, :, 3 * LANES :] = jnp.zeros((rows, LANES), BF)
        small[5:6, INNER : INNER + LANES] = d_alog
        small[5:6, INNER + LANES :] = d_dtb
        for s in range(shards):
            for at, (row, lane) in enumerate(small_tiles(s, shards)):
                small_rows[s, at : at + 1, :] = small[row : row + 1, lane : lane + LANES]

    @pl.when((step >= n_out) & (step < chunks - 1))
    def _():
        grad = dp[chunk_at(step - n_out, blocks)]
        for s in range(shards):
            dn[s] += mm(grad, w_ref[s])

    @pl.when(step == chunks - 1)
    def _():
        grad = dp[n_in - 1]
        keep_rows = iota(w_ref.shape[1:], 0) < tail
        for s in range(shards):
            dn[s] += mm(grad, jnp.where(keep_rows, w_ref[s], 0))

    wide_cols = gh_buf.shape[2]
    together = wide_cols // dn.shape[2]
    n_parts = shards // together

    def norm_part(i):
        cols = slice(i * wide_cols, (i + 1) * wide_cols)
        d_normed = jnp.concatenate([dn[s] for s in range(i * together, (i + 1) * together)], axis=1)
        unit = hidden_ref[:, cols].astype(F32) * inv[:, :1]
        return cols, d_normed, unit, d_normed * par_ref[ROW_NORM : ROW_NORM + 1, cols]

    def first_pass(i):
        cols, d_normed, unit, du = norm_part(i)
        grad_norm = jnp.sum(d_normed * unit, axis=0, keepdims=True)
        for j in range(wide_cols // LANES):
            at = i * (wide_cols // LANES) + j
            norm_out[at : at + 1, :] = grad_norm[:, j * LANES : (j + 1) * LANES]
        dots[...] += jnp.sum(du * unit, axis=1, keepdims=True) * (1.0 / hidden_ref.shape[1])

    def gh_copy(i):
        return pltpu.make_async_copy(
            gh_buf.at[i % 2], gh_out.at[:, i * wide_cols : (i + 1) * wide_cols], sgh.at[i % 2]
        )

    def second_pass(i):
        if i >= 2:
            gh_copy(i - 2).wait()
        cols, _, unit, du = norm_part(i)
        gh_buf[i % 2] = cot_ref[:, cols].astype(F32) + inv[:, :1] * (du - unit * dots[:, :1])
        gh_copy(i).start()

    @pl.when(step == chunks)
    def _():
        hid = hidden_ref[...].astype(F32)
        scale = lax.rsqrt(jnp.mean(hid * hid, axis=1, keepdims=True) + EPS)
        inv[...] = jnp.broadcast_to(scale, inv.shape)
        dots[...] = jnp.zeros_like(dots)
        first_pass(0)

    for i in range(1, n_parts):

        @pl.when(step == chunks + (i + 1) // 2)
        def _(i=i):
            first_pass(i)

    norm_from = chunks + n_parts // 2

    for i in range(n_parts):

        @pl.when(step == norm_from + 1 + i)
        def _(i=i):
            second_pass(i)

    @pl.when(step == norm_from + 1 + n_parts)
    def _():
        for i in range(max(0, n_parts - 2), n_parts):
            gh_copy(i).wait()

    for i in range(norm.stages):

        @pl.when(step == norm_from + i)
        def _(i=i):
            norm.stage(i)


def results_kernel(
    gin_ref, gout_ref, gh_ref, mixed_ref, norm_ref,
    gin_out, gout_out, gh_out, mixed_out, ngain_out, gain_out, cw_out, cb_out, alog_out, skip_out, dtb_out, *, shards
):
    step = pl.program_id(0)
    me = lax.axis_index("shard")
    gin_out[...] = gin_ref[...].astype(F32)
    gout_out[...] = gout_ref[...].astype(F32)
    gh_out[...] = gh_ref[...]
    mixed_out[...] = mixed_ref[...]

    @pl.when(step == pl.num_programs(0) - 1)
    def _():
        conv, gain, heads, ngain = cb_out.shape[0], gain_out.shape[0], alog_out.shape[0], ngain_out.shape[0]
        rows = gin_ref.shape[0]
        small = gin_ref[rows - LANES :, :].astype(F32).T
        norm = jnp.concatenate([norm_ref[i : i + 1, :] for i in range(norm_ref.shape[0])], axis=1)
        for s in range(shards):

            @pl.when(me == s)
            def _(s=s):
                tiles = small_tiles(s, shards)

                def part(row, base, size):
                    at = [i for i, (r, lane) in enumerate(tiles) if r == row and base <= lane < base + max(size, LANES) * shards]
                    flat = jnp.concatenate([small[i : i + 1, :] for i in at], axis=1)
                    first = s * size - (tiles[at[0]][1] - base)
                    return flat[:, first : first + size]

                for k in range(CONV):
                    cw_out[k : k + 1, :] = part(k, 0, conv)
                cb_out[...] = part(CONV, 0, conv).reshape(conv)
                gain_out[...] = part(5, 0, gain).reshape(gain)
                for ref, row, base in ((alog_out, 5, INNER), (dtb_out, 5, INNER + LANES), (skip_out, 6, 0)):
                    i = tiles.index((row, base))
                    ref[...] = small[i : i + 1, s * heads : (s + 1) * heads].reshape(heads)
                ngain_out[...] = norm[:, s * ngain : (s + 1) * ngain].reshape(ngain)


def results(g_in, g_out, grad_hidden, mixed, norm, columns, singles, shards):
    conv_w, conv_b, gain, ngain, a_log = singles[:5]
    depth, width = g_in.shape[1], g_out.shape[1]
    steps = 8
    f = lambda *s: jax.ShapeDtypeStruct(s, F32)
    strip = lambda v: pl.BlockSpec((v.shape[0] // steps, v.shape[1]), lambda i: (i, 0))
    whole = lambda s: pl.BlockSpec(s, lambda i: (0,) * len(s))
    small = [ngain.shape, gain.shape, conv_w.shape, conv_b.shape, a_log.shape, a_log.shape, a_log.shape]
    return pl.pallas_call(
        functools.partial(results_kernel, shards=shards),
        grid=(steps,),
        in_specs=[strip(g_in), strip(g_out), strip(grad_hidden), strip(mixed), whole(norm.shape)],
        out_specs=[strip(g_in), strip(g_out), strip(grad_hidden), strip(mixed), *(whole(s) for s in small)],
        out_shape=[
            f(columns, depth), f(*g_out.shape), f(*grad_hidden.shape), jax.ShapeDtypeStruct(mixed.shape, BF),
            *(f(*s) for s in small),
        ],
        name="results",
    )(g_in, g_out, grad_hidden, mixed, norm)


def mixer_backward_and_sums(saved, hidden, cotangent, seg_ids, rep, shards):
    (w3, ow3, proj, y, low_t, r, b, c, cbt, dt, cum, cumt, mask, normed_t, params, _, rd, seg_col, d_gated) = saved
    rows, width = hidden.shape
    inner = low_t.shape[0]
    depth = width // shards
    wide_block = 4 * LANES
    blocks = inner // wide_block
    n_out = width // (2 * LANES)
    n_in = proj.shape[1] // wide_block
    q = depth // 4
    chunks = n_out + n_in
    bits = shards.bit_length() - 1
    steps = chunks + stage_steps(bits)[0][-1]
    n_small = SmallSum.count(rep, shards)
    n_extra = max(1, n_small - 3 - (shards - 1))
    tile = 3 * LANES
    tiles = inner // tile
    mix = lambda offset: pl.BlockSpec((rows, tile), lambda i: (0, offset + jnp.minimum(i // 2, tiles - 1)))
    a_shard = inner // shards // tile

    def d_gated_at(i):
        at = jnp.minimum(i // 2, tiles - 1)
        return at // a_shard, 0, at % a_shard

    const = lambda shape, at=None: pl.BlockSpec(shape, lambda i: at or (0,) * len(shape), pipeline_mode=pl.Buffered(1))
    f = lambda *s: jax.ShapeDtypeStruct(s, F32)
    h = lambda *s: jax.ShapeDtypeStruct(s, BF)
    vm = pltpu.VMEM
    dma = lambda *s: pltpu.SemaphoreType.DMA(s)
    anywhere = pl.BlockSpec(memory_space=pl.ANY)
    pairs_bc = inner // LANES
    in_specs = [
        mix(0), mix(tiles), mix(0),
        pl.BlockSpec((1, rows, tile), d_gated_at),
        const((rows, 2 * LANES), (0, pairs_bc)), const((rows, LANES), (0, 2 * pairs_bc + 2)),
        const((rows, LANES)), const((rows, LANES)), const((rows, LANES)), const((rows, LANES)),
        const((rows, rows)), const((rows, LANES)), const((rows, LANES)), const((LANES, rows)),
        const((CONV - 1, rows, LANES)), const((rows, LANES)), const((1, rows)), const(params.shape),
        pl.BlockSpec(
            (shards, wide_block, depth), lambda i: (0, chunk_at(jnp.clip(i - n_out, 0, n_in - 1), blocks), 0)
        ),
        const((inner, rows)), const((rows, width)), const((width, rows)), const((rows, width)),
    ]
    whole_out = lambda shape: pl.BlockSpec(shape, lambda i: (0,) * len(shape))
    norm_shape = (16, LANES)
    small_height = -(-max(len(small_tiles(s, shards)) for s in range(shards)) // 16) * 16
    scratch = [
        vm((rows, 2 * LANES), BF), vm((rows, 3 * LANES), BF), vm((rows, rows), F32), vm((rows, LANES), F32),
        vm((rows, LANES), F32), vm((n_in, rows, wide_block), BF), vm((shards, rows, depth), F32), vm((2, rows, tile), F32), vm((rows, LANES), F32), vm((rows, LANES), F32),
        vm((8, 2, 4 * q, LANES), BF), vm((4, 2, LANES, 4 * q), BF),
        vm((8, CONV_CH), F32), vm((shards, small_height, LANES), F32), vm((n_small, *norm_shape), F32),
        dma(8, 2), dma(8, 2), dma(8, 2), dma(8, 2), dma(8, 2), dma(8, 2), dma(8, 2),
        vm((2, n_extra, 2, q, LANES), F32), dma(2, n_extra), dma(2, n_extra),
        dma(n_small), dma(n_small), dma(2),
    ]
    for level in range(1, 4 + bits):
        own, landing = {1: (1, 2), 2: (3, 8)}.get(level, (4, 8))
        shape = (2, (shards * 4 * q) >> (level - 1), LANES)
        scratch += [
            vm((own, *shape), F32), vm((own, *shape), BF), vm((landing, *shape), BF), dma(own, 2), dma(landing, 2),
        ]
    return pl.pallas_call(
        functools.partial(
            reduce_kernel, rep=rep, shards=shards, q=q, blocks=blocks, n_out=n_out, n_in=n_in,
            tail=w3.shape[1] - (n_in - 1) * wide_block,
        ),
        grid=(steps,),
        in_specs=in_specs,
        out_specs=[anywhere, anywhere, anywhere, whole_out(norm_shape)],
        out_shape=[
            h(n_in * wide_block, depth), h(inner // shards, width), f(rows, width), f(*norm_shape),
        ],
        scratch_shapes=scratch,
        compiler_params=pltpu.CompilerParams(
            vmem_limit_bytes=VMEM_LIMIT, collective_id=2, has_side_effects=True
        ),
        name="mixer_backward_and_sums",
    )(
        proj, proj, y, d_gated, proj, proj, r, rd, b, c, cbt, dt, cum, cumt, mask, seg_col, seg_ids,
        params, w3, low_t, cotangent, normed_t, hidden,
    )


def per_device(
    hidden, seg_ids, cotangent, in_weight, out_weight, norm_gain, gated_gain, conv_weight, conv_bias, a_log, d_skip,
    dt_bias,
):
    rep, shards = lax.axis_size("rep"), lax.axis_size("shard")
    singles = (conv_weight, conv_bias, gated_gain, norm_gain, a_log, d_skip, dt_bias)
    wt = in_weight.T
    saved = mixer_forward(hidden, cotangent, seg_ids, wt, out_weight, singles, rep, shards)
    mixed = saved[15]
    g_in, g_out, grad_hidden, norm = mixer_backward_and_sums(saved, hidden, cotangent, seg_ids, rep, shards)
    g_in, g_out, grad_hidden, mixed, *small = results(
        g_in, g_out, grad_hidden, mixed, norm, wt.shape[0], singles, shards
    )
    return (mixed, grad_hidden, g_in.T, g_out, *small)


def solution(mesh):
    both = ("rep", "shard")
    shard = P("shard")
    placed = (P(both, None), P(both, None), P(both, None), P("shard", None), P("shard", None), shard, shard,
              P(None, "shard"), shard, shard, shard, shard)
    outs = (P(both, None), P(both, None), P("shard", None), P("shard", None), shard, shard, P(None, "shard"), shard,
            shard, shard, shard)
    return jax.shard_map(per_device, mesh=mesh, in_specs=placed, out_specs=outs, check_vma=False)
```

```python
import functools
import jax
import jax.numpy as jnp
from jax import lax
from jax.experimental import pallas as pl
from jax.experimental.pallas import tpu as pltpu
from jax.sharding import PartitionSpec as P

HEADS = 48
HEAD_DIM = 64
STATE = 128
CONV = 4
INNER = 3072
CONV_CH = 3328
LANES = 128
EPS = 1e-05
LOG2E = 1.4426950408889634
BF = jnp.bfloat16
F32 = jnp.float32
HIGH = lax.Precision.HIGHEST
VMEM_LIMIT = 63 * 2**20
MESH = pl.DeviceIdType.MESH


def mm(a, b):
    return jnp.dot(a, b, preferred_element_type=F32)


def mm_t(a, b):
    return lax.dot_general(a, b, (((1,), (1,)), ((), ())), preferred_element_type=F32)


def pieces(value, count):
    parts = []
    for _ in range(count):
        part = value.astype(BF)
        parts.append(part)
        value = value - part.astype(F32)
    return parts


def iota(shape, dim):
    return lax.broadcasted_iota(jnp.int32, shape, dim)


def head_of_lane(pair):
    heads, lanes = iota((LANES, LANES), 0), iota((LANES, LANES), 1)
    return (heads == 2 * pair + lanes // HEAD_DIM).astype(BF)


def head_columns(cum3, pair):
    heads, lanes = iota((LANES, 2 * LANES), 0), iota((LANES, 2 * LANES), 1)
    pick = (heads == 2 * pair + lanes // LANES).astype(BF)
    cols = mm(cum3[...], jnp.concatenate([pick] * 3, axis=0))
    return cols[:, :LANES], cols[:, LANES:]


def conv_shifts(value, masks):
    return [pltpu.roll(value, k, 0) * masks[k - 1] for k in range(1, CONV)]


def conv_apply(value, shifts, weight, bias):
    total = bias + weight[CONV - 1 : CONV] * value
    for k in range(1, CONV):
        total = total + weight[CONV - 1 - k : CONV - k] * shifts[k - 1]
    return total


def conv_back(d_pre, value, shifts, masks, weight):
    rows = d_pre.shape[0]
    d_value = weight[CONV - 1 : CONV] * d_pre
    d_weight = [jnp.sum(d_pre * value, axis=0, keepdims=True)]
    for k in range(1, CONV):
        d_weight.append(jnp.sum(d_pre * shifts[k - 1], axis=0, keepdims=True))
        d_value = d_value + weight[CONV - 1 - k : CONV - k] * pltpu.roll(
            d_pre * masks[k - 1], rows - k, 0
        )
    d_bias = jnp.sum(d_pre, axis=0, keepdims=True)
    return d_value, d_weight[::-1], d_bias


def silu_parts(value):
    sig = 0.5 * jnp.tanh(0.5 * value) + 0.5
    return sig, value * sig


def silu_slope(sig, silu):
    return sig + silu - silu * sig


def decay(col, row, clamp):
    gap = col - row
    return jnp.exp2(jnp.minimum(gap, 0.0) if clamp else gap)


def wide(col, width):
    return jnp.concatenate([col] * (width // LANES), axis=1)


def backward_pair(
    pair, z, value, y, dgn, r, rd, cw, cb, skip, gain, masks, dt2, cum3, cumt_ref, cbt_ref, g_scr, dcum, ddt
):
    rows = z.shape[0]
    half = rows // 2
    shifts = conv_shifts(value, masks)
    pre = conv_apply(value, shifts, cw, cb)
    sp, x = silu_parts(pre)
    sg, sz = silu_parts(z)
    scanned = y + skip * x
    g = scanned * sz
    dgn_r = dgn * r
    d_gain = jnp.sum(dgn_r * g, axis=0, keepdims=True)
    dg = gain * dgn_r - g * rd
    dz = (dg * scanned * silu_slope(sg, sz)).astype(BF)
    dsc = dg * sz
    d_skip = jnp.sum(dsc * x, axis=0, keepdims=True)
    dy = dsc.astype(BF)
    spread = head_of_lane(pair)
    step = mm(dt2[...], jnp.concatenate([spread, spread], axis=0))
    both = jnp.concatenate([spread, spread], axis=1)
    xt = (x * step).astype(BF)
    first = iota((rows, LANES), 1) < HEAD_DIM
    zero = jnp.zeros_like(xt)
    columns = head_columns(cum3, pair)
    blocks = (
        (slice(0, half), slice(0, half), True),
        (slice(0, half), slice(half, rows), False),
        (slice(half, rows), slice(half, rows), True),
    )
    rows_of = [cumt_ref[pl.ds(2 * pair + side, 1), :] for side in range(2)]
    sides = [jnp.where(first == (side == 0), xt, zero) for side in range(2)]
    parts = [[], []]
    for js, is_, clamp in blocks:
        total = g_scr[js, is_]
        for side in range(2):
            e = decay(rows_of[side][:, is_], wide(columns[side][js], half), clamp)
            parts[side].append(mm((e * cbt_ref[js, is_]).astype(BF), dy[is_]))
            total = total + e * mm_t(sides[side][js], dy[is_])
        g_scr[js, is_] = total
    dxts = [jnp.concatenate([p[0] + p[1], p[2]], axis=0) for p in parts]
    dxt = jnp.where(first, dxts[0], dxts[1])
    for ref, term in ((dcum, dy.astype(F32) * y - xt.astype(F32) * dxt), (ddt, x * dxt)):
        ref[...] += mm_t(jnp.concatenate(pieces(term, 2), axis=1), both)
    dx = skip * dsc + step * dxt
    d_pre = dx * silu_slope(sp, x)
    d_value, d_weight, d_bias = conv_back(d_pre, value, shifts, masks, cw)
    return dz, d_value.astype(BF), d_gain, d_skip, d_weight, d_bias


def backward_tail(
    bc_ref, dtraw_ref, b_ref, c_ref, dt_ref, masks, seg_col, seg_row, cw_bc, cb_bc, alog_ref, bias_ref,
    g_scr, dcum, ddt
):
    rows = dt_ref.shape[0]
    same = wide(seg_col[...], rows) == seg_row[...]
    later = (iota((rows, rows), 0) <= iota((rows, rows), 1)) & same
    gt = jnp.where(later, g_scr[...], 0.0)
    db = jnp.dot(gt, c_ref[...], precision=HIGH, preferred_element_type=F32)
    dc = jnp.dot(gt.T, b_ref[...], precision=HIGH, preferred_element_type=F32)
    d_bc, d_weights, d_biases = [], [], []
    for i, d_out in enumerate((db, dc)):
        cols = slice(i * LANES, (i + 1) * LANES)
        value = bc_ref[:, cols]
        shifts = conv_shifts(value, masks)
        pre = conv_apply(value, shifts, cw_bc[:, cols], cb_bc[:, cols])
        sp, value_out = silu_parts(pre)
        d_pre = d_out * silu_slope(sp, value_out)
        d_value, d_weight, d_bias = conv_back(d_pre, value, shifts, masks, cw_bc[:, cols])
        d_bc.append(d_value)
        d_weights.append(d_weight)
        d_biases.append(d_bias)
    step = dt_ref[...]
    live = iota((rows, LANES), 1) < HEADS
    rate = -jnp.exp(alog_ref)
    later_bf = later.astype(BF)
    dlog = sum(mm(later_bf, part) for part in pieces(dcum[...], 3)[::-1])
    dstep = ddt[...] + dlog * rate
    raw = jnp.where(live, dtraw_ref[...] + bias_ref, 0.0)
    d_raw = jnp.where(live, dstep / (1.0 + jnp.exp(-raw)), 0.0)
    d_alog = jnp.sum(dlog * step, axis=0, keepdims=True) * rate
    return d_bc, d_raw, d_weights, d_biases, d_alog, jnp.sum(d_raw, axis=0, keepdims=True)


class Place:
    def __init__(self, rep, shards):
        self.rep, self.shards = rep, shards
        r, self.me = lax.axis_index("rep"), lax.axis_index("shard")
        self.r = r
        self.core, self.a, self.b = r % 2, (r // 2) % 2, (r // 4) % 2
        self.core_peer = (r + 1 - 2 * self.core, self.me)
        self.a_peer = (r + 2 - 4 * self.a, self.me)
        self.b_peer = (r + 4 - 8 * self.b, self.me)
        self.extra = []
        stride = 8
        while stride < rep:
            bit = (r // stride) % 2
            self.extra.append((r + stride - 2 * stride * bit, self.me))
            stride *= 2
        self.quarter = 2 * self.a + self.b

    def shard_bit(self, j):
        bit = (self.me // (1 << j)) % 2
        return bit, (self.r, self.me + (1 << j) - (2 << j) * bit)

    def shard_peer(self, distance):
        return (self.r, (self.me + distance) % self.shards)

    def partners(self):
        return [self.core_peer, self.a_peer, self.b_peer, *self.extra] + [
            self.shard_peer(d) for d in range(1, self.shards)
        ]

    def greet(self):
        barrier = pltpu.get_barrier_semaphore()
        partners = self.partners()
        for partner in partners:
            pl.semaphore_signal(barrier, inc=1, device_id=partner, device_id_type=MESH)
        pl.semaphore_wait(barrier, len(partners))


def remote(src, dst, send, recv, device):
    return pltpu.make_async_remote_copy(
        src_ref=src, dst_ref=dst, send_sem=send, recv_sem=recv, device_id=device, device_id_type=MESH
    )


class SmallSum:
    def __init__(self, place, buf, slots, sends, recvs):
        self.buf, self.slots, self.sends, self.recvs = buf, slots, sends, recvs
        pairs = [place.core_peer, place.a_peer, place.b_peer, *place.extra]
        self.groups = [[peer] for peer in pairs] + [[place.shard_peer(d) for d in range(1, place.shards)]]
        self.stages = len(self.groups) + 1

    @staticmethod
    def count(rep, shards):
        return rep.bit_length() - 1 + shards - 1

    def copies(self, group):
        at = sum(len(g) for g in self.groups[:group])
        return [
            remote(self.buf, self.slots.at[at + i], self.sends.at[at + i], self.recvs.at[at + i], peer)
            for i, peer in enumerate(self.groups[group])
        ]

    def stage(self, number):
        if number > 0:
            at = sum(len(g) for g in self.groups[: number - 1])
            copies = self.copies(number - 1)
            for copy in copies:
                copy.wait()
            total = self.buf[...]
            for i in range(len(copies)):
                total = total + self.slots[at + i]
            self.buf[...] = total
        if number < len(self.groups):
            for copy in self.copies(number):
                copy.start()


def small_tiles(s, shards):
    def span(total):
        size = total // shards
        return range(s * size // LANES * LANES, (s + 1) * size, LANES)

    tiles = [(row, lane) for row in range(CONV + 1) for lane in span(CONV_CH)]
    tiles += [(5, lane) for lane in span(INNER)]
    return tiles + [(5, INNER), (5, INNER + LANES), (6, 0)]


def forward_setup(
    bc, raw, seg_col, seg_row, cw, cb, alog, bias, outs, cb_scr, dt2, cum3
):
    b_out, c_out, cbt_out, dt_out, cum_out, cumt_out, mask_out = outs
    rows = raw.shape[0]
    at = iota((rows, LANES), 0)
    for k in range(1, CONV):
        same = (pltpu.roll(seg_col, k, 0) == seg_col) & (at >= k)
        mask_out[k - 1] = same.astype(F32)
    masks = [mask_out[k - 1] for k in range(1, CONV)]
    results = []
    for i in range(2):
        cols = slice(i * LANES, (i + 1) * LANES)
        value = bc[:, cols]
        pre = conv_apply(value, conv_shifts(value, masks), cw[:, cols], cb[:, cols])
        results.append(silu_parts(pre)[1])
    b_out[...] = results[0]
    c_out[...] = results[1]
    products = lax.dot_general(
        results[1], results[0], (((1,), (1,)), ((), ())), precision=HIGH, preferred_element_type=F32
    )
    lower = iota((rows, rows), 0) >= iota((rows, rows), 1)
    allowed = lower & (wide(seg_col, rows) == seg_row)
    products = jnp.where(allowed, products, 0.0)
    cb_scr[...] = products
    cbt_out[...] = products.T
    live = iota((rows, LANES), 1) < HEADS
    raw = jnp.where(live, raw + bias, 0.0)
    step = jnp.where(live, jnp.maximum(raw, 0.0) + jnp.log(1.0 + jnp.exp(-jnp.abs(raw))), 0.0)
    dt_out[...] = step
    hi, lo = pieces(step, 2)
    dt2[:, :LANES] = hi
    dt2[:, LANES:] = lo
    log_rate = step * (-LOG2E * jnp.exp(alog))
    tri = lower.astype(BF)
    cum = sum(mm(tri, part) for part in pieces(log_rate, 3)[::-1])
    cum_out[...] = cum
    cumt_out[...] = cum.T
    for i, part in enumerate(pieces(cum, 3)):
        cum3[:, i * LANES : (i + 1) * LANES] = part


def skip_lanes(skip_row, spread):
    return mm(jnp.broadcast_to(skip_row, (8, LANES)).astype(BF), spread)[0:1]


def forward_pair(pair, z, value, cw, cb, skip_row, masks, dt2, cum3, cumt_ref, cb_scr):
    rows = z.shape[0]
    half = rows // 2
    pre = conv_apply(value, conv_shifts(value, masks), cw, cb)
    x = silu_parts(pre)[1]
    spread = head_of_lane(pair)
    step = mm(dt2[...], jnp.concatenate([spread, spread], axis=0))
    xt = (x * step).astype(BF)
    first = iota((rows, LANES), 1) < HEAD_DIM
    ys = []
    columns = head_columns(cum3, pair)
    for side in range(2):
        head = 2 * pair + side
        col = columns[side]
        row = cumt_ref[pl.ds(head, 1), :]
        low_row, high_row = row[:, :half], row[:, half:]
        top, bottom = wide(col[:half], half), wide(col[half:], half)
        m00 = (decay(top, low_row, True) * cb_scr[:half, :half]).astype(BF)
        m10 = (decay(bottom, low_row, False) * cb_scr[half:, :half]).astype(BF)
        m11 = (decay(bottom, high_row, True) * cb_scr[half:, half:]).astype(BF)
        ys.append(
            jnp.concatenate([mm(m00, xt[:half]), mm(m10, xt[:half]) + mm(m11, xt[half:])], axis=0)
        )
    y = jnp.where(first, ys[0], ys[1])
    g = (y + skip_lanes(skip_row, spread) * x) * silu_parts(z)[1]
    return y, g


ROW_BIAS, ROW_GAIN, ROW_NORM, ROW_ALOG, ROW_SKIP, ROW_DTB = 4, 5, 6, 7, 8, 9


def forward_kernel(
    hidden_hbm, cot_hbm, seg_row, wt_ref, ow_ref, cw_ref, cb_ref, gain_ref, ngain_ref, alog_ref, skip_ref, dtb_ref,
    w3, ow3, proj_out, y_out, lowt_out, r_out, b_out, c_out, cbt_out, dt_out, cum_out, cumt_out, mask_out,
    normt_out, small_out, mixed_out, rd_out, segc_out, dg_out,
    normed3, normt, lowt, pack32, pack_ref, pk, wbuf, owbuf, xbuf, zbuf, cb_scr, dt2, cum3, gated, ssq, low, acc,
    sz, rz, s2, r2, s3, r3, s4, r4, lw, st, rt, sp, rp, lc, se, hidden_ref, cot_ref, si,
    *, rep, shards, blocks, n_out
):
    step = pl.program_id(0)
    place = Place(rep, shards)
    a, b, core, me, quarter = place.a, place.b, place.core, place.me, place.quarter
    rows, width = hidden_hbm.shape
    depth = width // shards
    inner = blocks * 4 * LANES
    per = 4
    n_mix = 1 + 2 * blocks
    chunks = n_mix + n_out
    tail_at = 2 * inner + 2 * LANES
    tail = w3.shape[1] - tail_at
    total_rows = w3.shape[1]

    def rows_of(kind, c):
        if kind == "bc":
            return 2 * inner, 2 * LANES
        if kind == "in":
            j = (c - 1) // 2
            return ((c % 2) * inner + j * 4 * LANES), 4 * LANES
        return (c - n_mix) * LANES, LANES

    def view(kind, c, s, start, count, half=None):
        ref = ow3 if kind == "out" else w3
        base, _ = rows_of(kind, c)
        if half is not None and kind != "out":
            start, count = start + half * (count // 2), count // 2
        at = pl.ds(pl.multiple_of(base + start, 16), count)
        if half is not None and kind == "out":
            return ref.at[s, at, half * (width // 2) : (half + 1) * (width // 2)]
        return ref.at[s, at]

    def piece(kind, c, s, quarter, half=None):
        n = rows_of(kind, c)[1]
        return view(kind, c, s, core * (n // 2) + quarter * (n // 8), n // 8, half)

    def others():
        return [(d - 1, (me + d) % shards) for d in range(1, shards)]

    def copy1(kind, c):
        n = rows_of(kind, c)[1]
        base = rows_of(kind, c)[0]
        src = (ow_ref if kind == "out" else wt_ref).at[
            pl.ds(pl.multiple_of(base + core * (n // 2) + quarter * (n // 8), 16), n // 8)
        ]
        k = c % 8
        return [
            remote(src, piece(kind, c, me, quarter), sz.at[k, d - 1], rz.at[k, d - 1], place.shard_peer(d))
            for d in range(1, shards)
        ]

    def copy2(kind, c):
        k = c % 8
        return [
            remote(piece(kind, c, s, quarter), piece(kind, c, s, quarter), s2.at[k, i, d], r2.at[k, i, d], peer)
            for d, s in others()
            for i, peer in enumerate((place.a_peer, place.b_peer))
        ]

    def copy3(kind, c):
        k = c % 8
        from_a, from_b = 2 * (1 - a) + b, 2 * a + 1 - b
        return [
            remote(
                piece(kind, c, s, origin, i), piece(kind, c, s, origin, i), s3.at[k, i, d], r3.at[k, i, d], peer
            )
            for d, s in others()
            for i, (origin, peer) in enumerate(((from_a, place.b_peer), (from_b, place.a_peer)))
        ]

    def copy4(kind, c):
        k = c % 8
        n = rows_of(kind, c)[1]
        return [
            remote(
                view(kind, c, s, core * (n // 2), n // 2), view(kind, c, s, core * (n // 2), n // 2),
                s4.at[k, d], r4.at[k, d], place.core_peer,
            )
            for d, s in others()
        ]

    def load(kind, c, back=False):
        k = c % 2
        base, n = rows_of(kind, c)
        if kind == "bc":
            n = total_rows - base
        full, own, buf = (ow3, ow_ref, owbuf) if kind == "out" else (w3, wt_ref, wbuf)
        at = pl.ds(pl.multiple_of(base, LANES), n)
        mine = buf.at[k, me, pl.ds(0, n)]
        if back:
            return [pltpu.make_async_copy(mine, full.at[me, at], lc.at[k])]
        copies = [pltpu.make_async_copy(own.at[at], mine, lw.at[k, 0])]
        for d, s in others():
            copies.append(pltpu.make_async_copy(full.at[s, at], buf.at[k, s, pl.ds(0, n)], lw.at[k, 1 + d]))
        return copies

    def at_chunk(c, run):
        @pl.when(c == 0)
        def _():
            run("bc", 0)

        @pl.when((c >= 1) & (c < n_mix))
        def _():
            run("in", c)

        @pl.when((c >= n_mix) & (c < chunks))
        def _():
            run("out", c)

    def tails():
        return [
            remote(
                wt_ref.at[tail_at:total_rows], w3.at[me, tail_at:total_rows], st.at[d - 1], rt.at[d - 1],
                place.shard_peer(d),
            )
            for d in range(1, shards)
        ]

    def packs():
        return [
            remote(pack_ref, pk.at[me], sp.at[d - 1], rp.at[d - 1], place.shard_peer(d)) for d in range(1, shards)
        ]

    def early(i):
        src, dst = ((normt, normt_out), (lowt, lowt_out))[i]
        return [pltpu.make_async_copy(src, dst, se.at[i])]

    def fetch():
        return [
            pltpu.make_async_copy(hidden_hbm, hidden_ref, si.at[0]),
            pltpu.make_async_copy(cot_hbm, cot_ref, si.at[1]),
        ]

    def start(copies):
        for copy in copies:
            copy.start()

    def finish(copies):
        for copy in copies:
            copy.wait()

    def stage5(kind, c):
        finish(copy4(kind, c))
        start(load(kind, c))

    def stage4(kind, c):
        finish(copy3(kind, c))
        start(copy4(kind, c))

    def stage3(kind, c):
        finish(copy2(kind, c))
        start(copy3(kind, c))

    def stage2(kind, c):
        finish(copy1(kind, c))
        start(copy2(kind, c))

    def stage1(kind, c):
        start(copy1(kind, c))

    @pl.when(step == 0)
    def _():
        place.greet()
        stage1("bc", 0)
        start(fetch())
        pack32[...] = jnp.zeros_like(pack32)
        pack32[:CONV, : cw_ref.shape[1]] = cw_ref[...].astype(F32)
        for i, ref in enumerate((cb_ref, gain_ref, ngain_ref, alog_ref, skip_ref, dtb_ref)):
            n = ref.shape[0]
            pack32[CONV + i : CONV + i + 1, :n] = ref[...].astype(F32).reshape(1, n)
        pack_ref[...] = pack32[...].astype(BF)
        pk[me] = pack_ref[...]
        wbuf[0, :, total_rows - 2 * inner :] = jnp.zeros(
            (shards, 4 * LANES - (total_rows - 2 * inner), depth), BF
        )
        ssq[...] = jnp.zeros_like(ssq)
        acc[...] = jnp.zeros_like(acc)
        small_out[...] = jnp.zeros_like(small_out)

    @pl.when(step == 4)
    def _():
        finish(tails())

    at_chunk(step - 7, lambda kind, c: finish(load(kind, c, True)))
    for run, after in ((stage3, 3), (stage4, 4), (stage2, 1), (stage1, -1), (stage5, 5)):
        at_chunk(step - after, run)

    @pl.when(step == 1)
    def _():
        start(packs())

    @pl.when(step == 2)
    def _():
        start(tails())

    @pl.when(step == 3)
    def _():
        finish(packs() + fetch())
        conv_n, gain_n, heads_n = CONV_CH // shards, inner // shards, HEADS // shards
        for s in range(shards):
            part = pk[s].astype(F32)
            small_out[0 : CONV + 1, s * conv_n : (s + 1) * conv_n] = part[0 : CONV + 1, :conv_n]
            small_out[ROW_GAIN : ROW_GAIN + 1, s * gain_n : (s + 1) * gain_n] = part[5:6, :gain_n]
            small_out[ROW_NORM : ROW_NORM + 1, s * depth : (s + 1) * depth] = part[6:7, :depth]
            for i in range(3):
                small_out[ROW_ALOG + i : ROW_ALOG + i + 1, s * heads_n : (s + 1) * heads_n] = part[
                    7 + i : 8 + i, :heads_n
                ]
        hid = hidden_ref[...].astype(F32)
        scale = lax.rsqrt(jnp.mean(hid * hid, axis=1, keepdims=True) + EPS)
        normed = hid * scale * small_out[ROW_NORM : ROW_NORM + 1, :width]
        for s in range(shards):
            normed3[s] = normed[:, s * depth : (s + 1) * depth].astype(BF)
        normt[...] = normed.T.astype(BF)
        start(early(0))
        seg = jnp.broadcast_to(seg_row[...], (LANES, rows)).astype(F32)
        segc_out[...] = seg.T.astype(jnp.int32)

    def arrive(kind, c):
        finish(load(kind, c))
        start(load(kind, c, True))

    c = step - 6
    masks = lambda: [mask_out[k - 1] for k in range(1, CONV)]

    def project(k):
        return sum(mm_t(normed3[s], wbuf[k, s]) for s in range(shards))

    @pl.when(c == 0)
    def _():
        arrive("bc", 0)
        proj_out[...] = project(0)
        outs = (b_out, c_out, cbt_out, dt_out, cum_out, cumt_out, mask_out)
        end = slice(inner, inner + 2 * LANES)
        forward_setup(
            proj_out[:, : 2 * LANES], proj_out[:, 2 * LANES : 3 * LANES], segc_out[...], seg_row[...],
            small_out[:CONV, end], small_out[ROW_BIAS : ROW_BIAS + 1, end],
            small_out[ROW_ALOG : ROW_ALOG + 1, :LANES], small_out[ROW_DTB : ROW_DTB + 1, :LANES],
            outs, cb_scr, dt2, cum3,
        )

    def pairs(j, first):
        def one(p, carry):
            pair = j * per + p
            cols = pl.ds(pl.multiple_of(p * LANES, LANES), LANES)
            at = pl.ds(pl.multiple_of(pair * LANES, LANES), LANES)
            y, g = forward_pair(
                pair, zbuf[:, cols], xbuf[:, cols], small_out[:CONV, at], small_out[ROW_BIAS : ROW_BIAS + 1, at],
                small_out[ROW_SKIP : ROW_SKIP + 1, :LANES], masks(), dt2, cum3, cumt_out, cb_scr,
            )
            y_out[:, cols] = y
            gated[pair] = g
            ssq[...] += g * g
            return carry

        lax.fori_loop(first, first + per // 2, one, 0)

    @pl.when((c >= 3) & (c <= n_mix) & (c % 2 == 1))
    def _():
        pairs((c - 3) // 2, per // 2)

    is_in = (c >= 1) & (c < n_mix)

    @pl.when(is_in & (c % 2 == 1))
    def _():
        arrive("in", c)
        value = project(c % 2)
        proj_out[...] = value
        xbuf[...] = value

    @pl.when(is_in & (c % 2 == 0))
    def _():
        arrive("in", c)
        value = project(c % 2)
        proj_out[...] = value
        zbuf[...] = value
        pairs((c - 2) // 2, 0)

    @pl.when(c == n_mix)
    def _():
        mean = jnp.sum(ssq[...], axis=1, keepdims=True) * (1.0 / inner)
        r = jnp.broadcast_to(lax.rsqrt(mean + EPS), (rows, LANES))
        r_out[...] = r

        def write(i, carry):
            cols = pl.ds(pl.multiple_of(i * LANES, LANES), LANES)
            value = gated[i] * r * small_out[ROW_GAIN : ROW_GAIN + 1, cols]
            low[:, cols] = value.astype(BF)
            lowt[cols, :] = value.T.astype(BF)
            return carry

        lax.fori_loop(0, inner // LANES, write, 0)
        start(early(1))

    @pl.when((c >= n_mix) & (c < chunks))
    def _():
        arrive("out", c)
        part = owbuf[c % 2].reshape(shards * LANES, width)
        lows = [
            low[:, pl.ds(pl.multiple_of(s * (inner // shards) + (c - n_mix) * LANES, LANES), LANES)]
            for s in range(shards)
        ]
        acc[...] += mm(jnp.concatenate(lows, axis=1), part)
        grads = mm_t(cot_ref[...], part)
        for s in range(shards):
            dg_out[s] = grads[:, s * LANES : (s + 1) * LANES]

    @pl.when(c == chunks - 1)
    def _():
        added = acc[...]
        mixed_out[...] = (hidden_ref[...].astype(F32) + added).astype(BF)
        dots = jnp.sum(cot_ref[...].astype(F32) * added, axis=1, keepdims=True)
        r = r_out[...]
        rd_out[...] = r * r * (dots * (1.0 / inner))
        finish(early(0) + early(1))


def mixer_forward(hidden, cotangent, seg_ids, wt, ow, singles, rep, shards):
    rows, width = hidden.shape
    depth = width // shards
    inner = ow.shape[0] * shards
    blocks = inner // (4 * LANES)
    n_out = ow.shape[0] // LANES
    n_mix = 1 + 2 * blocks
    n_in = -(-wt.shape[0] // (4 * LANES))
    steps = n_mix + n_out + 7
    pack = (16, -(-singles[1].shape[0] // LANES) * LANES)
    f = lambda *s: jax.ShapeDtypeStruct(s, F32)
    h = lambda *s: jax.ShapeDtypeStruct(s, BF)
    vm = pltpu.VMEM
    dma = lambda *s: pltpu.SemaphoreType.DMA(s)
    anywhere = pl.BlockSpec(memory_space=pl.ANY)
    const = lambda shape: pl.BlockSpec(shape, lambda i: (0,) * len(shape), pipeline_mode=pl.Buffered(1))
    fixed = lambda shape: pl.BlockSpec(shape, lambda i: (0,) * len(shape))

    def proj_at(i):
        c = jnp.clip(i - 6, 0, n_mix - 1)
        return (0, jnp.where(c == 0, 2 * blocks, (c % 2) * blocks + (c - 1) // 2))

    def y_at(i):
        return (0, jnp.clip((i - 8) // 2, 0, blocks - 1))

    out_shape = [
        h(shards, wt.shape[0], depth), h(shards, *ow.shape), f(rows, n_in * 4 * LANES), f(rows, inner),
        h(inner, rows), f(rows, LANES), f(rows, LANES), f(rows, LANES), f(rows, rows), f(rows, LANES),
        f(rows, LANES), f(LANES, rows), f(CONV - 1, rows, LANES), h(width, rows), f(16, CONV_CH), h(rows, width),
        f(rows, LANES), jax.ShapeDtypeStruct((rows, LANES), jnp.int32), f(shards, rows, inner // shards),
    ]
    block = (rows, 4 * LANES)
    out_specs = [anywhere, anywhere, pl.BlockSpec(block, proj_at), pl.BlockSpec(block, y_at)] + [
        anywhere if s.dtype == BF and s.shape[1] == rows else fixed(s.shape) for s in out_shape[4:-1]
    ]
    out_specs.append(pl.BlockSpec((shards, rows, LANES), lambda i: (0, 0, jnp.clip(i - 6 - n_mix, 0, n_out - 1))))
    n = shards - 1
    return pl.pallas_call(
        functools.partial(forward_kernel, rep=rep, shards=shards, blocks=blocks, n_out=n_out),
        grid=(steps,),
        in_specs=[
            anywhere, anywhere, const((1, rows)), anywhere, anywhere, *(const(v.shape) for v in singles),
        ],
        out_specs=out_specs,
        out_shape=out_shape,
        scratch_shapes=[
            vm((shards, rows, depth), BF), vm((width, rows), BF), vm((inner, rows), BF), vm(pack, F32), vm(pack, BF), vm((shards, *pack), BF), vm((2, shards, 4 * LANES, depth), BF),
            vm((2, shards, LANES, width), BF), vm(block, F32), vm(block, F32), vm((rows, rows), F32), vm((rows, 2 * LANES), BF),
            vm((rows, 3 * LANES), BF), vm((inner // LANES, rows, LANES), F32), vm((rows, LANES), F32),
            vm((rows, inner), BF), vm((rows, width), F32),
            dma(8, n), dma(8, n), dma(8, 2, n), dma(8, 2, n), dma(8, 2, n), dma(8, 2, n), dma(8, n), dma(8, n),
            dma(2, shards), dma(n), dma(n), dma(n), dma(n), dma(2), dma(2), vm((rows, width), BF), vm((rows, width), BF), dma(2),
        ],
        compiler_params=pltpu.CompilerParams(
            vmem_limit_bytes=VMEM_LIMIT, collective_id=1, has_side_effects=True
        ),
        name="mixer_forward",
    )(hidden, cotangent, seg_ids, wt, ow, *singles)


def chunk_at(j, blocks):
    return jnp.where(j < 2 * blocks, j // 2 + blocks * (j % 2), j)


def first_over_shards(c):
    return c % 3 == 1


def stage_steps(bits):
    more = list(range(1, bits - 1))
    n = len(more)
    rep_first = [0, 1, 2, 4, 6] + [6 + i for i in more] + [8 + n, 9 + n, 11 + n, 12 + n]
    shard_first = [0, 1, 3, 5, 7] + [7 + i for i in more] + [8 + n, 9 + n, 10 + n, 12 + n]
    return rep_first, shard_first


def reduce_kernel(*refs, rep, shards, q, blocks, n_out, n_in, tail):
    (
        z_ref, x_ref, y_ref, dgn_ref, bc_ref, dtraw_ref, r_ref, rd_ref, b_ref, c_ref, cbt_ref, dt_ref, cum_ref,
        cumt_ref, mask_ref, seg_col, seg_row, par_ref, w_ref, low_hbm, cot_ref, normed_hbm, hidden_hbm,
        gin_out, gout_out, gh_out, norm_out,
        dt2, cum3, g_scr, dcum, ddt, dp, dn, gh_buf, inv, dots, ag, agt, small, small_rows, slots_norm,
        s5, r5, s6, r6, l7, s7, r7, xtra, sx, rx, sn, rn, sgh, low_t, normed_t, hidden_ref, si,
    ) = refs[:59]
    levels = refs[59:]
    bits = shards.bit_length() - 1
    last = 3 + bits
    keep, send, land, ssem, rsem = (dict(zip(range(1, last + 1), levels[i::5])) for i in range(5))

    step = pl.program_id(0)
    place = Place(rep, shards)
    rows = z_ref.shape[0]
    tile = z_ref.shape[1]
    mix_steps = dp.shape[2] * blocks // tile * 2
    chunks = n_out + n_in
    a, b, core, me, quarter = place.a, place.b, place.core, place.me, place.quarter

    norm = SmallSum(place, norm_out, slots_norm, sn, rn)

    def fetch(i):
        src, dst = ((low_hbm, low_t), (normed_hbm, normed_t), (hidden_hbm, hidden_ref))[i]
        return pltpu.make_async_copy(src, dst, si.at[i])

    @pl.when(step == 1)
    def _():
        fetch(1).wait()
        fetch(2).wait()

    @pl.when(step == 0)
    def _():
        for i in range(3):
            fetch(i).start()
        place.greet()
        norm_out[...] = jnp.zeros_like(norm_out)
        small[6:7, :LANES] = jnp.zeros((1, LANES), F32)
        dn[...] = jnp.zeros_like(dn)
        hi, lo = pieces(dt_ref[...], 2)
        dt2[:, :LANES] = hi
        dt2[:, LANES:] = lo
        for i, part in enumerate(pieces(cum_ref[...], 3)):
            cum3[:, i * LANES : (i + 1) * LANES] = part
        g_scr[...] = jnp.zeros_like(g_scr)
        dcum[...] = jnp.zeros_like(dcum)
        ddt[...] = jnp.zeros_like(ddt)
        fetch(0).wait()

    def halving(shard_first, level):
        at = level - 2
        if shard_first != (at >= 2):
            j = at if shard_first else at - 2
            if j < bits:
                bit, peer = place.shard_bit(j)
                return [(shards >> (j + 1), 4 * q if shard_first else q, bit, peer)] * 2
        n = 1 if shard_first else shards
        turn = at - bits if shard_first else at
        by_a, by_b = (a, place.a_peer), (b, place.b_peer)
        if turn == 0:
            return [(n, 2 * q, *by_a), (2 * n, q, *by_b)]
        return [(n, q, *by_b), (n, q, *by_a)]

    def copies(shard_first, level, c):
        k, w = c % keep[level].shape[0], c % land[level].shape[0]
        peers = [place.core_peer] * 2 if level == 1 else [part[3] for part in halving(shard_first, level)]
        return [
            remote(
                send[level].at[k, o], land[level].at[w, o], ssem[level].at[k, o], rsem[level].at[w, o], peers[o]
            )
            for o in range(2)
        ]

    def start(group):
        for copy in group:
            copy.start()

    def finish(group):
        for copy in group:
            copy.wait()

    def block(g, quarter):
        return ag.at[g, :, pl.ds(pl.multiple_of(quarter * q, q), q)]

    def half_block(g, o, quarter):
        return ag.at[g, o, pl.ds(pl.multiple_of(quarter * q, q), q)]

    def copy5(g):
        mine = block(g, quarter)
        return [
            remote(mine, mine, s5.at[g, i], r5.at[g, i], peer) for i, peer in enumerate((place.a_peer, place.b_peer))
        ]

    def copy6(g):
        from_a = half_block(g, 0, 2 * (1 - a) + b)
        from_b = half_block(g, 1, 2 * a + 1 - b)
        return [
            remote(from_a, from_a, s6.at[g, 0], r6.at[g, 0], place.b_peer),
            remote(from_b, from_b, s6.at[g, 1], r6.at[g, 1], place.a_peer),
        ]

    def targets(c, is_out):
        if is_out:
            cols = pl.ds(pl.multiple_of(c * 2 * LANES + core * LANES, LANES), LANES)
            return [gout_out.at[pl.ds(o * 4 * q, 4 * q), cols] for o in range(2)]
        base = chunk_at(c - n_out, blocks) * 4 * LANES + core * 2 * LANES
        return [gin_out.at[pl.ds(pl.multiple_of(base + o * LANES, LANES), LANES)] for o in range(2)]

    def copy7(c, is_out):
        g, t = c % ag.shape[0], c % agt.shape[0]
        ends = targets(c, is_out)
        own = [ag.at[g, o] if is_out else agt.at[t, o] for o in range(2)]
        local = [pltpu.make_async_copy(own[o], ends[o], l7.at[g, o]) for o in range(2)]
        return local + [remote(own[o], ends[o], s7.at[g, o], r7.at[g, o], place.core_peer) for o in range(2)]

    def by_target(c, run):
        for is_out in (True, False):

            @pl.when((c < n_out) == is_out)
            def _(is_out=is_out):
                run(is_out)

    def stage_first(c):
        @pl.when(c < n_out)
        def _():
            base = c * 2 * LANES
            for s in range(shards):
                lhs = low_t[s * 8 * q : (s + 1) * 8 * q, :]
                for side, ref in ((core, keep[1]), (1 - core, send[1])):
                    cols = pl.ds(pl.multiple_of(base + side * LANES, LANES), LANES)
                    grad = mm(lhs, cot_ref[:, cols])
                    for o in range(2):
                        ref[0, o, s * 4 * q : (s + 1) * 4 * q] = grad[o * 4 * q : (o + 1) * 4 * q].astype(ref.dtype)

        @pl.when(c >= n_out)
        def _():
            n = chunk_at(c - n_out, blocks)
            for s in range(shards):
                own = slice(s * 4 * q, (s + 1) * 4 * q)
                for side, ref in ((core, keep[1]), (1 - core, send[1])):
                    cols = pl.ds(pl.multiple_of(side * 2 * LANES, 2 * LANES), 2 * LANES)
                    grad = mm(normed_t[own, :], dp[n, :, cols])
                    for o in range(2):
                        ref[0, o, own] = grad[:, o * LANES : (o + 1) * LANES].astype(ref.dtype)

        for side, ref in ((1, keep[1]), (0, send[1])):

            @pl.when((c == chunks - 1) & (core == side))
            def _(ref=ref):
                for s in range(shards):
                    at = s * 4 * q
                    ref[0, 1, at : at + small_rows.shape[1]] = small_rows[s].astype(ref.dtype)

        start(copies(False, 1, c))

    def stage_halve(shard_first, level, c):
        finish(copies(shard_first, level - 1, c))
        k0, w0 = c % keep[level - 1].shape[0], c % land[level - 1].shape[0]
        k = c % keep[level].shape[0]
        for o, (runs, size, bit, _) in enumerate(halving(shard_first, level)):

            def part(u, carry, o=o, size=size, bit=bit):
                own = pl.ds(pl.multiple_of((2 * u + bit) * size, size), size)
                other = pl.ds(pl.multiple_of((2 * u + 1 - bit) * size, size), size)
                end = pl.ds(pl.multiple_of(u * size, size), size)
                keep[level][k, o, end] = keep[level - 1][k0, o, own] + land[level - 1][w0, o, own].astype(F32)
                send[level][k, o, end] = (
                    keep[level - 1][k0, o, other] + land[level - 1][w0, o, other].astype(F32)
                ).astype(BF)
                return carry

            if runs == 1:
                part(0, 0)
            else:
                lax.fori_loop(0, runs, part, 0)
        start(copies(shard_first, level, c))

    def stage_total(shard_first, c):
        finish(copies(shard_first, last, c))
        k, w, g = c % keep[last].shape[0], c % land[last].shape[0], c % ag.shape[0]
        total = keep[last][k] + land[last][w].astype(F32)
        for i, peer in enumerate(place.extra):
            keep[last][k] = total
            copy = remote(keep[last].at[k], xtra.at[c % 2, i], sx.at[c % 2, i], rx.at[c % 2, i], peer)
            copy.start()
            copy.wait()
            total = total + xtra[c % 2, i]
        for o in range(2):
            ag[g, o, pl.ds(pl.multiple_of(quarter * q, q), q)] = total[o].astype(BF)
        start(copy5(g))

    def stage_forward(c):
        g = c % ag.shape[0]
        for copy in copy5(g):
            copy.wait_recv()
        start(copy6(g))

    def stage_out(c):
        g, t = c % ag.shape[0], c % agt.shape[0]
        for copy in copy6(g):
            copy.wait_recv()

        def run(is_out):
            if not is_out:
                for o in range(2):
                    agt[t, o] = ag[g, o].astype(F32).T.astype(BF)
            start(copy7(c, is_out))

        by_target(c, run)

    def stage_end(c):
        by_target(c, lambda is_out: finish(copy7(c, is_out)))
        g = c % ag.shape[0]
        for copy in copy5(g) + copy6(g):
            copy.wait_send()

    plans = stage_steps(bits)

    def run_stage(number):
        for shard_first in (False, True):
            c = step - plans[shard_first][number - 1]

            @pl.when((c >= 0) & (c < chunks) & (first_over_shards(c) == shard_first))
            def _(c=c, shard_first=shard_first):
                if number == 1:
                    stage_first(c)
                elif number <= last:
                    stage_halve(shard_first, number, c)
                elif number == last + 1:
                    stage_total(shard_first, c)
                else:
                    (stage_forward, stage_out, stage_end)[number - last - 2](c)

    order = [5, 6, 8, 9, 7, 2, 4, 1, 3]
    for number in order + list(range(10, last + 5)):
        run_stage(number)

    masks = lambda: [mask_ref[k - 1] for k in range(1, CONV)]

    def pairs(first, count):
        def one(p, carry):
            pair = step // 2 * (tile // LANES) + p
            cols = pl.ds(pl.multiple_of(p * LANES, LANES), LANES)
            at = pl.ds(pl.multiple_of(pair * LANES, LANES), LANES)
            skip = skip_lanes(par_ref[ROW_SKIP : ROW_SKIP + 1, :LANES], head_of_lane(pair))
            res = backward_pair(
                pair, z_ref[:, cols], x_ref[:, cols], y_ref[:, cols], dgn_ref[0, :, cols], r_ref[...], rd_ref[...],
                par_ref[:CONV, at], par_ref[ROW_BIAS : ROW_BIAS + 1, at], skip, par_ref[ROW_GAIN : ROW_GAIN + 1, at],
                masks(), dt2, cum3, cumt_ref, cbt_ref, g_scr, dcum, ddt,
            )
            end = pl.ds(pl.multiple_of(pair % 4 * LANES, LANES), LANES)
            dp[pair // 4, :, end] = res[0]
            dp[blocks + pair // 4, :, end] = res[1]
            for k in range(CONV):
                small[k : k + 1, at] = res[4][k]
            small[4:5, at] = res[5]
            small[5:6, at] = res[2]
            per_head = jnp.concatenate(pieces(jnp.broadcast_to(res[3], (8, LANES)), 3), axis=1)
            small[6:7, :LANES] += mm_t(per_head, jnp.concatenate([head_of_lane(pair)] * 3, axis=1))[0:1]
            return carry

        lax.fori_loop(first, first + count, one, 0)

    @pl.when((step < mix_steps) & (step % 2 == 0))
    def _():
        pairs(0, 1)

    @pl.when((step < mix_steps) & (step % 2 == 1))
    def _():
        pairs(1, tile // LANES - 1)

    @pl.when(step == mix_steps - 1)
    def _():
        end = slice(INNER, INNER + 2 * LANES)
        d_bc, d_raw, d_weight, d_bias, d_alog, d_dtb = backward_tail(
            bc_ref, dtraw_ref, b_ref, c_ref, dt_ref, masks(), seg_col, seg_row, par_ref[:CONV, end],
            par_ref[ROW_BIAS : ROW_BIAS + 1, end], par_ref[ROW_ALOG : ROW_ALOG + 1, :LANES],
            par_ref[ROW_DTB : ROW_DTB + 1, :LANES], g_scr, dcum, ddt,
        )
        for i in range(2):
            cols = slice(i * LANES, (i + 1) * LANES)
            dp[2 * blocks, :, cols] = d_bc[i].astype(BF)
            end = slice(INNER + i * LANES, INNER + (i + 1) * LANES)
            for k in range(CONV):
                small[k : k + 1, end] = d_weight[i][k]
            small[4:5, end] = d_bias[i]
        dp[2 * blocks, :, 2 * LANES : 3 * LANES] = d_raw.astype(BF)
        dp[2 * blocks, :, 3 * LANES :] = jnp.zeros((rows, LANES), BF)
        small[5:6, INNER : INNER + LANES] = d_alog
        small[5:6, INNER + LANES :] = d_dtb
        for s in range(shards):
            for at, (row, lane) in enumerate(small_tiles(s, shards)):
                small_rows[s, at : at + 1, :] = small[row : row + 1, lane : lane + LANES]

    @pl.when((step >= n_out) & (step < chunks - 1))
    def _():
        grad = dp[chunk_at(step - n_out, blocks)]
        for s in range(shards):
            dn[s] += mm(grad, w_ref[s])

    @pl.when(step == chunks - 1)
    def _():
        grad = dp[n_in - 1]
        keep_rows = iota(w_ref.shape[1:], 0) < tail
        for s in range(shards):
            dn[s] += mm(grad, jnp.where(keep_rows, w_ref[s], 0))

    wide_cols = gh_buf.shape[2]
    together = wide_cols // dn.shape[2]
    n_parts = shards // together

    def norm_part(i):
        cols = slice(i * wide_cols, (i + 1) * wide_cols)
        d_normed = jnp.concatenate([dn[s] for s in range(i * together, (i + 1) * together)], axis=1)
        unit = hidden_ref[:, cols].astype(F32) * inv[:, :1]
        return cols, d_normed, unit, d_normed * par_ref[ROW_NORM : ROW_NORM + 1, cols]

    def first_pass(i):
        cols, d_normed, unit, du = norm_part(i)
        grad_norm = jnp.sum(d_normed * unit, axis=0, keepdims=True)
        for j in range(wide_cols // LANES):
            at = i * (wide_cols // LANES) + j
            norm_out[at : at + 1, :] = grad_norm[:, j * LANES : (j + 1) * LANES]
        dots[...] += jnp.sum(du * unit, axis=1, keepdims=True) * (1.0 / hidden_ref.shape[1])

    def gh_copy(i):
        return pltpu.make_async_copy(
            gh_buf.at[i % 2], gh_out.at[:, i * wide_cols : (i + 1) * wide_cols], sgh.at[i % 2]
        )

    def second_pass(i):
        if i >= 2:
            gh_copy(i - 2).wait()
        cols, _, unit, du = norm_part(i)
        gh_buf[i % 2] = cot_ref[:, cols].astype(F32) + inv[:, :1] * (du - unit * dots[:, :1])
        gh_copy(i).start()

    @pl.when(step == chunks)
    def _():
        hid = hidden_ref[...].astype(F32)
        scale = lax.rsqrt(jnp.mean(hid * hid, axis=1, keepdims=True) + EPS)
        inv[...] = jnp.broadcast_to(scale, inv.shape)
        dots[...] = jnp.zeros_like(dots)
        first_pass(0)

    for i in range(1, n_parts):

        @pl.when(step == chunks + (i + 1) // 2)
        def _(i=i):
            first_pass(i)

    norm_from = chunks + n_parts // 2

    for i in range(n_parts):

        @pl.when(step == norm_from + 1 + i)
        def _(i=i):
            second_pass(i)

    @pl.when(step == norm_from + 1 + n_parts)
    def _():
        for i in range(max(0, n_parts - 2), n_parts):
            gh_copy(i).wait()

    for i in range(norm.stages):

        @pl.when(step == norm_from + i)
        def _(i=i):
            norm.stage(i)


def results_kernel(
    gin_ref, gout_ref, gh_ref, mixed_ref, norm_ref,
    gin_out, gout_out, gh_out, mixed_out, ngain_out, gain_out, cw_out, cb_out, alog_out, skip_out, dtb_out, *, shards
):
    step = pl.program_id(0)
    me = lax.axis_index("shard")
    gin_out[...] = gin_ref[...].astype(F32)
    gout_out[...] = gout_ref[...].astype(F32)
    gh_out[...] = gh_ref[...]
    mixed_out[...] = mixed_ref[...]

    @pl.when(step == pl.num_programs(0) - 1)
    def _():
        conv, gain, heads, ngain = cb_out.shape[0], gain_out.shape[0], alog_out.shape[0], ngain_out.shape[0]
        rows = gin_ref.shape[0]
        small = gin_ref[rows - LANES :, :].astype(F32).T
        norm = jnp.concatenate([norm_ref[i : i + 1, :] for i in range(norm_ref.shape[0])], axis=1)
        for s in range(shards):

            @pl.when(me == s)
            def _(s=s):
                tiles = small_tiles(s, shards)

                def part(row, base, size):
                    at = [i for i, (r, lane) in enumerate(tiles) if r == row and base <= lane < base + max(size, LANES) * shards]
                    flat = jnp.concatenate([small[i : i + 1, :] for i in at], axis=1)
                    first = s * size - (tiles[at[0]][1] - base)
                    return flat[:, first : first + size]

                for k in range(CONV):
                    cw_out[k : k + 1, :] = part(k, 0, conv)
                cb_out[...] = part(CONV, 0, conv).reshape(conv)
                gain_out[...] = part(5, 0, gain).reshape(gain)
                for ref, row, base in ((alog_out, 5, INNER), (dtb_out, 5, INNER + LANES), (skip_out, 6, 0)):
                    i = tiles.index((row, base))
                    ref[...] = small[i : i + 1, s * heads : (s + 1) * heads].reshape(heads)
                ngain_out[...] = norm[:, s * ngain : (s + 1) * ngain].reshape(ngain)


def results(g_in, g_out, grad_hidden, mixed, norm, columns, singles, shards):
    conv_w, conv_b, gain, ngain, a_log = singles[:5]
    depth, width = g_in.shape[1], g_out.shape[1]
    steps = 8
    f = lambda *s: jax.ShapeDtypeStruct(s, F32)
    strip = lambda v: pl.BlockSpec((v.shape[0] // steps, v.shape[1]), lambda i: (i, 0))
    whole = lambda s: pl.BlockSpec(s, lambda i: (0,) * len(s))
    small = [ngain.shape, gain.shape, conv_w.shape, conv_b.shape, a_log.shape, a_log.shape, a_log.shape]
    return pl.pallas_call(
        functools.partial(results_kernel, shards=shards),
        grid=(steps,),
        in_specs=[strip(g_in), strip(g_out), strip(grad_hidden), strip(mixed), whole(norm.shape)],
        out_specs=[strip(g_in), strip(g_out), strip(grad_hidden), strip(mixed), *(whole(s) for s in small)],
        out_shape=[
            f(columns, depth), f(*g_out.shape), f(*grad_hidden.shape), jax.ShapeDtypeStruct(mixed.shape, BF),
            *(f(*s) for s in small),
        ],
        name="results",
    )(g_in, g_out, grad_hidden, mixed, norm)


def mixer_backward_and_sums(saved, hidden, cotangent, seg_ids, rep, shards):
    (w3, ow3, proj, y, low_t, r, b, c, cbt, dt, cum, cumt, mask, normed_t, params, _, rd, seg_col, d_gated) = saved
    rows, width = hidden.shape
    inner = low_t.shape[0]
    depth = width // shards
    wide_block = 4 * LANES
    blocks = inner // wide_block
    n_out = width // (2 * LANES)
    n_in = proj.shape[1] // wide_block
    q = depth // 4
    chunks = n_out + n_in
    bits = shards.bit_length() - 1
    steps = chunks + stage_steps(bits)[0][-1]
    n_small = SmallSum.count(rep, shards)
    n_extra = max(1, n_small - 3 - (shards - 1))
    tile = 3 * LANES
    tiles = inner // tile
    mix = lambda offset: pl.BlockSpec((rows, tile), lambda i: (0, offset + jnp.minimum(i // 2, tiles - 1)))
    a_shard = inner // shards // tile

    def d_gated_at(i):
        at = jnp.minimum(i // 2, tiles - 1)
        return at // a_shard, 0, at % a_shard

    const = lambda shape, at=None: pl.BlockSpec(shape, lambda i: at or (0,) * len(shape), pipeline_mode=pl.Buffered(1))
    f = lambda *s: jax.ShapeDtypeStruct(s, F32)
    h = lambda *s: jax.ShapeDtypeStruct(s, BF)
    vm = pltpu.VMEM
    dma = lambda *s: pltpu.SemaphoreType.DMA(s)
    anywhere = pl.BlockSpec(memory_space=pl.ANY)
    pairs_bc = inner // LANES
    in_specs = [
        mix(0), mix(tiles), mix(0),
        pl.BlockSpec((1, rows, tile), d_gated_at),
        const((rows, 2 * LANES), (0, pairs_bc)), const((rows, LANES), (0, 2 * pairs_bc + 2)),
        const((rows, LANES)), const((rows, LANES)), const((rows, LANES)), const((rows, LANES)),
        const((rows, rows)), const((rows, LANES)), const((rows, LANES)), const((LANES, rows)),
        const((CONV - 1, rows, LANES)), const((rows, LANES)), const((1, rows)), const(params.shape),
        pl.BlockSpec(
            (shards, wide_block, depth), lambda i: (0, chunk_at(jnp.clip(i - n_out, 0, n_in - 1), blocks), 0)
        ),
        anywhere, const((rows, width)), anywhere, anywhere,
    ]
    whole_out = lambda shape: pl.BlockSpec(shape, lambda i: (0,) * len(shape))
    norm_shape = (16, LANES)
    small_height = -(-max(len(small_tiles(s, shards)) for s in range(shards)) // 16) * 16
    scratch = [
        vm((rows, 2 * LANES), BF), vm((rows, 3 * LANES), BF), vm((rows, rows), F32), vm((rows, LANES), F32),
        vm((rows, LANES), F32), vm((n_in, rows, wide_block), BF), vm((shards, rows, depth), F32), vm((2, rows, tile), F32), vm((rows, LANES), F32), vm((rows, LANES), F32),
        vm((8, 2, 4 * q, LANES), BF), vm((4, 2, LANES, 4 * q), BF),
        vm((8, CONV_CH), F32), vm((shards, small_height, LANES), F32), vm((n_small, *norm_shape), F32),
        dma(8, 2), dma(8, 2), dma(8, 2), dma(8, 2), dma(8, 2), dma(8, 2), dma(8, 2),
        vm((2, n_extra, 2, q, LANES), F32), dma(2, n_extra), dma(2, n_extra),
        dma(n_small), dma(n_small), dma(2),
        vm((inner, rows), BF), vm((width, rows), BF), vm((rows, width), BF), dma(3),
    ]
    for level in range(1, 4 + bits):
        own, landing = {1: (1, 2), 2: (3, 8)}.get(level, (4, 8))
        shape = (2, (shards * 4 * q) >> (level - 1), LANES)
        scratch += [
            vm((own, *shape), F32), vm((own, *shape), BF), vm((landing, *shape), BF), dma(own, 2), dma(landing, 2),
        ]
    return pl.pallas_call(
        functools.partial(
            reduce_kernel, rep=rep, shards=shards, q=q, blocks=blocks, n_out=n_out, n_in=n_in,
            tail=w3.shape[1] - (n_in - 1) * wide_block,
        ),
        grid=(steps,),
        in_specs=in_specs,
        out_specs=[anywhere, anywhere, anywhere, whole_out(norm_shape)],
        out_shape=[
            h(n_in * wide_block, depth), h(inner // shards, width), f(rows, width), f(*norm_shape),
        ],
        scratch_shapes=scratch,
        compiler_params=pltpu.CompilerParams(
            vmem_limit_bytes=VMEM_LIMIT, collective_id=2, has_side_effects=True
        ),
        name="mixer_backward_and_sums",
    )(
        proj, proj, y, d_gated, proj, proj, r, rd, b, c, cbt, dt, cum, cumt, mask, seg_col, seg_ids,
        params, w3, low_t, cotangent, normed_t, hidden,
    )


def per_device(
    hidden, seg_ids, cotangent, in_weight, out_weight, norm_gain, gated_gain, conv_weight, conv_bias, a_log, d_skip,
    dt_bias,
):
    rep, shards = lax.axis_size("rep"), lax.axis_size("shard")
    singles = (conv_weight, conv_bias, gated_gain, norm_gain, a_log, d_skip, dt_bias)
    wt = in_weight.T
    saved = mixer_forward(hidden, cotangent, seg_ids, wt, out_weight, singles, rep, shards)
    mixed = saved[15]
    g_in, g_out, grad_hidden, norm = mixer_backward_and_sums(saved, hidden, cotangent, seg_ids, rep, shards)
    g_in, g_out, grad_hidden, mixed, *small = results(
        g_in, g_out, grad_hidden, mixed, norm, wt.shape[0], singles, shards
    )
    return (mixed, grad_hidden, g_in.T, g_out, *small)


def solution(mesh):
    both = ("rep", "shard")
    shard = P("shard")
    placed = (P(both, None), P(both, None), P(both, None), P("shard", None), P("shard", None), shard, shard,
              P(None, "shard"), shard, shard, shard, shard)
    outs = (P(both, None), P(both, None), P("shard", None), P("shard", None), shard, shard, P(None, "shard"), shard,
            shard, shard, shard)
    return jax.shard_map(per_device, mesh=mesh, in_specs=placed, out_specs=outs, check_vma=False)
```

```python
import functools
import jax
import jax.numpy as jnp
from jax import lax
from jax.experimental import pallas as pl
from jax.experimental.pallas import tpu as pltpu
from jax.sharding import PartitionSpec as P

HEADS = 48
HEAD_DIM = 64
STATE = 128
CONV = 4
INNER = 3072
CONV_CH = 3328
LANES = 128
EPS = 1e-05
LOG2E = 1.4426950408889634
BF = jnp.bfloat16
F32 = jnp.float32
HIGH = lax.Precision.HIGHEST
VMEM_LIMIT = 63 * 2**20
MESH = pl.DeviceIdType.MESH


def mm(a, b):
    return jnp.dot(a, b, preferred_element_type=F32)


def mm_t(a, b):
    return lax.dot_general(a, b, (((1,), (1,)), ((), ())), preferred_element_type=F32)


def pieces(value, count):
    parts = []
    for _ in range(count):
        part = value.astype(BF)
        parts.append(part)
        value = value - part.astype(F32)
    return parts


def iota(shape, dim):
    return lax.broadcasted_iota(jnp.int32, shape, dim)


def head_of_lane(pair):
    heads, lanes = iota((LANES, LANES), 0), iota((LANES, LANES), 1)
    return (heads == 2 * pair + lanes // HEAD_DIM).astype(BF)


def head_columns(cum3, pair):
    heads, lanes = iota((LANES, 2 * LANES), 0), iota((LANES, 2 * LANES), 1)
    pick = (heads == 2 * pair + lanes // LANES).astype(BF)
    cols = mm(cum3[...], jnp.concatenate([pick] * 3, axis=0))
    return cols[:, :LANES], cols[:, LANES:]


def conv_shifts(value, masks):
    return [pltpu.roll(value, k, 0) * masks[k - 1] for k in range(1, CONV)]


def conv_apply(value, shifts, weight, bias):
    total = bias + weight[CONV - 1 : CONV] * value
    for k in range(1, CONV):
        total = total + weight[CONV - 1 - k : CONV - k] * shifts[k - 1]
    return total


def conv_back(d_pre, value, shifts, masks, weight):
    rows = d_pre.shape[0]
    d_value = weight[CONV - 1 : CONV] * d_pre
    d_weight = [jnp.sum(d_pre * value, axis=0, keepdims=True)]
    for k in range(1, CONV):
        d_weight.append(jnp.sum(d_pre * shifts[k - 1], axis=0, keepdims=True))
        d_value = d_value + weight[CONV - 1 - k : CONV - k] * pltpu.roll(
            d_pre * masks[k - 1], rows - k, 0
        )
    d_bias = jnp.sum(d_pre, axis=0, keepdims=True)
    return d_value, d_weight[::-1], d_bias


def silu_parts(value):
    sig = 0.5 * jnp.tanh(0.5 * value) + 0.5
    return sig, value * sig


def silu_slope(sig, silu):
    return sig + silu - silu * sig


def decay(col, row, clamp):
    gap = col - row
    return jnp.exp2(jnp.minimum(gap, 0.0) if clamp else gap)


def wide(col, width):
    return jnp.concatenate([col] * (width // LANES), axis=1)


def backward_pair(
    pair, z, value, y, dgn, r, rd, cw, cb, skip, gain, masks, dt2, cum3, cumt_ref, cbt_ref, g_scr, dcum, ddt
):
    rows = z.shape[0]
    half = rows // 2
    shifts = conv_shifts(value, masks)
    pre = conv_apply(value, shifts, cw, cb)
    sp, x = silu_parts(pre)
    sg, sz = silu_parts(z)
    scanned = y + skip * x
    g = scanned * sz
    dgn_r = dgn * r
    d_gain = jnp.sum(dgn_r * g, axis=0, keepdims=True)
    dg = gain * dgn_r - g * rd
    dz = (dg * scanned * silu_slope(sg, sz)).astype(BF)
    dsc = dg * sz
    d_skip = jnp.sum(dsc * x, axis=0, keepdims=True)
    dy = dsc.astype(BF)
    spread = head_of_lane(pair)
    step = mm(dt2[...], jnp.concatenate([spread, spread], axis=0))
    both = jnp.concatenate([spread, spread], axis=1)
    xt = (x * step).astype(BF)
    first = iota((rows, LANES), 1) < HEAD_DIM
    zero = jnp.zeros_like(xt)
    columns = head_columns(cum3, pair)
    blocks = (
        (slice(0, half), slice(0, half), True),
        (slice(0, half), slice(half, rows), False),
        (slice(half, rows), slice(half, rows), True),
    )
    rows_of = [cumt_ref[pl.ds(2 * pair + side, 1), :] for side in range(2)]
    sides = [jnp.where(first == (side == 0), xt, zero) for side in range(2)]
    parts = [[], []]
    for js, is_, clamp in blocks:
        total = g_scr[js, is_]
        for side in range(2):
            e = decay(rows_of[side][:, is_], wide(columns[side][js], half), clamp)
            parts[side].append(mm((e * cbt_ref[js, is_]).astype(BF), dy[is_]))
            total = total + e * mm_t(sides[side][js], dy[is_])
        g_scr[js, is_] = total
    dxts = [jnp.concatenate([p[0] + p[1], p[2]], axis=0) for p in parts]
    dxt = jnp.where(first, dxts[0], dxts[1])
    for ref, term in ((dcum, dy.astype(F32) * y - xt.astype(F32) * dxt), (ddt, x * dxt)):
        ref[...] += mm_t(jnp.concatenate(pieces(term, 2), axis=1), both)
    dx = skip * dsc + step * dxt
    d_pre = dx * silu_slope(sp, x)
    d_value, d_weight, d_bias = conv_back(d_pre, value, shifts, masks, cw)
    return dz, d_value.astype(BF), d_gain, d_skip, d_weight, d_bias


def backward_tail(
    bc_ref, dtraw_ref, b_ref, c_ref, dt_ref, masks, seg_col, seg_row, cw_bc, cb_bc, alog_ref, bias_ref,
    g_scr, dcum, ddt
):
    rows = dt_ref.shape[0]
    same = wide(seg_col[...], rows) == seg_row[...]
    later = (iota((rows, rows), 0) <= iota((rows, rows), 1)) & same
    gt = jnp.where(later, g_scr[...], 0.0)
    db = jnp.dot(gt, c_ref[...], precision=HIGH, preferred_element_type=F32)
    dc = jnp.dot(gt.T, b_ref[...], precision=HIGH, preferred_element_type=F32)
    d_bc, d_weights, d_biases = [], [], []
    for i, d_out in enumerate((db, dc)):
        cols = slice(i * LANES, (i + 1) * LANES)
        value = bc_ref[:, cols]
        shifts = conv_shifts(value, masks)
        pre = conv_apply(value, shifts, cw_bc[:, cols], cb_bc[:, cols])
        sp, value_out = silu_parts(pre)
        d_pre = d_out * silu_slope(sp, value_out)
        d_value, d_weight, d_bias = conv_back(d_pre, value, shifts, masks, cw_bc[:, cols])
        d_bc.append(d_value)
        d_weights.append(d_weight)
        d_biases.append(d_bias)
    step = dt_ref[...]
    live = iota((rows, LANES), 1) < HEADS
    rate = -jnp.exp(alog_ref)
    later_bf = later.astype(BF)
    dlog = sum(mm(later_bf, part) for part in pieces(dcum[...], 3)[::-1])
    dstep = ddt[...] + dlog * rate
    raw = jnp.where(live, dtraw_ref[...] + bias_ref, 0.0)
    d_raw = jnp.where(live, dstep / (1.0 + jnp.exp(-raw)), 0.0)
    d_alog = jnp.sum(dlog * step, axis=0, keepdims=True) * rate
    return d_bc, d_raw, d_weights, d_biases, d_alog, jnp.sum(d_raw, axis=0, keepdims=True)


class Place:
    def __init__(self, rep, shards):
        self.rep, self.shards = rep, shards
        r, self.me = lax.axis_index("rep"), lax.axis_index("shard")
        self.r = r
        self.core, self.a, self.b = r % 2, (r // 2) % 2, (r // 4) % 2
        self.core_peer = (r + 1 - 2 * self.core, self.me)
        self.a_peer = (r + 2 - 4 * self.a, self.me)
        self.b_peer = (r + 4 - 8 * self.b, self.me)
        self.extra = []
        stride = 8
        while stride < rep:
            bit = (r // stride) % 2
            self.extra.append((r + stride - 2 * stride * bit, self.me))
            stride *= 2
        self.quarter = 2 * self.a + self.b

    def shard_bit(self, j):
        bit = (self.me // (1 << j)) % 2
        return bit, (self.r, self.me + (1 << j) - (2 << j) * bit)

    def shard_peer(self, distance):
        return (self.r, (self.me + distance) % self.shards)

    def partners(self):
        return [self.core_peer, self.a_peer, self.b_peer, *self.extra] + [
            self.shard_peer(d) for d in range(1, self.shards)
        ]

    def greet(self):
        barrier = pltpu.get_barrier_semaphore()
        partners = self.partners()
        for partner in partners:
            pl.semaphore_signal(barrier, inc=1, device_id=partner, device_id_type=MESH)
        pl.semaphore_wait(barrier, len(partners))


def remote(src, dst, send, recv, device):
    return pltpu.make_async_remote_copy(
        src_ref=src, dst_ref=dst, send_sem=send, recv_sem=recv, device_id=device, device_id_type=MESH
    )


class SmallSum:
    def __init__(self, place, buf, slots, sends, recvs):
        self.buf, self.slots, self.sends, self.recvs = buf, slots, sends, recvs
        pairs = [place.core_peer, place.a_peer, place.b_peer, *place.extra]
        self.groups = [[peer] for peer in pairs] + [[place.shard_peer(d) for d in range(1, place.shards)]]
        self.stages = len(self.groups) + 1

    @staticmethod
    def count(rep, shards):
        return rep.bit_length() - 1 + shards - 1

    def copies(self, group):
        at = sum(len(g) for g in self.groups[:group])
        return [
            remote(self.buf, self.slots.at[at + i], self.sends.at[at + i], self.recvs.at[at + i], peer)
            for i, peer in enumerate(self.groups[group])
        ]

    def stage(self, number):
        if number > 0:
            at = sum(len(g) for g in self.groups[: number - 1])
            copies = self.copies(number - 1)
            for copy in copies:
                copy.wait()
            total = self.buf[...]
            for i in range(len(copies)):
                total = total + self.slots[at + i]
            self.buf[...] = total
        if number < len(self.groups):
            for copy in self.copies(number):
                copy.start()


def small_tiles(s, shards):
    def span(total):
        size = total // shards
        return range(s * size // LANES * LANES, (s + 1) * size, LANES)

    tiles = [(row, lane) for row in range(CONV + 1) for lane in span(CONV_CH)]
    tiles += [(5, lane) for lane in span(INNER)]
    return tiles + [(5, INNER), (5, INNER + LANES), (6, 0)]


def forward_setup(
    bc, raw, seg_col, seg_row, cw, cb, alog, bias, outs, cb_scr, dt2, cum3
):
    b_out, c_out, cbt_out, dt_out, cum_out, cumt_out, mask_out = outs
    rows = raw.shape[0]
    at = iota((rows, LANES), 0)
    for k in range(1, CONV):
        same = (pltpu.roll(seg_col, k, 0) == seg_col) & (at >= k)
        mask_out[k - 1] = same.astype(F32)
    masks = [mask_out[k - 1] for k in range(1, CONV)]
    results = []
    for i in range(2):
        cols = slice(i * LANES, (i + 1) * LANES)
        value = bc[:, cols]
        pre = conv_apply(value, conv_shifts(value, masks), cw[:, cols], cb[:, cols])
        results.append(silu_parts(pre)[1])
    b_out[...] = results[0]
    c_out[...] = results[1]
    products = lax.dot_general(
        results[1], results[0], (((1,), (1,)), ((), ())), precision=HIGH, preferred_element_type=F32
    )
    lower = iota((rows, rows), 0) >= iota((rows, rows), 1)
    allowed = lower & (wide(seg_col, rows) == seg_row)
    products = jnp.where(allowed, products, 0.0)
    cb_scr[...] = products
    cbt_out[...] = products.T
    live = iota((rows, LANES), 1) < HEADS
    raw = jnp.where(live, raw + bias, 0.0)
    step = jnp.where(live, jnp.maximum(raw, 0.0) + jnp.log1p(jnp.exp(-jnp.abs(raw))), 0.0)
    dt_out[...] = step
    hi, lo = pieces(step, 2)
    dt2[:, :LANES] = hi
    dt2[:, LANES:] = lo
    log_rate = step * (-LOG2E * jnp.exp(alog))
    tri = lower.astype(BF)
    cum = sum(mm(tri, part) for part in pieces(log_rate, 3)[::-1])
    cum_out[...] = cum
    cumt_out[...] = cum.T
    for i, part in enumerate(pieces(cum, 3)):
        cum3[:, i * LANES : (i + 1) * LANES] = part


def skip_lanes(skip_row, spread):
    return mm(jnp.broadcast_to(skip_row, (8, LANES)).astype(BF), spread)[0:1]


def forward_pair(pair, z, value, cw, cb, skip_row, masks, dt2, cum3, cumt_ref, cb_scr):
    rows = z.shape[0]
    half = rows // 2
    pre = conv_apply(value, conv_shifts(value, masks), cw, cb)
    x = silu_parts(pre)[1]
    spread = head_of_lane(pair)
    step = mm(dt2[...], jnp.concatenate([spread, spread], axis=0))
    xt = (x * step).astype(BF)
    first = iota((rows, LANES), 1) < HEAD_DIM
    ys = []
    columns = head_columns(cum3, pair)
    for side in range(2):
        head = 2 * pair + side
        col = columns[side]
        row = cumt_ref[pl.ds(head, 1), :]
        low_row, high_row = row[:, :half], row[:, half:]
        top, bottom = wide(col[:half], half), wide(col[half:], half)
        m00 = (decay(top, low_row, True) * cb_scr[:half, :half]).astype(BF)
        m10 = (decay(bottom, low_row, False) * cb_scr[half:, :half]).astype(BF)
        m11 = (decay(bottom, high_row, True) * cb_scr[half:, half:]).astype(BF)
        ys.append(
            jnp.concatenate([mm(m00, xt[:half]), mm(m10, xt[:half]) + mm(m11, xt[half:])], axis=0)
        )
    y = jnp.where(first, ys[0], ys[1])
    g = (y + skip_lanes(skip_row, spread) * x) * silu_parts(z)[1]
    return y, g


ROW_BIAS, ROW_GAIN, ROW_NORM, ROW_ALOG, ROW_SKIP, ROW_DTB = 4, 5, 6, 7, 8, 9


def forward_kernel(
    hidden_hbm, cot_hbm, seg_row, wt_ref, ow_ref, cw_ref, cb_ref, gain_ref, ngain_ref, alog_ref, skip_ref, dtb_ref,
    w3, ow3, proj_out, y_out, lowt_out, r_out, b_out, c_out, cbt_out, dt_out, cum_out, cumt_out, mask_out,
    normt_out, small_out, mixed_out, rd_out, segc_out, dg_out,
    normed3, normt, lowt, pack32, pack_ref, pk, wbuf, owbuf, xbuf, zbuf, cb_scr, dt2, cum3, gated, ssq, low, acc,
    sz, rz, s2, r2, s3, r3, s4, r4, lw, st, rt, sp, rp, lc, se, hidden_ref, cot_ref, si,
    *, rep, shards, blocks, n_out
):
    step = pl.program_id(0)
    place = Place(rep, shards)
    a, b, core, me, quarter = place.a, place.b, place.core, place.me, place.quarter
    rows, width = hidden_hbm.shape
    depth = width // shards
    inner = blocks * 4 * LANES
    per = 4
    n_mix = 1 + 2 * blocks
    chunks = n_mix + n_out
    tail_at = 2 * inner + 2 * LANES
    tail = w3.shape[1] - tail_at
    total_rows = w3.shape[1]

    def rows_of(kind, c):
        if kind == "bc":
            return 2 * inner, 2 * LANES
        if kind == "in":
            j = (c - 1) // 2
            return ((c % 2) * inner + j * 4 * LANES), 4 * LANES
        return (c - n_mix) * LANES, LANES

    def view(kind, c, s, start, count, half=None):
        ref = ow3 if kind == "out" else w3
        base, _ = rows_of(kind, c)
        if half is not None and kind != "out":
            start, count = start + half * (count // 2), count // 2
        at = pl.ds(pl.multiple_of(base + start, 16), count)
        if half is not None and kind == "out":
            return ref.at[s, at, half * (width // 2) : (half + 1) * (width // 2)]
        return ref.at[s, at]

    def piece(kind, c, s, quarter, half=None):
        n = rows_of(kind, c)[1]
        return view(kind, c, s, core * (n // 2) + quarter * (n // 8), n // 8, half)

    def others():
        return [(d - 1, (me + d) % shards) for d in range(1, shards)]

    def copy1(kind, c):
        n = rows_of(kind, c)[1]
        base = rows_of(kind, c)[0]
        src = (ow_ref if kind == "out" else wt_ref).at[
            pl.ds(pl.multiple_of(base + core * (n // 2) + quarter * (n // 8), 16), n // 8)
        ]
        k = c % 8
        return [
            remote(src, piece(kind, c, me, quarter), sz.at[k, d - 1], rz.at[k, d - 1], place.shard_peer(d))
            for d in range(1, shards)
        ]

    def copy2(kind, c):
        k = c % 8
        return [
            remote(piece(kind, c, s, quarter), piece(kind, c, s, quarter), s2.at[k, i, d], r2.at[k, i, d], peer)
            for d, s in others()
            for i, peer in enumerate((place.a_peer, place.b_peer))
        ]

    def copy3(kind, c):
        k = c % 8
        from_a, from_b = 2 * (1 - a) + b, 2 * a + 1 - b
        return [
            remote(
                piece(kind, c, s, origin, i), piece(kind, c, s, origin, i), s3.at[k, i, d], r3.at[k, i, d], peer
            )
            for d, s in others()
            for i, (origin, peer) in enumerate(((from_a, place.b_peer), (from_b, place.a_peer)))
        ]

    def copy4(kind, c):
        k = c % 8
        n = rows_of(kind, c)[1]
        return [
            remote(
                view(kind, c, s, core * (n // 2), n // 2), view(kind, c, s, core * (n // 2), n // 2),
                s4.at[k, d], r4.at[k, d], place.core_peer,
            )
            for d, s in others()
        ]

    def load(kind, c, back=False):
        k = c % 2
        base, n = rows_of(kind, c)
        if kind == "bc":
            n = total_rows - base
        full, own, buf = (ow3, ow_ref, owbuf) if kind == "out" else (w3, wt_ref, wbuf)
        at = pl.ds(pl.multiple_of(base, LANES), n)
        mine = buf.at[k, me, pl.ds(0, n)]
        if back:
            return [pltpu.make_async_copy(mine, full.at[me, at], lc.at[k])]
        copies = [pltpu.make_async_copy(own.at[at], mine, lw.at[k, 0])]
        for d, s in others():
            copies.append(pltpu.make_async_copy(full.at[s, at], buf.at[k, s, pl.ds(0, n)], lw.at[k, 1 + d]))
        return copies

    def at_chunk(c, run):
        @pl.when(c == 0)
        def _():
            run("bc", 0)

        @pl.when((c >= 1) & (c < n_mix))
        def _():
            run("in", c)

        @pl.when((c >= n_mix) & (c < chunks))
        def _():
            run("out", c)

    def tails():
        return [
            remote(
                wt_ref.at[tail_at:total_rows], w3.at[me, tail_at:total_rows], st.at[d - 1], rt.at[d - 1],
                place.shard_peer(d),
            )
            for d in range(1, shards)
        ]

    def packs():
        return [
            remote(pack_ref, pk.at[me], sp.at[d - 1], rp.at[d - 1], place.shard_peer(d)) for d in range(1, shards)
        ]

    def early(i):
        src, dst = ((normt, normt_out), (lowt, lowt_out))[i]
        return [pltpu.make_async_copy(src, dst, se.at[i])]

    def fetch():
        return [
            pltpu.make_async_copy(hidden_hbm, hidden_ref, si.at[0]),
            pltpu.make_async_copy(cot_hbm, cot_ref, si.at[1]),
        ]

    def start(copies):
        for copy in copies:
            copy.start()

    def finish(copies):
        for copy in copies:
            copy.wait()

    def stage5(kind, c):
        finish(copy4(kind, c))
        start(load(kind, c))

    def stage4(kind, c):
        finish(copy3(kind, c))
        start(copy4(kind, c))

    def stage3(kind, c):
        finish(copy2(kind, c))
        start(copy3(kind, c))

    def stage2(kind, c):
        finish(copy1(kind, c))
        start(copy2(kind, c))

    def stage1(kind, c):
        start(copy1(kind, c))

    @pl.when(step == 0)
    def _():
        place.greet()
        stage1("bc", 0)
        start(fetch())
        pack32[...] = jnp.zeros_like(pack32)
        pack32[:CONV, : cw_ref.shape[1]] = cw_ref[...].astype(F32)
        for i, ref in enumerate((cb_ref, gain_ref, ngain_ref, alog_ref, skip_ref, dtb_ref)):
            n = ref.shape[0]
            pack32[CONV + i : CONV + i + 1, :n] = ref[...].astype(F32).reshape(1, n)
        pack_ref[...] = pack32[...].astype(BF)
        pk[me] = pack_ref[...]
        wbuf[0, :, total_rows - 2 * inner :] = jnp.zeros(
            (shards, 4 * LANES - (total_rows - 2 * inner), depth), BF
        )
        ssq[...] = jnp.zeros_like(ssq)
        acc[...] = jnp.zeros_like(acc)
        small_out[...] = jnp.zeros_like(small_out)

    @pl.when(step == 4)
    def _():
        finish(tails())

    at_chunk(step - 7, lambda kind, c: finish(load(kind, c, True)))
    for run, after in ((stage3, 3), (stage4, 4), (stage2, 1), (stage1, -1), (stage5, 5)):
        at_chunk(step - after, run)

    @pl.when(step == 1)
    def _():
        start(packs())

    @pl.when(step == 2)
    def _():
        start(tails())

    @pl.when(step == 3)
    def _():
        finish(packs() + fetch())
        conv_n, gain_n, heads_n = CONV_CH // shards, inner // shards, HEADS // shards
        for s in range(shards):
            part = pk[s].astype(F32)
            small_out[0 : CONV + 1, s * conv_n : (s + 1) * conv_n] = part[0 : CONV + 1, :conv_n]
            small_out[ROW_GAIN : ROW_GAIN + 1, s * gain_n : (s + 1) * gain_n] = part[5:6, :gain_n]
            small_out[ROW_NORM : ROW_NORM + 1, s * depth : (s + 1) * depth] = part[6:7, :depth]
            for i in range(3):
                small_out[ROW_ALOG + i : ROW_ALOG + i + 1, s * heads_n : (s + 1) * heads_n] = part[
                    7 + i : 8 + i, :heads_n
                ]
        hid = hidden_ref[...].astype(F32)
        scale = lax.rsqrt(jnp.mean(hid * hid, axis=1, keepdims=True) + EPS)
        normed = hid * scale * small_out[ROW_NORM : ROW_NORM + 1, :width]
        for s in range(shards):
            normed3[s] = normed[:, s * depth : (s + 1) * depth].astype(BF)
        normt[...] = normed.T.astype(BF)
        start(early(0))
        seg = jnp.broadcast_to(seg_row[...], (LANES, rows)).astype(F32)
        segc_out[...] = seg.T.astype(jnp.int32)

    def arrive(kind, c):
        finish(load(kind, c))
        start(load(kind, c, True))

    c = step - 6
    masks = lambda: [mask_out[k - 1] for k in range(1, CONV)]

    def project(k):
        return sum(mm_t(normed3[s], wbuf[k, s]) for s in range(shards))

    @pl.when(c == 0)
    def _():
        arrive("bc", 0)
        proj_out[...] = project(0)
        outs = (b_out, c_out, cbt_out, dt_out, cum_out, cumt_out, mask_out)
        end = slice(inner, inner + 2 * LANES)
        forward_setup(
            proj_out[:, : 2 * LANES], proj_out[:, 2 * LANES : 3 * LANES], segc_out[...], seg_row[...],
            small_out[:CONV, end], small_out[ROW_BIAS : ROW_BIAS + 1, end],
            small_out[ROW_ALOG : ROW_ALOG + 1, :LANES], small_out[ROW_DTB : ROW_DTB + 1, :LANES],
            outs, cb_scr, dt2, cum3,
        )

    def pairs(j, first):
        def one(p, carry):
            pair = j * per + p
            cols = pl.ds(pl.multiple_of(p * LANES, LANES), LANES)
            at = pl.ds(pl.multiple_of(pair * LANES, LANES), LANES)
            y, g = forward_pair(
                pair, zbuf[:, cols], xbuf[:, cols], small_out[:CONV, at], small_out[ROW_BIAS : ROW_BIAS + 1, at],
                small_out[ROW_SKIP : ROW_SKIP + 1, :LANES], masks(), dt2, cum3, cumt_out, cb_scr,
            )
            y_out[:, cols] = y
            gated[pair] = g
            ssq[...] += g * g
            return carry

        lax.fori_loop(first, first + per // 2, one, 0)

    @pl.when((c >= 3) & (c <= n_mix) & (c % 2 == 1))
    def _():
        pairs((c - 3) // 2, per // 2)

    is_in = (c >= 1) & (c < n_mix)

    @pl.when(is_in & (c % 2 == 1))
    def _():
        arrive("in", c)
        value = project(c % 2)
        proj_out[...] = value
        xbuf[...] = value

    @pl.when(is_in & (c % 2 == 0))
    def _():
        arrive("in", c)
        value = project(c % 2)
        proj_out[...] = value
        zbuf[...] = value
        pairs((c - 2) // 2, 0)

    @pl.when(c == n_mix)
    def _():
        mean = jnp.sum(ssq[...], axis=1, keepdims=True) * (1.0 / inner)
        r = jnp.broadcast_to(lax.rsqrt(mean + EPS), (rows, LANES))
        r_out[...] = r

        def write(i, carry):
            cols = pl.ds(pl.multiple_of(i * LANES, LANES), LANES)
            value = gated[i] * r * small_out[ROW_GAIN : ROW_GAIN + 1, cols]
            low[:, cols] = value.astype(BF)
            lowt[cols, :] = value.T.astype(BF)
            return carry

        lax.fori_loop(0, inner // LANES, write, 0)
        start(early(1))

    @pl.when((c >= n_mix) & (c < chunks))
    def _():
        arrive("out", c)
        part = owbuf[c % 2].reshape(shards * LANES, width)
        lows = [
            low[:, pl.ds(pl.multiple_of(s * (inner // shards) + (c - n_mix) * LANES, LANES), LANES)]
            for s in range(shards)
        ]
        acc[...] += mm(jnp.concatenate(lows, axis=1), part)
        grads = mm_t(cot_ref[...], part)
        for s in range(shards):
            dg_out[s] = grads[:, s * LANES : (s + 1) * LANES]

    @pl.when(c == chunks - 1)
    def _():
        added = acc[...]
        mixed_out[...] = (hidden_ref[...].astype(F32) + added).astype(BF)
        dots = jnp.sum(cot_ref[...].astype(F32) * added, axis=1, keepdims=True)
        r = r_out[...]
        rd_out[...] = r * r * (dots * (1.0 / inner))
        finish(early(0) + early(1))


def mixer_forward(hidden, cotangent, seg_ids, wt, ow, singles, rep, shards):
    rows, width = hidden.shape
    depth = width // shards
    inner = ow.shape[0] * shards
    blocks = inner // (4 * LANES)
    n_out = ow.shape[0] // LANES
    n_mix = 1 + 2 * blocks
    n_in = -(-wt.shape[0] // (4 * LANES))
    steps = n_mix + n_out + 7
    pack = (16, -(-singles[1].shape[0] // LANES) * LANES)
    f = lambda *s: jax.ShapeDtypeStruct(s, F32)
    h = lambda *s: jax.ShapeDtypeStruct(s, BF)
    vm = pltpu.VMEM
    dma = lambda *s: pltpu.SemaphoreType.DMA(s)
    anywhere = pl.BlockSpec(memory_space=pl.ANY)
    const = lambda shape: pl.BlockSpec(shape, lambda i: (0,) * len(shape), pipeline_mode=pl.Buffered(1))
    fixed = lambda shape: pl.BlockSpec(shape, lambda i: (0,) * len(shape))

    def proj_at(i):
        c = jnp.clip(i - 6, 0, n_mix - 1)
        return (0, jnp.where(c == 0, 2 * blocks, (c % 2) * blocks + (c - 1) // 2))

    def y_at(i):
        return (0, jnp.clip((i - 8) // 2, 0, blocks - 1))

    out_shape = [
        h(shards, wt.shape[0], depth), h(shards, *ow.shape), f(rows, n_in * 4 * LANES), f(rows, inner),
        h(inner, rows), f(rows, LANES), f(rows, LANES), f(rows, LANES), f(rows, rows), f(rows, LANES),
        f(rows, LANES), f(LANES, rows), f(CONV - 1, rows, LANES), h(width, rows), f(16, CONV_CH), h(rows, width),
        f(rows, LANES), jax.ShapeDtypeStruct((rows, LANES), jnp.int32), f(shards, rows, inner // shards),
    ]
    block = (rows, 4 * LANES)
    out_specs = [anywhere, anywhere, pl.BlockSpec(block, proj_at), pl.BlockSpec(block, y_at)] + [
        anywhere if s.dtype == BF and s.shape[1] == rows else fixed(s.shape) for s in out_shape[4:-1]
    ]
    out_specs.append(pl.BlockSpec((shards, rows, LANES), lambda i: (0, 0, jnp.clip(i - 6 - n_mix, 0, n_out - 1))))
    n = shards - 1
    return pl.pallas_call(
        functools.partial(forward_kernel, rep=rep, shards=shards, blocks=blocks, n_out=n_out),
        grid=(steps,),
        in_specs=[
            anywhere, anywhere, const((1, rows)), anywhere, anywhere, *(const(v.shape) for v in singles),
        ],
        out_specs=out_specs,
        out_shape=out_shape,
        scratch_shapes=[
            vm((shards, rows, depth), BF), vm((width, rows), BF), vm((inner, rows), BF), vm(pack, F32), vm(pack, BF), vm((shards, *pack), BF), vm((2, shards, 4 * LANES, depth), BF),
            vm((2, shards, LANES, width), BF), vm(block, F32), vm(block, F32), vm((rows, rows), F32), vm((rows, 2 * LANES), BF),
            vm((rows, 3 * LANES), BF), vm((inner // LANES, rows, LANES), F32), vm((rows, LANES), F32),
            vm((rows, inner), BF), vm((rows, width), F32),
            dma(8, n), dma(8, n), dma(8, 2, n), dma(8, 2, n), dma(8, 2, n), dma(8, 2, n), dma(8, n), dma(8, n),
            dma(2, shards), dma(n), dma(n), dma(n), dma(n), dma(2), dma(2), vm((rows, width), BF), vm((rows, width), BF), dma(2),
        ],
        compiler_params=pltpu.CompilerParams(
            vmem_limit_bytes=VMEM_LIMIT, collective_id=1, has_side_effects=True
        ),
        name="mixer_forward",
    )(hidden, cotangent, seg_ids, wt, ow, *singles)


def chunk_at(j, blocks):
    return jnp.where(j < 2 * blocks, j // 2 + blocks * (j % 2), j)


def first_over_shards(c):
    return c % 3 == 1


def stage_steps(bits):
    more = list(range(1, bits - 1))
    n = len(more)
    rep_first = [0, 1, 2, 4, 6] + [6 + i for i in more] + [8 + n, 9 + n, 11 + n, 12 + n]
    shard_first = [0, 1, 3, 5, 7] + [7 + i for i in more] + [8 + n, 9 + n, 10 + n, 12 + n]
    return rep_first, shard_first


def reduce_kernel(*refs, rep, shards, q, blocks, n_out, n_in, tail):
    (
        z_ref, x_ref, y_ref, dgn_ref, bc_ref, dtraw_ref, r_ref, rd_ref, b_ref, c_ref, cbt_ref, dt_ref, cum_ref,
        cumt_ref, mask_ref, seg_col, seg_row, par_ref, w_ref, low_hbm, cot_ref, normed_hbm, hidden_hbm,
        gin_out, gout_out, gh_out, norm_out,
        dt2, cum3, g_scr, dcum, ddt, dp, dn, gh_buf, inv, dots, ag, agt, small, small_rows, slots_norm,
        s5, r5, s6, r6, l7, s7, r7, xtra, sx, rx, sn, rn, sgh, low_t, normed_t, hidden_ref, si,
    ) = refs[:59]
    levels = refs[59:]
    bits = shards.bit_length() - 1
    last = 3 + bits
    keep, send, land, ssem, rsem = (dict(zip(range(1, last + 1), levels[i::5])) for i in range(5))

    step = pl.program_id(0)
    place = Place(rep, shards)
    rows = z_ref.shape[0]
    tile = z_ref.shape[1]
    mix_steps = dp.shape[2] * blocks // tile * 2
    chunks = n_out + n_in
    a, b, core, me, quarter = place.a, place.b, place.core, place.me, place.quarter

    norm = SmallSum(place, norm_out, slots_norm, sn, rn)

    def fetch(i):
        src, dst = ((low_hbm, low_t), (normed_hbm, normed_t), (hidden_hbm, hidden_ref))[i]
        return pltpu.make_async_copy(src, dst, si.at[i])

    @pl.when(step == 1)
    def _():
        fetch(1).wait()
        fetch(2).wait()

    @pl.when(step == 0)
    def _():
        for i in range(3):
            fetch(i).start()
        place.greet()
        norm_out[...] = jnp.zeros_like(norm_out)
        small[6:7, :LANES] = jnp.zeros((1, LANES), F32)
        dn[...] = jnp.zeros_like(dn)
        hi, lo = pieces(dt_ref[...], 2)
        dt2[:, :LANES] = hi
        dt2[:, LANES:] = lo
        for i, part in enumerate(pieces(cum_ref[...], 3)):
            cum3[:, i * LANES : (i + 1) * LANES] = part
        g_scr[...] = jnp.zeros_like(g_scr)
        dcum[...] = jnp.zeros_like(dcum)
        ddt[...] = jnp.zeros_like(ddt)
        fetch(0).wait()

    def halving(shard_first, level):
        at = level - 2
        if shard_first != (at >= 2):
            j = at if shard_first else at - 2
            if j < bits:
                bit, peer = place.shard_bit(j)
                return [(shards >> (j + 1), 4 * q if shard_first else q, bit, peer)] * 2
        n = 1 if shard_first else shards
        turn = at - bits if shard_first else at
        by_a, by_b = (a, place.a_peer), (b, place.b_peer)
        if turn == 0:
            return [(n, 2 * q, *by_a), (2 * n, q, *by_b)]
        return [(n, q, *by_b), (n, q, *by_a)]

    def copies(shard_first, level, c):
        k, w = c % keep[level].shape[0], c % land[level].shape[0]
        peers = [place.core_peer] * 2 if level == 1 else [part[3] for part in halving(shard_first, level)]
        return [
            remote(
                send[level].at[k, o], land[level].at[w, o], ssem[level].at[k, o], rsem[level].at[w, o], peers[o]
            )
            for o in range(2)
        ]

    def start(group):
        for copy in group:
            copy.start()

    def finish(group):
        for copy in group:
            copy.wait()

    def block(g, quarter):
        return ag.at[g, :, pl.ds(pl.multiple_of(quarter * q, q), q)]

    def half_block(g, o, quarter):
        return ag.at[g, o, pl.ds(pl.multiple_of(quarter * q, q), q)]

    def copy5(g):
        mine = block(g, quarter)
        return [
            remote(mine, mine, s5.at[g, i], r5.at[g, i], peer) for i, peer in enumerate((place.a_peer, place.b_peer))
        ]

    def copy6(g):
        from_a = half_block(g, 0, 2 * (1 - a) + b)
        from_b = half_block(g, 1, 2 * a + 1 - b)
        return [
            remote(from_a, from_a, s6.at[g, 0], r6.at[g, 0], place.b_peer),
            remote(from_b, from_b, s6.at[g, 1], r6.at[g, 1], place.a_peer),
        ]

    def targets(c, is_out):
        if is_out:
            cols = pl.ds(pl.multiple_of(c * 2 * LANES + core * LANES, LANES), LANES)
            return [gout_out.at[pl.ds(o * 4 * q, 4 * q), cols] for o in range(2)]
        base = chunk_at(c - n_out, blocks) * 4 * LANES + core * 2 * LANES
        return [gin_out.at[pl.ds(pl.multiple_of(base + o * LANES, LANES), LANES)] for o in range(2)]

    def copy7(c, is_out):
        g, t = c % ag.shape[0], c % agt.shape[0]
        ends = targets(c, is_out)
        own = [ag.at[g, o] if is_out else agt.at[t, o] for o in range(2)]
        local = [pltpu.make_async_copy(own[o], ends[o], l7.at[g, o]) for o in range(2)]
        return local + [remote(own[o], ends[o], s7.at[g, o], r7.at[g, o], place.core_peer) for o in range(2)]

    def by_target(c, run):
        for is_out in (True, False):

            @pl.when((c < n_out) == is_out)
            def _(is_out=is_out):
                run(is_out)

    def stage_first(c):
        @pl.when(c < n_out)
        def _():
            base = c * 2 * LANES
            for s in range(shards):
                lhs = low_t[s * 8 * q : (s + 1) * 8 * q, :]
                for side, ref in ((core, keep[1]), (1 - core, send[1])):
                    cols = pl.ds(pl.multiple_of(base + side * LANES, LANES), LANES)
                    grad = mm(lhs, cot_ref[:, cols])
                    for o in range(2):
                        ref[0, o, s * 4 * q : (s + 1) * 4 * q] = grad[o * 4 * q : (o + 1) * 4 * q].astype(ref.dtype)

        @pl.when(c >= n_out)
        def _():
            n = chunk_at(c - n_out, blocks)
            for s in range(shards):
                own = slice(s * 4 * q, (s + 1) * 4 * q)
                for side, ref in ((core, keep[1]), (1 - core, send[1])):
                    cols = pl.ds(pl.multiple_of(side * 2 * LANES, 2 * LANES), 2 * LANES)
                    grad = mm(normed_t[own, :], dp[n, :, cols])
                    for o in range(2):
                        ref[0, o, own] = grad[:, o * LANES : (o + 1) * LANES].astype(ref.dtype)

        for side, ref in ((1, keep[1]), (0, send[1])):

            @pl.when((c == chunks - 1) & (core == side))
            def _(ref=ref):
                for s in range(shards):
                    at = s * 4 * q
                    ref[0, 1, at : at + small_rows.shape[1]] = small_rows[s].astype(ref.dtype)

        start(copies(False, 1, c))

    def stage_halve(shard_first, level, c):
        finish(copies(shard_first, level - 1, c))
        k0, w0 = c % keep[level - 1].shape[0], c % land[level - 1].shape[0]
        k = c % keep[level].shape[0]
        for o, (runs, size, bit, _) in enumerate(halving(shard_first, level)):

            def part(u, carry, o=o, size=size, bit=bit):
                own = pl.ds(pl.multiple_of((2 * u + bit) * size, size), size)
                other = pl.ds(pl.multiple_of((2 * u + 1 - bit) * size, size), size)
                end = pl.ds(pl.multiple_of(u * size, size), size)
                keep[level][k, o, end] = keep[level - 1][k0, o, own] + land[level - 1][w0, o, own].astype(F32)
                send[level][k, o, end] = (
                    keep[level - 1][k0, o, other] + land[level - 1][w0, o, other].astype(F32)
                ).astype(BF)
                return carry

            if runs == 1:
                part(0, 0)
            else:
                lax.fori_loop(0, runs, part, 0)
        start(copies(shard_first, level, c))

    def stage_total(shard_first, c):
        finish(copies(shard_first, last, c))
        k, w, g = c % keep[last].shape[0], c % land[last].shape[0], c % ag.shape[0]
        total = keep[last][k] + land[last][w].astype(F32)
        for i, peer in enumerate(place.extra):
            keep[last][k] = total
            copy = remote(keep[last].at[k], xtra.at[c % 2, i], sx.at[c % 2, i], rx.at[c % 2, i], peer)
            copy.start()
            copy.wait()
            total = total + xtra[c % 2, i]
        for o in range(2):
            ag[g, o, pl.ds(pl.multiple_of(quarter * q, q), q)] = total[o].astype(BF)
        start(copy5(g))

    def stage_forward(c):
        g = c % ag.shape[0]
        for copy in copy5(g):
            copy.wait_recv()
        start(copy6(g))

    def stage_out(c):
        g, t = c % ag.shape[0], c % agt.shape[0]
        for copy in copy6(g):
            copy.wait_recv()

        def run(is_out):
            if not is_out:
                for o in range(2):
                    agt[t, o] = ag[g, o].astype(F32).T.astype(BF)
            start(copy7(c, is_out))

        by_target(c, run)

    def stage_end(c):
        by_target(c, lambda is_out: finish(copy7(c, is_out)))
        g = c % ag.shape[0]
        for copy in copy5(g) + copy6(g):
            copy.wait_send()

    plans = stage_steps(bits)

    def run_stage(number):
        for shard_first in (False, True):
            c = step - plans[shard_first][number - 1]

            @pl.when((c >= 0) & (c < chunks) & (first_over_shards(c) == shard_first))
            def _(c=c, shard_first=shard_first):
                if number == 1:
                    stage_first(c)
                elif number <= last:
                    stage_halve(shard_first, number, c)
                elif number == last + 1:
                    stage_total(shard_first, c)
                else:
                    (stage_forward, stage_out, stage_end)[number - last - 2](c)

    order = [5, 6, 8, 9, 7, 2, 4, 1, 3]
    for number in order + list(range(10, last + 5)):
        run_stage(number)

    masks = lambda: [mask_ref[k - 1] for k in range(1, CONV)]

    def pairs(first, count):
        def one(p, carry):
            pair = step // 2 * (tile // LANES) + p
            cols = pl.ds(pl.multiple_of(p * LANES, LANES), LANES)
            at = pl.ds(pl.multiple_of(pair * LANES, LANES), LANES)
            skip = skip_lanes(par_ref[ROW_SKIP : ROW_SKIP + 1, :LANES], head_of_lane(pair))
            res = backward_pair(
                pair, z_ref[:, cols], x_ref[:, cols], y_ref[:, cols], dgn_ref[0, :, cols], r_ref[...], rd_ref[...],
                par_ref[:CONV, at], par_ref[ROW_BIAS : ROW_BIAS + 1, at], skip, par_ref[ROW_GAIN : ROW_GAIN + 1, at],
                masks(), dt2, cum3, cumt_ref, cbt_ref, g_scr, dcum, ddt,
            )
            end = pl.ds(pl.multiple_of(pair % 4 * LANES, LANES), LANES)
            dp[pair // 4, :, end] = res[0]
            dp[blocks + pair // 4, :, end] = res[1]
            for k in range(CONV):
                small[k : k + 1, at] = res[4][k]
            small[4:5, at] = res[5]
            small[5:6, at] = res[2]
            per_head = jnp.concatenate(pieces(jnp.broadcast_to(res[3], (8, LANES)), 3), axis=1)
            small[6:7, :LANES] += mm_t(per_head, jnp.concatenate([head_of_lane(pair)] * 3, axis=1))[0:1]
            return carry

        lax.fori_loop(first, first + count, one, 0)

    @pl.when((step < mix_steps) & (step % 2 == 0))
    def _():
        pairs(0, 1)

    @pl.when((step < mix_steps) & (step % 2 == 1))
    def _():
        pairs(1, tile // LANES - 1)

    @pl.when(step == mix_steps - 1)
    def _():
        end = slice(INNER, INNER + 2 * LANES)
        d_bc, d_raw, d_weight, d_bias, d_alog, d_dtb = backward_tail(
            bc_ref, dtraw_ref, b_ref, c_ref, dt_ref, masks(), seg_col, seg_row, par_ref[:CONV, end],
            par_ref[ROW_BIAS : ROW_BIAS + 1, end], par_ref[ROW_ALOG : ROW_ALOG + 1, :LANES],
            par_ref[ROW_DTB : ROW_DTB + 1, :LANES], g_scr, dcum, ddt,
        )
        for i in range(2):
            cols = slice(i * LANES, (i + 1) * LANES)
            dp[2 * blocks, :, cols] = d_bc[i].astype(BF)
            end = slice(INNER + i * LANES, INNER + (i + 1) * LANES)
            for k in range(CONV):
                small[k : k + 1, end] = d_weight[i][k]
            small[4:5, end] = d_bias[i]
        dp[2 * blocks, :, 2 * LANES : 3 * LANES] = d_raw.astype(BF)
        dp[2 * blocks, :, 3 * LANES :] = jnp.zeros((rows, LANES), BF)
        small[5:6, INNER : INNER + LANES] = d_alog
        small[5:6, INNER + LANES :] = d_dtb
        for s in range(shards):
            for at, (row, lane) in enumerate(small_tiles(s, shards)):
                small_rows[s, at : at + 1, :] = small[row : row + 1, lane : lane + LANES]

    @pl.when((step >= n_out) & (step < chunks - 1))
    def _():
        grad = dp[chunk_at(step - n_out, blocks)]
        for s in range(shards):
            dn[s] += mm(grad, w_ref[s])

    @pl.when(step == chunks - 1)
    def _():
        grad = dp[n_in - 1]
        keep_rows = iota(w_ref.shape[1:], 0) < tail
        for s in range(shards):
            dn[s] += mm(grad, jnp.where(keep_rows, w_ref[s], 0))

    wide_cols = gh_buf.shape[2]
    together = wide_cols // dn.shape[2]
    n_parts = shards // together

    def norm_part(i):
        cols = slice(i * wide_cols, (i + 1) * wide_cols)
        d_normed = jnp.concatenate([dn[s] for s in range(i * together, (i + 1) * together)], axis=1)
        unit = hidden_ref[:, cols].astype(F32) * inv[:, :1]
        return cols, d_normed, unit, d_normed * par_ref[ROW_NORM : ROW_NORM + 1, cols]

    def first_pass(i):
        cols, d_normed, unit, du = norm_part(i)
        grad_norm = jnp.sum(d_normed * unit, axis=0, keepdims=True)
        for j in range(wide_cols // LANES):
            at = i * (wide_cols // LANES) + j
            norm_out[at : at + 1, :] = grad_norm[:, j * LANES : (j + 1) * LANES]
        dots[...] += jnp.sum(du * unit, axis=1, keepdims=True) * (1.0 / hidden_ref.shape[1])

    def gh_copy(i):
        return pltpu.make_async_copy(
            gh_buf.at[i % 2], gh_out.at[:, i * wide_cols : (i + 1) * wide_cols], sgh.at[i % 2]
        )

    def second_pass(i):
        if i >= 2:
            gh_copy(i - 2).wait()
        cols, _, unit, du = norm_part(i)
        gh_buf[i % 2] = cot_ref[:, cols].astype(F32) + inv[:, :1] * (du - unit * dots[:, :1])
        gh_copy(i).start()

    @pl.when(step == chunks)
    def _():
        hid = hidden_ref[...].astype(F32)
        scale = lax.rsqrt(jnp.mean(hid * hid, axis=1, keepdims=True) + EPS)
        inv[...] = jnp.broadcast_to(scale, inv.shape)
        dots[...] = jnp.zeros_like(dots)
        first_pass(0)

    for i in range(1, n_parts):

        @pl.when(step == chunks + (i + 1) // 2)
        def _(i=i):
            first_pass(i)

    norm_from = chunks + n_parts // 2

    for i in range(n_parts):

        @pl.when(step == norm_from + 1 + i)
        def _(i=i):
            second_pass(i)

    @pl.when(step == norm_from + 1 + n_parts)
    def _():
        for i in range(max(0, n_parts - 2), n_parts):
            gh_copy(i).wait()

    for i in range(norm.stages):

        @pl.when(step == norm_from + i)
        def _(i=i):
            norm.stage(i)


def results_kernel(
    gin_ref, gout_ref, gh_ref, mixed_ref, norm_ref,
    gin_out, gout_out, gh_out, mixed_out, ngain_out, gain_out, cw_out, cb_out, alog_out, skip_out, dtb_out, *, shards
):
    step = pl.program_id(0)
    me = lax.axis_index("shard")
    gin_out[...] = gin_ref[...].astype(F32)
    gout_out[...] = gout_ref[...].astype(F32)
    gh_out[...] = gh_ref[...]
    mixed_out[...] = mixed_ref[...]

    @pl.when(step == pl.num_programs(0) - 1)
    def _():
        conv, gain, heads, ngain = cb_out.shape[0], gain_out.shape[0], alog_out.shape[0], ngain_out.shape[0]
        rows = gin_ref.shape[0]
        small = gin_ref[rows - LANES :, :].astype(F32).T
        norm = jnp.concatenate([norm_ref[i : i + 1, :] for i in range(norm_ref.shape[0])], axis=1)
        for s in range(shards):

            @pl.when(me == s)
            def _(s=s):
                tiles = small_tiles(s, shards)

                def part(row, base, size):
                    at = [i for i, (r, lane) in enumerate(tiles) if r == row and base <= lane < base + max(size, LANES) * shards]
                    flat = jnp.concatenate([small[i : i + 1, :] for i in at], axis=1)
                    first = s * size - (tiles[at[0]][1] - base)
                    return flat[:, first : first + size]

                for k in range(CONV):
                    cw_out[k : k + 1, :] = part(k, 0, conv)
                cb_out[...] = part(CONV, 0, conv).reshape(conv)
                gain_out[...] = part(5, 0, gain).reshape(gain)
                for ref, row, base in ((alog_out, 5, INNER), (dtb_out, 5, INNER + LANES), (skip_out, 6, 0)):
                    i = tiles.index((row, base))
                    ref[...] = small[i : i + 1, s * heads : (s + 1) * heads].reshape(heads)
                ngain_out[...] = norm[:, s * ngain : (s + 1) * ngain].reshape(ngain)


def results(g_in, g_out, grad_hidden, mixed, norm, columns, singles, shards):
    conv_w, conv_b, gain, ngain, a_log = singles[:5]
    depth, width = g_in.shape[1], g_out.shape[1]
    steps = 8
    f = lambda *s: jax.ShapeDtypeStruct(s, F32)
    strip = lambda v: pl.BlockSpec((v.shape[0] // steps, v.shape[1]), lambda i: (i, 0))
    whole = lambda s: pl.BlockSpec(s, lambda i: (0,) * len(s))
    small = [ngain.shape, gain.shape, conv_w.shape, conv_b.shape, a_log.shape, a_log.shape, a_log.shape]
    return pl.pallas_call(
        functools.partial(results_kernel, shards=shards),
        grid=(steps,),
        in_specs=[strip(g_in), strip(g_out), strip(grad_hidden), strip(mixed), whole(norm.shape)],
        out_specs=[strip(g_in), strip(g_out), strip(grad_hidden), strip(mixed), *(whole(s) for s in small)],
        out_shape=[
            f(columns, depth), f(*g_out.shape), f(*grad_hidden.shape), jax.ShapeDtypeStruct(mixed.shape, BF),
            *(f(*s) for s in small),
        ],
        name="results",
    )(g_in, g_out, grad_hidden, mixed, norm)


def mixer_backward_and_sums(saved, hidden, cotangent, seg_ids, rep, shards):
    (w3, ow3, proj, y, low_t, r, b, c, cbt, dt, cum, cumt, mask, normed_t, params, _, rd, seg_col, d_gated) = saved
    rows, width = hidden.shape
    inner = low_t.shape[0]
    depth = width // shards
    wide_block = 4 * LANES
    blocks = inner // wide_block
    n_out = width // (2 * LANES)
    n_in = proj.shape[1] // wide_block
    q = depth // 4
    chunks = n_out + n_in
    bits = shards.bit_length() - 1
    steps = chunks + stage_steps(bits)[0][-1]
    n_small = SmallSum.count(rep, shards)
    n_extra = max(1, n_small - 3 - (shards - 1))
    tile = 3 * LANES
    tiles = inner // tile
    mix = lambda offset: pl.BlockSpec((rows, tile), lambda i: (0, offset + jnp.minimum(i // 2, tiles - 1)))
    a_shard = inner // shards // tile

    def d_gated_at(i):
        at = jnp.minimum(i // 2, tiles - 1)
        return at // a_shard, 0, at % a_shard

    const = lambda shape, at=None: pl.BlockSpec(shape, lambda i: at or (0,) * len(shape), pipeline_mode=pl.Buffered(1))
    f = lambda *s: jax.ShapeDtypeStruct(s, F32)
    h = lambda *s: jax.ShapeDtypeStruct(s, BF)
    vm = pltpu.VMEM
    dma = lambda *s: pltpu.SemaphoreType.DMA(s)
    anywhere = pl.BlockSpec(memory_space=pl.ANY)
    pairs_bc = inner // LANES
    in_specs = [
        mix(0), mix(tiles), mix(0),
        pl.BlockSpec((1, rows, tile), d_gated_at),
        const((rows, 2 * LANES), (0, pairs_bc)), const((rows, LANES), (0, 2 * pairs_bc + 2)),
        const((rows, LANES)), const((rows, LANES)), const((rows, LANES)), const((rows, LANES)),
        const((rows, rows)), const((rows, LANES)), const((rows, LANES)), const((LANES, rows)),
        const((CONV - 1, rows, LANES)), const((rows, LANES)), const((1, rows)), const(params.shape),
        pl.BlockSpec(
            (shards, wide_block, depth), lambda i: (0, chunk_at(jnp.clip(i - n_out, 0, n_in - 1), blocks), 0)
        ),
        anywhere, const((rows, width)), anywhere, anywhere,
    ]
    whole_out = lambda shape: pl.BlockSpec(shape, lambda i: (0,) * len(shape))
    norm_shape = (16, LANES)
    small_height = -(-max(len(small_tiles(s, shards)) for s in range(shards)) // 16) * 16
    scratch = [
        vm((rows, 2 * LANES), BF), vm((rows, 3 * LANES), BF), vm((rows, rows), F32), vm((rows, LANES), F32),
        vm((rows, LANES), F32), vm((n_in, rows, wide_block), BF), vm((shards, rows, depth), F32), vm((2, rows, tile), F32), vm((rows, LANES), F32), vm((rows, LANES), F32),
        vm((8, 2, 4 * q, LANES), BF), vm((4, 2, LANES, 4 * q), BF),
        vm((8, CONV_CH), F32), vm((shards, small_height, LANES), F32), vm((n_small, *norm_shape), F32),
        dma(8, 2), dma(8, 2), dma(8, 2), dma(8, 2), dma(8, 2), dma(8, 2), dma(8, 2),
        vm((2, n_extra, 2, q, LANES), F32), dma(2, n_extra), dma(2, n_extra),
        dma(n_small), dma(n_small), dma(2),
        vm((inner, rows), BF), vm((width, rows), BF), vm((rows, width), BF), dma(3),
    ]
    for level in range(1, 4 + bits):
        own, landing = {1: (1, 2), 2: (3, 8)}.get(level, (4, 8))
        shape = (2, (shards * 4 * q) >> (level - 1), LANES)
        scratch += [
            vm((own, *shape), F32), vm((own, *shape), BF), vm((landing, *shape), BF), dma(own, 2), dma(landing, 2),
        ]
    return pl.pallas_call(
        functools.partial(
            reduce_kernel, rep=rep, shards=shards, q=q, blocks=blocks, n_out=n_out, n_in=n_in,
            tail=w3.shape[1] - (n_in - 1) * wide_block,
        ),
        grid=(steps,),
        in_specs=in_specs,
        out_specs=[anywhere, anywhere, anywhere, whole_out(norm_shape)],
        out_shape=[
            h(n_in * wide_block, depth), h(inner // shards, width), f(rows, width), f(*norm_shape),
        ],
        scratch_shapes=scratch,
        compiler_params=pltpu.CompilerParams(
            vmem_limit_bytes=VMEM_LIMIT, collective_id=2, has_side_effects=True
        ),
        name="mixer_backward_and_sums",
    )(
        proj, proj, y, d_gated, proj, proj, r, rd, b, c, cbt, dt, cum, cumt, mask, seg_col, seg_ids,
        params, w3, low_t, cotangent, normed_t, hidden,
    )


def per_device(
    hidden, seg_ids, cotangent, in_weight, out_weight, norm_gain, gated_gain, conv_weight, conv_bias, a_log, d_skip,
    dt_bias,
):
    rep, shards = lax.axis_size("rep"), lax.axis_size("shard")
    singles = (conv_weight, conv_bias, gated_gain, norm_gain, a_log, d_skip, dt_bias)
    wt = in_weight.T
    saved = mixer_forward(hidden, cotangent, seg_ids, wt, out_weight, singles, rep, shards)
    mixed = saved[15]
    g_in, g_out, grad_hidden, norm = mixer_backward_and_sums(saved, hidden, cotangent, seg_ids, rep, shards)
    g_in, g_out, grad_hidden, mixed, *small = results(
        g_in, g_out, grad_hidden, mixed, norm, wt.shape[0], singles, shards
    )
    return (mixed, grad_hidden, g_in.T, g_out, *small)


def solution(mesh):
    both = ("rep", "shard")
    shard = P("shard")
    placed = (P(both, None), P(both, None), P(both, None), P("shard", None), P("shard", None), shard, shard,
              P(None, "shard"), shard, shard, shard, shard)
    outs = (P(both, None), P(both, None), P("shard", None), P("shard", None), shard, shard, P(None, "shard"), shard,
            shard, shard, shard)
    return jax.shard_map(per_device, mesh=mesh, in_specs=placed, out_specs=outs, check_vma=False)
```
